128 devices in a mesh: fs: 16 (over z, x), sp: 8 (over y, core).
Axes of the slice: x: 4, y: 4, z: 4, core: 2. Of those that a mesh axis runs over, the one named last changes fastest.
Arguments:
- layer_input: bfloat16 [16, 1024, 2048], P('fs', 'sp'), may hold values from -6 to 6
- output_gradient: bfloat16 [16, 1024, 2048], P('fs', 'sp'), may hold values from -6 to 6
- norm_gain_pair: float32 [2, 2048], replicated, may hold values from 0.25 to 1.75
- query_key_value_weight: bfloat16 [2048, 3, 2048], P('fs'), may hold values from -0.125 to 0.125
- output_weight: bfloat16 [2048, 2048], P('fs'), may hold values from -0.25 to 0.25
- gate_up_weight: bfloat16 [2048, 2, 8192], P('fs'), may hold values from -0.125 to 0.125
- down_weight: bfloat16 [8192, 2048], P('fs'), may hold values from -0.0625 to 0.0625
- adapter_input_model: bfloat16 [6, 2048, 128], P(None, 'fs'), may hold values from -0.125 to 0.125
- adapter_output_model: bfloat16 [5, 2048, 128], P(None, 'fs'), may hold values from -0.75 to 0.75
- adapter_input_hidden: bfloat16 [1, 8192, 128], P(None, 'fs'), may hold values from -0.0625 to 0.0625
- adapter_output_hidden: bfloat16 [2, 8192, 128], P(None, 'fs'), may hold values from -0.75 to 0.75
- spans: int32 [16, 3], P('fs'), may hold values from 1 to 512, 1024 in all within a row
- adapter_choice_rows: int32 [16, 3], P('fs'), may hold values from 0 to 7
Outputs:
- layer_output: bfloat16 [16, 1024, 2048], P('fs', 'sp')
- grad_in: float32 [16, 1024, 2048], P('fs', 'sp')
- grad_lora_in_d: float32 [6, 2048, 128], P(None, 'fs')
- grad_lora_out_d: float32 [5, 2048, 128], P(None, 'fs')
- grad_lora_in_ff: float32 [1, 8192, 128], P(None, 'fs')
- grad_lora_out_ff: float32 [2, 8192, 128], P(None, 'fs')
The draws below stay inside these ranges and needn't reach their ends.
Inputs may be any that keep to these rules, and one draw needn't show every extreme that they name: `spans`: per group, the prompt, first continuation and second continuation lie end to end in that order and fill all 1024 tokens; the longest is 512.
All inputs are finite; a program needn't handle non-finite values.
Results may differ from the reference program's by a relative error of at most 0.02.
Values may be sent and summed in bfloat16 or wider, within the bound.
No kernel may reach another device: no remote copies, remote signals or barrier semaphores. Data moves between devices by JAX's collectives and lax.ppermute only.
A program may use at most 512 MiB of HBM per device.

```python
import math
import jax
import jax.numpy as jnp
import numpy as np
from jax import lax

MODEL_DIM = 2048
HEAD_SIZE = 64
HIDDEN_UNITS = 8192
NA = 8
ADAPTER_RANK = 16
GTOK = 1024
GROUPS = 16
ADAPTER_COLUMNS = 128


def set_ends(array, rng, low, largest):
    spot = [jax.random.randint(jax.random.fold_in(rng, axis), (), 0, length) for axis, length in enumerate(array.shape)]
    longest = array.shape.index(max(array.shape))
    beside = spot[:longest] + [(spot[longest] + 1) % array.shape[longest]] + spot[longest + 1:]
    return array.at[tuple(spot)].set(low).at[tuple(beside)].set(largest)


def levels(stream_key, extent, shards, smallest, top_value):
    def one(dim, shards_of):
        steps = jax.random.uniform(jax.random.fold_in(jax.random.fold_in(stream_key, 6), dim), (shards_of,), jnp.float32, smallest / len(shards), top_value / len(shards))
        return jnp.repeat(jnp.exp(steps), extent[dim] // shards_of).reshape((-1,) + (1,) * (len(extent) - dim - 1))

    level = one(*shards[0])
    for cut in shards[1:]:
        level = level * one(*cut)
    return level


def profile(amount, total, reach, skew):
    loads = [(1 << 20) // math.isqrt(grade ** skew) + 1 for grade in range(2, amount + 1)]
    rest, counts = total - reach - (amount - 1), [1] * (amount - 1)
    while rest > 0:
        free = [i for i in range(amount - 1) if counts[i] < reach]
        pool, remaining = sum([loads[i] for i in free]), rest
        for i in free:
            extra = min(reach - counts[i], max(1, remaining * loads[i] // pool), rest)
            counts[i] = counts[i] + extra
            rest = rest - extra
    return np.array([reach] + counts)


def uneven_parts(rng, number_of, total, most, lean):
    if number_of == 2:
        one = jax.random.randint(rng, (), max(1, total - most), min(most, total - 1) + 1)
        return jnp.stack([one, total - one])
    sizes = jnp.asarray(profile(number_of, total, most, lean), jnp.int32)
    pairs = (number_of - 1) // 2
    giver, sink = sizes[1:1 + 2 * pairs:2], sizes[2:2 + 2 * pairs:2]
    room = jnp.minimum(giver - 1, most - sink)
    passed = jax.random.randint(jax.random.fold_in(rng, 1), (pairs,), 0, 1 << 20) % (room + 1)
    sizes = sizes.at[1:1 + 2 * pairs:2].set(giver - passed).at[2:2 + 2 * pairs:2].set(sink + passed)
    return sizes[jax.random.permutation(jax.random.fold_in(rng, 2), number_of)]


def centred(stream_key, extent, spread, most, pieces=(), held_as=jnp.bfloat16):
    level = levels(stream_key, extent, pieces, -0.22, 0.18) if pieces else 1.0
    values = jax.random.normal(stream_key, extent, jnp.float32) * spread * level
    return jnp.minimum(jnp.maximum(values, -most), most).astype(held_as)


def setup_inputs(seed: int = 0) -> dict:
    splits = jax.random.split(jax.random.key(seed), 14)
    return {
        "layer_input": centred(splits[0], (GROUPS, GTOK, MODEL_DIM), 1.0, 6.0, ((0, 16), (1, 8))),
        "output_gradient": centred(splits[1], (GROUPS, GTOK, MODEL_DIM), 1.0, 6.0, ((0, 16), (1, 8))),
        "norm_gain_pair": jnp.clip(1.0 + 0.15 * jax.random.normal(splits[2], (2, MODEL_DIM), jnp.float32), 0.25, 1.75),
        "query_key_value_weight": centred(splits[3], (MODEL_DIM, 3, MODEL_DIM), MODEL_DIM ** -0.5, 0.125, ((0, 16),)),
        "output_weight": centred(splits[4], (MODEL_DIM, MODEL_DIM), (MODEL_DIM // 4) ** -0.5, 0.25, ((0, 16),)),
        "gate_up_weight": centred(splits[5], (MODEL_DIM, 2, HIDDEN_UNITS), MODEL_DIM ** -0.5, 0.125, ((0, 16),)),
        "down_weight": centred(splits[6], (HIDDEN_UNITS, MODEL_DIM), HIDDEN_UNITS ** -0.5, 0.0625, ((0, 16),)),
        "adapter_input_model": centred(splits[7], (6, MODEL_DIM, ADAPTER_COLUMNS), MODEL_DIM ** -0.5, 0.125, ((1, 16),)),
        "adapter_output_model": centred(splits[8], (5, MODEL_DIM, ADAPTER_COLUMNS), (4 * ADAPTER_RANK) ** -0.5, 0.75, ((1, 16),)),
        "adapter_input_hidden": centred(splits[9], (1, HIDDEN_UNITS, ADAPTER_COLUMNS), HIDDEN_UNITS ** -0.5, 0.0625, ((1, 16),)),
        "adapter_output_hidden": centred(splits[10], (2, HIDDEN_UNITS, ADAPTER_COLUMNS), (4 * ADAPTER_RANK) ** -0.5, 0.75, ((1, 16),)),
        "spans": jax.vmap(lambda own: uneven_parts(own, 3, GTOK, GTOK // 2, 0))(jax.random.split(splits[11], GROUPS)).reshape((GROUPS, 3)).astype(jnp.int32),
        "adapter_choice_rows": set_ends(jax.random.randint(splits[12], (GROUPS, 3), 0, NA), jax.random.fold_in(splits[12], 1), 0, NA - 1).astype(jnp.int32),
    }


NORM_EPS = 1e-05
ROPE_BASE = 130000.0
MASK_FILL = -1e+30
HIGH = lax.Precision.HIGHEST

@jax.custom_vjp
def low(v):
    return lax.optimization_barrier(v.astype(jnp.bfloat16)).astype(jnp.float32)

@jax.custom_vjp
def low_back(v):
    return v

def low_keep(v):
    return (low(v), None)

def low_pass(kept, grad):
    return (grad,)

def back_keep(v):
    return (v, None)

def back_low(kept, grad):
    return (low(grad),)
low.defvjp(low_keep, low_pass)
low_back.defvjp(back_keep, back_low)

def low_both(value):
    return low(low_back(value))

def matrix_product(left, right):
    return jnp.dot(left, right, precision=HIGH, preferred_element_type=jnp.float32)

def rmsnorm(values, gain):
    return values * lax.rsqrt(lax.optimization_barrier(jnp.mean(values * values, -1, keepdims=True)) + NORM_EPS) * gain

def angles(position):
    half_dim = HEAD_SIZE // 2
    freq = ROPE_BASE ** (-(jnp.arange(half_dim, dtype=jnp.float32) * 2.0 / HEAD_SIZE))
    phase = position.astype(jnp.float32)[:, None] * freq[None, :]
    return (jnp.cos(phase)[:, None, :], jnp.sin(phase)[:, None, :])

def rotate(values, cosine, sine_part):
    half_dim = values.shape[-1] // 2
    first_half = values[..., :half_dim]
    second_half = values[..., half_dim:]
    return jnp.concatenate([first_half * cosine - second_half * sine_part, second_half * cosine + first_half * sine_part], -1)

def token_info(spans, adapter_choice_rows, group_tokens):
    token_pos = jnp.arange(group_tokens, dtype=jnp.int32)[None, :]
    prompt_len = spans[..., 0:1]
    first_len = spans[..., 1:2]
    segment = (token_pos >= prompt_len).astype(jnp.int32) + (token_pos >= prompt_len + first_len).astype(jnp.int32)
    position = token_pos - jnp.where(segment == 2, first_len, 0)
    chosen = jnp.where(segment == 0, adapter_choice_rows[..., 0:1], jnp.where(segment == 1, adapter_choice_rows[..., 1:2], adapter_choice_rows[..., 2:3]))
    return (segment, position, chosen)

def allowed_mask(segment, offset, block_rows):
    key_idx = jnp.arange(segment.shape[0])
    query_idx = offset + jnp.arange(block_rows)
    query_seg = segment[offset:offset + block_rows]
    return (key_idx[None, :] <= query_idx[:, None]) & ((segment[None, :] == query_seg[:, None]) | (segment[None, :] == 0))

def reduced_rank_forward(source, down_map, up_map, adapter_select_mask):
    low_rank = low_both(matrix_product(source, down_map) * adapter_select_mask)
    return matrix_product(low_rank, up_map.T)

def group_layer(layer_in, input_model_map, output_model_map, input_hidden_map, output_hidden_map, gains, wqkv, output_matrix, wgu, wdown, adapter_select_mask, cosine, sine_part, allowed):
    head_split = MODEL_DIM // HEAD_SIZE
    normalized_first = low(rmsnorm(layer_in, gains[0]))
    q_base = matrix_product(normalized_first, wqkv[:, 0, :]) + reduced_rank_forward(normalized_first, input_model_map[0], output_model_map[0], adapter_select_mask)
    k_base = matrix_product(normalized_first, wqkv[:, 1, :]) + reduced_rank_forward(normalized_first, input_model_map[1], output_model_map[1], adapter_select_mask)
    v_base = matrix_product(normalized_first, wqkv[:, 2, :]) + reduced_rank_forward(normalized_first, input_model_map[2], output_model_map[2], adapter_select_mask)
    query = low_both(rotate(low_back(q_base).reshape(GTOK, head_split, HEAD_SIZE), cosine, sine_part))
    key_all = low_both(rotate(low_back(k_base).reshape(GTOK, head_split, HEAD_SIZE), cosine, sine_part))
    value_all = low_both(v_base).reshape(GTOK, head_split, HEAD_SIZE)
    scores = jnp.einsum('qhd,khd->hqk', query, key_all, precision=HIGH) * HEAD_SIZE ** (-0.5)
    scores = low_back(jnp.where(allowed[None], scores, MASK_FILL))
    softmax_w = low(jax.nn.softmax(scores, axis=-1))
    attention_mixed = low_both(jnp.einsum('hqk,khd->qhd', softmax_w, value_all, precision=HIGH).reshape(GTOK, MODEL_DIM))
    attn_out = low_back(matrix_product(attention_mixed, output_matrix) + reduced_rank_forward(attention_mixed, input_model_map[3], output_model_map[3], adapter_select_mask))
    residual_stream = layer_in + attn_out
    normalized_second = low(rmsnorm(residual_stream, gains[1]))
    gate_preact = low_back(matrix_product(normalized_second, wgu[:, 0, :]) + reduced_rank_forward(normalized_second, input_model_map[4], output_hidden_map[0], adapter_select_mask))
    up_preact = low_back(matrix_product(normalized_second, wgu[:, 1, :]) + reduced_rank_forward(normalized_second, input_model_map[5], output_hidden_map[1], adapter_select_mask))
    hidden_activated = low(jax.nn.silu(gate_preact) * up_preact)
    mlp_out = low_back(matrix_product(hidden_activated, wdown) + reduced_rank_forward(hidden_activated, input_hidden_map[0], output_model_map[4], adapter_select_mask))
    return residual_stream + mlp_out

def reference(layer_input, output_gradient, norm_gain_pair, query_key_value_weight, output_weight, gate_up_weight, down_weight, adapter_input_model, adapter_output_model, adapter_input_hidden, adapter_output_hidden, spans, adapter_choice_rows):
    gains = norm_gain_pair.astype(jnp.float32)
    wqkv = query_key_value_weight.astype(jnp.float32)
    output_matrix = output_weight.astype(jnp.float32)
    wgu = gate_up_weight.astype(jnp.float32)
    wdown = down_weight.astype(jnp.float32)
    adapter_table = (adapter_input_model.astype(jnp.float32), adapter_output_model.astype(jnp.float32), adapter_input_hidden.astype(jnp.float32), adapter_output_hidden.astype(jnp.float32))

    def group_step(totals_now, group_item):
        layer_in, gradient_row_block, span_row, id_row = group_item
        segment, position, chosen = token_info(span_row, id_row, GTOK)
        segment = segment[0]
        position = position[0]
        chosen = chosen[0]
        adapter_select_mask = (chosen[:, None] == jnp.arange(NA * ADAPTER_RANK)[None, :] // ADAPTER_RANK).astype(jnp.float32)
        cosine, sine_part = angles(position)
        allowed = allowed_mask(segment, 0, GTOK)

        def forward(values, input_model_map, output_model_map, input_hidden_map, output_hidden_map):
            return group_layer(values, input_model_map, output_model_map, input_hidden_map, output_hidden_map, gains, wqkv, output_matrix, wgu, wdown, adapter_select_mask, cosine, sine_part, allowed)
        result, backward = jax.vjp(forward, layer_in.astype(jnp.float32), *adapter_table)
        grads = backward(gradient_row_block.astype(jnp.float32))
        updated = tuple((total + grad for total, grad in zip(totals_now, grads[1:])))
        return (updated, (result.astype(jnp.bfloat16), grads[0]))
    initial = tuple((jnp.zeros_like(adapter) for adapter in adapter_table))
    totals, (layer_output, grad_in) = lax.scan(group_step, initial, (layer_input, output_gradient, spans, adapter_choice_rows))
    return (layer_output, grad_in, totals[0], totals[1], totals[2], totals[3])
```

```python
import jax
import jax.numpy as jnp
from jax import lax
from jax.sharding import PartitionSpec as P

HEAD_SIZE = 64
ADAPTER_RANK = 16
NORM_EPS = 1e-05
ROPE_BASE = 130000.0
MASK_FILL = -1e30
BF = jnp.bfloat16
F32 = jnp.float32


def mm(left, right):
    return jnp.dot(left, right, preferred_element_type=F32)


def mm_nt(left, right):
    return lax.dot_general(left, right, (((1,), (1,)), ((), ())), preferred_element_type=F32)


def mm_tn(left, right):
    return lax.dot_general(left, right, (((0,), (0,)), ((), ())), preferred_element_type=F32)


def shift(x, chips):
    return lax.ppermute(x, "sp", [(i, ((i // 2 + chips) % 4) * 2 + i % 2) for i in range(8)])


def swap(x):
    return lax.ppermute(x, "sp", [(i, i ^ 1) for i in range(8)])


def gather_tokens(x):
    near = jnp.concatenate([x, shift(x, -1), shift(x, 2), shift(x, 1)], 0)
    return jnp.concatenate([near, swap(near)], 0)


def scatter_tokens(parts):
    got = swap(parts[1].astype(BF))
    pair = parts[0] + got.astype(F32)
    total = pair[0]
    for d, back in ((1, 1), (2, 2), (3, -1)):
        total = total + shift(pair[d].astype(BF), back).astype(F32)
    return total


def rms_inverse(values):
    return lax.rsqrt(jnp.mean(values * values, -1, keepdims=True) + NORM_EPS)


def norm_back(grad_norm, values, inverse, gain):
    normed = values * inverse
    scaled = grad_norm * gain
    return inverse * (scaled - normed * jnp.mean(scaled * normed, -1, keepdims=True))


def rope_pair(values, cosine, sine):
    half = values.shape[1] // 2
    a, b = values[:, :half], values[:, half:]
    return jnp.concatenate([a * cosine - b * sine, b * cosine + a * sine], 1)


def split_heads(values, paired):
    rows = values.shape[0]
    if paired:
        return values.reshape(rows, 2, 4, 32).transpose(2, 0, 1, 3).reshape(4, rows, 64)
    return values.reshape(rows, 4, 64).transpose(1, 0, 2)


def join_heads(values, paired):
    rows = values.shape[1]
    if paired:
        return values.reshape(4, rows, 2, 32).transpose(1, 2, 0, 3).reshape(rows, 256)
    return values.transpose(1, 0, 2).reshape(rows, 256)


def attend(q, k, v, allowed):
    scores = jnp.einsum("hqd,hkd->hqk", q, k, preferred_element_type=F32) * 0.125
    scores = jnp.where(allowed[None], scores, MASK_FILL)
    top = jnp.max(scores, -1, keepdims=True)
    weights = jnp.exp(scores - top)
    total = jnp.sum(weights, -1, keepdims=True)
    probs = (weights / total).astype(BF)
    out = jnp.einsum("hqk,hkd->hqd", probs, v, preferred_element_type=F32).astype(BF)
    return out, top + jnp.log(total)


def attend_back(q, k, v, grad, log_total, allowed):
    scores = jnp.einsum("hqd,hkd->hqk", q, k, preferred_element_type=F32) * 0.125
    scores = jnp.where(allowed[None], scores, MASK_FILL)
    probs = jnp.exp(scores - log_total)
    grad_probs = jnp.einsum("hqd,hkd->hqk", grad, v, preferred_element_type=F32)
    inner = jnp.sum(probs * grad_probs, -1, keepdims=True)
    grad_scores = (probs * (grad_probs - inner)).astype(BF)
    gq = jnp.einsum("hqk,hkd->hqd", grad_scores, k, preferred_element_type=F32) * 0.125
    gk = jnp.einsum("hqk,hqd->hkd", grad_scores, q, preferred_element_type=F32) * 0.125
    gv = jnp.einsum("hqk,hqd->hkd", probs.astype(BF), grad, preferred_element_type=F32)
    return gq.astype(BF), gk.astype(BF), gv.astype(BF)


def body(
    layer_input,
    output_gradient,
    norm_gain_pair,
    query_key_value_weight,
    output_weight,
    gate_up_weight,
    down_weight,
    adapter_input_model,
    adapter_output_model,
    adapter_input_hidden,
    adapter_output_hidden,
    spans,
    adapter_choice_rows,
):
    f_at, s_at = lax.axis_index("fs"), lax.axis_index("sp")
    y_at, c_at = s_at // 2, s_at % 2
    x_l = layer_input[0]
    og_l = output_gradient[0]
    rows, width = x_l.shape
    tokens = 8 * rows
    gain_one, gain_two = norm_gain_pair[0], norm_gain_pair[1]

    i512 = lax.broadcasted_iota(jnp.int32, (512, 256), 0)
    j256 = lax.broadcasted_iota(jnp.int32, (512, 256), 1)
    source_qk = ((j256 % 128) // 32) * 128 + c_at * 64 + (j256 // 128) * 32 + j256 % 32
    source_v = (j256 // 64) * 128 + c_at * 64 + j256 % 64
    pick_qk = (i512 == source_qk).astype(BF)
    pick_v = (i512 == source_v).astype(BF)
    wide = lax.dynamic_slice(query_key_value_weight, (0, 0, 512 * y_at), (rows, 3, 512))
    pack_one = jnp.concatenate(
        [
            mm(wide[:, 0], pick_qk).astype(BF),
            mm(wide[:, 1], pick_qk).astype(BF),
            mm(wide[:, 2], pick_v).astype(BF),
            adapter_input_model[0],
            adapter_input_model[1],
            adapter_input_model[2],
        ],
        1,
    )
    pieces = [
        lax.dynamic_slice(gate_up_weight, (0, 0, 512 * f + 64 * s_at), (128, 2, 64)) for f in range(16)
    ]
    gate_up = jnp.concatenate(pieces, 2)
    pack_two = jnp.concatenate(
        [
            gate_up[:, 0],
            gate_up[:, 1],
            adapter_input_model[4],
            adapter_input_model[5],
            adapter_output_model[3],
            adapter_output_model[4],
        ],
        1,
    )
    half = lambda a: lax.dynamic_slice_in_dim(a, 64 * c_at, 64, 0)
    eighth = lambda a: lax.dynamic_slice_in_dim(a, 64 * s_at, 64, 0)
    pack_three = jnp.concatenate(
        [
            eighth(down_weight),
            half(output_weight),
            eighth(adapter_input_hidden[0]),
            eighth(adapter_output_hidden[0]),
            eighth(adapter_output_hidden[1]),
            half(adapter_output_model[0]),
            half(adapter_output_model[1]),
            half(adapter_output_model[2]),
            half(adapter_input_model[3]),
        ],
        1,
    )
    all_one = lax.all_gather(pack_one, "fs", axis=0, tiled=True)
    all_two = lax.all_gather(pack_two, "fs", axis=0, tiled=True)
    all_three = lax.all_gather(pack_three, "fs", axis=0, tiled=True)
    w_qkv, a_qkv = all_one[:, :768], all_one[:, 768:]
    w_gu, a_gu, b_o, b_d = all_two[:, :2048], all_two[:, 2048:2304], all_two[:, 2304:2432], all_two[:, 2432:]
    w_d, w_o = all_three[:, :2048], all_three[:, 2048:4096]
    in_ff, out_g, out_u = all_three[:, 4096:4224], all_three[:, 4224:4352], all_three[:, 4352:4480]
    own_b = lax.dynamic_slice(all_three, (256 * y_at, 4480), (256, 384))
    b_q = own_b[:, :128].reshape(4, 2, 32, 128).transpose(1, 0, 2, 3).reshape(256, 128)
    b_k = own_b[:, 128:256].reshape(4, 2, 32, 128).transpose(1, 0, 2, 3).reshape(256, 128)
    b_v = own_b[:, 256:]
    a_o = all_three[:, 4864:4992]

    at = jnp.arange(tokens, dtype=jnp.int32)
    prompt, second = spans[0, 0], spans[0, 0] + spans[0, 1]

    def mask_of(token):
        segment = (token >= prompt).astype(jnp.int32) + (token >= second).astype(jnp.int32)
        chosen = jnp.where(
            segment == 0,
            adapter_choice_rows[0, 0],
            jnp.where(segment == 1, adapter_choice_rows[0, 1], adapter_choice_rows[0, 2]),
        )
        return (chosen[:, None] == jnp.arange(128)[None, :] // ADAPTER_RANK).astype(F32)

    core_of = jnp.where(at < 4 * rows, c_at, 1 - c_at)
    chip_of = (y_at + (at // rows) % 4) % 4
    relative = (chip_of * 2 + core_of) * rows + at % rows
    own_tokens = s_at * rows + jnp.arange(rows, dtype=jnp.int32)
    mask_abs, mask_rel, mask_own = mask_of(at), mask_of(relative), mask_of(own_tokens)
    mask_chip = mask_of(y_at * 256 + jnp.arange(256, dtype=jnp.int32))
    position = at - jnp.where(at >= second, spans[0, 1], 0)
    freq = ROPE_BASE ** (-(jnp.arange(32, dtype=F32) * 2.0 / HEAD_SIZE))
    phase = position.astype(F32)[:, None] * jnp.tile(freq, 4)[None, :]
    cosine, sine = jnp.cos(phase), jnp.sin(phase)
    i_at, j_at = at[:, None], at[None, :]
    allowed = (j_at <= i_at) & ((j_at < prompt) | (j_at >= second) | (i_at < second))

    def absolute(values):
        blocks = values.reshape(2, 4, rows, -1)
        blocks = jnp.where(c_at == 0, blocks, blocks[::-1])
        twice = jnp.concatenate([blocks, blocks], 1)
        turned = lax.dynamic_slice_in_dim(twice, (4 - y_at) % 4, 4, 1)
        return turned.transpose(1, 0, 2, 3).reshape(tokens, -1)

    x_f = x_l.astype(F32)
    inv_one = rms_inverse(x_f)
    n1_l = (x_f * inv_one * gain_one).astype(BF)
    n1 = gather_tokens(n1_l)
    og = gather_tokens(og_l)
    base = absolute(mm(n1, all_one))
    low = (base[:, 768:] * jnp.tile(mask_abs, (1, 3))).astype(BF)
    low_q, low_k, low_v = low[:, :128], low[:, 128:256], low[:, 256:]
    q = rope_pair(base[:, :256] + mm_nt(low_q, b_q), cosine, sine).astype(BF)
    k = rope_pair(base[:, 256:512] + mm_nt(low_k, b_k), cosine, sine).astype(BF)
    v = (base[:, 512:768] + mm_nt(low_v, b_v)).astype(BF)
    qh, kh, vh = split_heads(q, True), split_heads(k, True), split_heads(v, False)
    out_heads, log_total = attend(qh, kh, vh, allowed)
    mix = join_heads(out_heads, False)

    chunk = lambda values, d: lax.dynamic_slice_in_dim(values, 256 * ((y_at + d) % 4), 256, 0)
    chip_mix = [chunk(mix, 0)] + [shift(chunk(mix, d), d) for d in (1, 2, 3)]
    partial = jnp.zeros((256, width + 128), F32)
    w_o_cat = jnp.concatenate([w_o, a_o], 1)
    for d in range(4):
        partial = partial + mm(chip_mix[d], chunk(w_o_cat, -d))
    pair = partial.reshape(2, rows, -1)
    mine = lax.dynamic_index_in_dim(pair, c_at, 0, False)
    other = lax.dynamic_index_in_dim(pair, 1 - c_at, 0, False)
    summed = mine + swap(other.astype(BF)).astype(F32)
    low_o = (summed[:, width:] * mask_own).astype(BF)
    resid = x_f + summed[:, :width] + mm_nt(low_o, b_o)

    inv_two = rms_inverse(resid)
    n2_l = (resid * inv_two * gain_two).astype(BF)
    n2 = gather_tokens(n2_l)
    low_gu = (mm(n2, a_gu) * jnp.tile(mask_rel, (1, 2))).astype(BF)
    low_g, low_u = low_gu[:, :128], low_gu[:, 128:]
    gate = mm(n2, w_gu[:, :1024]) + mm_nt(low_g, out_g)
    up = mm(n2, w_gu[:, 1024:]) + mm_nt(low_u, out_u)
    sig = jax.nn.sigmoid(gate)
    act = gate * sig
    hidden = (act * up).astype(BF)
    down = jnp.concatenate([mm(hidden, w_d), mm(hidden, in_ff)], 1)
    down = scatter_tokens(down.reshape(2, 4, rows, -1))
    low_d = (down[:, width:] * mask_own).astype(BF)
    layer_output = (resid + down[:, :width] + mm_nt(low_d, b_d)).astype(BF)

    glow_d = (mm(og, b_d).astype(BF)) * mask_rel.astype(BF)
    grad_hidden = mm_nt(og, w_d) + mm_nt(glow_d, in_ff)
    grad_gate = (grad_hidden * up * sig * (1.0 + gate * (1.0 - sig))).astype(BF)
    grad_up = (grad_hidden * act).astype(BF)
    grad_gu = jnp.concatenate([grad_gate, grad_up], 1)
    back = jnp.concatenate([mm_nt(grad_gu, w_gu), mm(grad_gate, out_g), mm(grad_up, out_u)], 1)
    back = scatter_tokens(back.reshape(2, 4, rows, -1))
    glow_gu = back[:, width:].astype(BF) * jnp.tile(mask_own, (1, 2)).astype(BF)
    grad_n2 = back[:, :width] + mm_nt(glow_gu, a_gu)
    grad_resid = og_l.astype(F32) + norm_back(grad_n2, resid, inv_two, gain_two)
    grad_attn = grad_resid.astype(BF)

    other_attn = swap(grad_attn)
    chip_attn = jnp.where(
        c_at == 0,
        jnp.concatenate([grad_attn, other_attn], 0),
        jnp.concatenate([other_attn, grad_attn], 0),
    )
    chip_glow = mm(chip_attn, b_o).astype(BF) * mask_chip.astype(BF)
    grad_mix = (mm_nt(chip_attn, w_o) + mm_nt(chip_glow, a_o)).astype(BF)
    parts = []
    for d in range(4):
        columns = lax.dynamic_slice_in_dim(grad_mix, 256 * ((y_at + d) % 4), 256, 1)
        part = jnp.concatenate([columns, chip_glow], 1)
        parts.append(part if d == 0 else shift(part, d))
    stacked = jnp.stack([parts[0], parts[3], parts[2], parts[1]])
    stacked = lax.dynamic_slice_in_dim(jnp.concatenate([stacked, stacked], 0), (4 - y_at) % 4, 4, 0)
    stacked = stacked.reshape(tokens, 384)
    gmix, glow_o = stacked[:, :256], stacked[:, 256:]

    gqh, gkh, gvh = attend_back(qh, kh, vh, split_heads(gmix, False), log_total, allowed)
    gq = rope_pair(join_heads(gqh, True).astype(F32), cosine, -sine).astype(BF)
    gk = rope_pair(join_heads(gkh, True).astype(F32), cosine, -sine).astype(BF)
    gv = join_heads(gvh, False)
    gqkv = jnp.concatenate([gq, gk, gv], 1)
    back = jnp.concatenate([mm_nt(gqkv, w_qkv), mm(gq, b_q), mm(gk, b_k), mm(gv, b_v)], 1)
    back = back.reshape(4, 2, rows, -1).transpose(1, 0, 2, 3)
    back = jnp.where(c_at == 0, back, back[::-1])
    back = lax.dynamic_slice_in_dim(jnp.concatenate([back, back], 1), y_at, 4, 1)
    back = scatter_tokens(back)
    glow_qkv = back[:, width:].astype(BF) * jnp.tile(mask_own, (1, 3)).astype(BF)
    grad_n1 = back[:, :width] + mm_nt(glow_qkv, a_qkv)
    grad_in = grad_resid + norm_back(grad_n1, x_f, inv_one, gain_one)

    by_token = jnp.concatenate(
        [
            mm_tn(n1_l, glow_qkv),
            mm_tn(n2_l, glow_gu),
            mm_tn(grad_attn, low_o),
            mm_tn(og_l, low_d),
        ],
        1,
    ).astype(BF)
    by_token = by_token.reshape(16, 8, 16, 7, 128).transpose(1, 3, 0, 2, 4)
    by_token = lax.all_to_all(by_token, "sp", split_axis=0, concat_axis=0, tiled=False)
    by_token = jnp.sum(by_token.astype(F32), 0).astype(BF)
    own_q = mm_tn(gq, low_q).reshape(2, 4, 32, 128).transpose(1, 0, 2, 3).reshape(4, 64, 128)
    own_k = mm_tn(gk, low_k).reshape(2, 4, 32, 128).transpose(1, 0, 2, 3).reshape(4, 64, 128)
    own_v = mm_tn(gv, low_v).reshape(4, 64, 128)
    own_o = mm_tn(mix, glow_o).reshape(4, 64, 128)
    own = jnp.concatenate([own_o, own_q, own_k, own_v], 1).astype(BF)
    own = lax.dynamic_update_slice(jnp.zeros((16, 256, 128), BF), own, (4 * y_at, 0, 0))
    feed = jnp.concatenate(
        [
            mm_tn(hidden, glow_d).reshape(16, 64, 128),
            mm_tn(grad_gate, low_g).reshape(16, 64, 128),
            mm_tn(grad_up, low_u).reshape(16, 64, 128),
        ],
        1,
    ).astype(BF)
    everything = jnp.concatenate(
        [by_token.transpose(1, 0, 2, 3).reshape(16, 7 * 16, 128), feed, own], 1
    )
    everything = lax.all_to_all(everything, "fs", split_axis=0, concat_axis=0, tiled=False)
    everything = jnp.sum(everything.astype(F32), 0).astype(BF)
    everything = lax.all_gather(everything, "sp", axis=0, tiled=False).astype(F32)
    by_token = everything[:, :112].reshape(8, 7, 16, 128).transpose(1, 0, 2, 3).reshape(7, 128, 128)
    feed = everything[:, 112:304].reshape(8, 3, 64, 128).transpose(1, 0, 2, 3).reshape(3, 512, 128)
    own = lax.dynamic_slice_in_dim(everything[:, 304:], 2 * (f_at // 4), 2, 0)
    own = own.reshape(2, 4, 64, 128).transpose(1, 0, 2, 3).reshape(4, 128, 128)
    grad_in_d = jnp.concatenate([by_token[:3], own[:1], by_token[3:5]], 0)
    grad_out_d = jnp.concatenate([own[1:], by_token[5:]], 0)
    return (layer_output[None], grad_in[None], grad_in_d, grad_out_d, feed[:1], feed[1:])


def solution(mesh):
    in_specs = (
        P("fs", "sp", None),
        P("fs", "sp", None),
        P(),
        P("fs", None, None),
        P("fs", None),
        P("fs", None, None),
        P("fs", None),
        P(None, "fs", None),
        P(None, "fs", None),
        P(None, "fs", None),
        P(None, "fs", None),
        P("fs", None),
        P("fs", None),
    )
    out_specs = (
        P("fs", "sp", None),
        P("fs", "sp", None),
        P(None, "fs", None),
        P(None, "fs", None),
        P(None, "fs", None),
        P(None, "fs", None),
    )
    return jax.shard_map(body, mesh=mesh, in_specs=in_specs, out_specs=out_specs, check_vma=False)
```

```python
import functools

import jax
import jax.numpy as jnp
from jax import lax
from jax.experimental import pallas as pl
from jax.experimental.pallas import tpu as pltpu
from jax.sharding import PartitionSpec as P

HEAD_SIZE = 64
ADAPTER_RANK = 16
NORM_EPS = 1e-05
ROPE_BASE = 130000.0
MASK_FILL = -1e30
BF = jnp.bfloat16
F32 = jnp.float32
WIDTH = 2048
ROWS = 128
ORDER = (2, 1, 3, 0)


def mm(left, right):
    return jnp.dot(left, right, preferred_element_type=F32)


def mm_nt(left, right):
    return lax.dot_general(left, right, (((1,), (1,)), ((), ())), preferred_element_type=F32)


def mm_tn(left, right):
    return lax.dot_general(left, right, (((0,), (0,)), ((), ())), preferred_element_type=F32)


def shift(x, chips):
    return lax.ppermute(x, "sp", [(i, ((i // 2 + chips) % 4) * 2 + i % 2) for i in range(8)])


def swap(x):
    return lax.ppermute(x, "sp", [(i, i ^ 1) for i in range(8)])


def shift_z(x, chips):
    return lax.ppermute(x, "fs", [(i, (i + 4 * chips) % 16) for i in range(16)])


def shift_x(x, chips):
    return lax.ppermute(x, "fs", [(i, i - i % 4 + (i + chips) % 4) for i in range(16)])


Y_LINES = [[0, 2, 4, 6], [1, 3, 5, 7]]


def gather_y(x):
    return lax.all_gather(x, "sp", axis=0, tiled=False, axis_index_groups=Y_LINES)


def exchange_y(x):
    return lax.all_to_all(x, "sp", split_axis=0, concat_axis=0, axis_index_groups=Y_LINES)


def line(x, move):
    return [x, move(x, -1), move(x, 2), move(x, 1)]


VMEM = pl.BlockSpec(memory_space=pltpu.VMEM)
SMEM = pl.BlockSpec(memory_space=pltpu.SMEM)


class Info:
    def __init__(self, spans, choice):
        s_at, f_at = lax.axis_index("sp"), lax.axis_index("fs")
        self.values = [s_at >> 1, s_at & 1]
        if spans is None:
            self.values += [None] * 5
        else:
            self.values += [spans[0, 0], spans[0, 0] + spans[0, 1]] + [choice[0, i] for i in range(3)]
        self.values += [f_at >> 2, f_at & 3]

    def __getitem__(self, index):
        return self.values[index]


def call(kernel, outs, scratch, args, limit, deps=()):
    outs = [jax.ShapeDtypeStruct(shape, dtype) for shape, dtype in outs]
    rows, args = args[0], args[1:]
    first = len(rows)
    count, skip = first + len(args), first + len(args) + len(deps)

    def run(*refs):
        info = Info(*refs[:2]) if rows else Info(None, None)
        kernel(info, *refs[first:count], *refs[skip:])

    return pl.pallas_call(
        run,
        out_shape=outs,
        in_specs=[SMEM] * first + [VMEM] * len(args) + [pl.BlockSpec(memory_space=pl.ANY)] * len(deps),
        out_specs=[VMEM] * len(outs),
        scratch_shapes=[pltpu.VMEM(shape, dtype) for shape, dtype in scratch],
        compiler_params=pltpu.CompilerParams(vmem_limit_bytes=limit << 20),
        cost_estimate=pl.CostEstimate(flops=1 << 10, bytes_accessed=1 << 10, transcendentals=0),
    )(*rows, *args, *deps)


def lane_mask(info, first, rows):
    token = first + lax.broadcasted_iota(jnp.int32, (rows, 128), 0)
    lane = lax.broadcasted_iota(jnp.int32, (rows, 128), 1) // ADAPTER_RANK
    chosen = jnp.where(token < info[2], info[4], jnp.where(token < info[3], info[5], info[6]))
    return lane == chosen


def chip_mask(info, step):
    chip, core = (info[0] + step) % 4, info[1]
    return jnp.concatenate(
        [
            lane_mask(info, (2 * chip + core) * ROWS, ROWS),
            lane_mask(info, (2 * chip + 1 - core) * ROWS, ROWS),
        ],
        0,
    )


def turn(a, b, cosine, sine):
    return a * cosine - b * sine, b * cosine + a * sine


def aligned(index, unit):
    return pl.ds(pl.multiple_of(index, unit), unit)


def own_first(info, block):
    return (block // 2) * 256 + ((info[1] + block) % 2) * ROWS


def pack_kernel(info, w, a_in, a_out, w_o, w_pack, ab_pack):
    y_at, core = info[0], info[1]
    i = lax.broadcasted_iota(jnp.int32, (512, 256), 0)
    j = lax.broadcasted_iota(jnp.int32, (512, 256), 1)
    pick_qk = i == ((j % 128) // 32) * 128 + core * 64 + (j // 128) * 32 + j % 32
    pick_v = i == (j // 64) * 128 + core * 64 + j % 64
    for part, pick in enumerate((pick_qk, pick_qk, pick_v)):
        wide = w[part, :, aligned(512 * y_at, 512)]
        w_pack[:, 256 * part : 256 * part + 256] = mm(wide, pick.astype(BF)).astype(BF)
    half = aligned(64 * core, 64)
    for part in range(3):
        ab_pack[:, 128 * part : 128 * part + 128] = a_in[part]
    ab_pack[:64, 384:512] = a_out[0, half, :]
    ab_pack[64:, 384:512] = a_out[1, half, :]
    ab_pack[:64, 512:640] = a_out[2, half, :]
    ab_pack[64:, 512:640] = a_in[3, half, :]
    ab_pack[:, 640:] = a_out[3]
    for part in range(8):
        lanes = slice(256 * part, 256 * part + 256)
        w_pack[16 * part : 16 * part + 16, 768:] = w_o[aligned(64 * core + 16 * y_at, 16), lanes]


def pack(w, a_in, a_out, w_o):
    return call(
        pack_kernel,
        [((ROWS, 1024), BF), ((ROWS, 768), BF)],
        [],
        ((), w, a_in, a_out, w_o),
        8,
    )


def pack_feed_kernel(info, w_gu, w_d, a_in, a_out, in_ff, out_ff, out):
    y_at, core = info[0], info[1]
    i = lax.broadcasted_iota(jnp.int32, (128, 128), 0)
    j = lax.broadcasted_iota(jnp.int32, (128, 128), 1)
    first = ((j < 64) & (i == j + 64 * core)).astype(BF)
    second = ((j >= 64) & (i == j - 64 + 64 * core)).astype(BF)
    for part in range(2):
        for block in range(8):
            left = w_gu[:, part, aligned(1024 * block + 128 * y_at, 128)]
            right = w_gu[:, part, aligned(1024 * block + 512 + 128 * y_at, 128)]
            lanes = slice(1024 * part + 128 * block, 1024 * part + 128 * block + 128)
            out[:ROWS, lanes] = (mm(left, first) + mm(right, second)).astype(BF)
    out[:ROWS, 2048:2176] = a_in[4]
    out[:ROWS, 2176:2304] = a_in[5]
    out[:ROWS, 2304:] = a_out[4]
    eighth = aligned(64 * (2 * y_at + core), 64)
    out[ROWS:, :WIDTH] = w_d[eighth, :]
    out[ROWS:, 2048:2176] = in_ff[0, eighth, :]
    out[ROWS:, 2176:2304] = out_ff[0, eighth, :]
    out[ROWS:, 2304:] = out_ff[1, eighth, :]


def pack_feed(deps, *args):
    return call(pack_feed_kernel, [((192, 2432), BF)], [], ((), *args), 12, deps)[0]


def stack_rows(deps, *lists):
    counts = [len(parts) for parts in lists]

    def kernel(info, *refs):
        at = 0
        for count, out in zip(counts, refs[sum(counts) :]):
            for i in range(count):
                out[i] = refs[at + i][...]
            at += count

    outs = [((len(parts),) + parts[0].shape, parts[0].dtype) for parts in lists]
    return call(kernel, outs, [], ((), *sum(lists, [])), 8, deps)


def order_chips(parts):
    def kernel(info, *refs):
        for d, part in enumerate(refs[:-1]):
            refs[-1][(info[0] + d) % 4] = part[...]

    return call(kernel, [((4,) + parts[0].shape, parts[0].dtype)], [], ((), *parts), 8)[0]


def stack_output(deps, parts):
    def kernel(info, *refs):
        for i, part in enumerate(refs[:-1]):
            refs[-1][i] = part[:, :, 768:]

    return call(kernel, [((4, 4, ROWS, 256), BF)], [], ((), *parts), 8, deps)[0]


def stack_output(deps, parts):
    def kernel(info, *refs):
        for i, part in enumerate(refs[:-1]):
            refs[-1][i] = part[:, :, 768:]

    return call(kernel, [((4, 4, ROWS, 256), BF)], [], ((), *parts), 8, deps)[0]


def hold(deps, *pairs):
    firsts = [first for _, first in pairs]

    def kernel(info, *refs):
        for first, ref, out in zip(firsts, refs, refs[len(firsts) :]):
            out[...] = ref[first : first + 2]

    arrays = [array for array, _ in pairs]
    outs = [((2,) + array.shape[1:], array.dtype) for array in arrays]
    return call(kernel, outs, [], ((), *arrays), 8, deps)


def norm_kernel(info, x, gain, out):
    values = x[...].astype(F32)
    inverse = lax.rsqrt(jnp.mean(values * values, -1, keepdims=True) + NORM_EPS)
    out[...] = (values * inverse * gain[0:1, :]).astype(BF)


def norm_first(deps, info, x, gain):
    return call(norm_kernel, [((ROWS, WIDTH), BF)], [], (info, x, gain), 4, deps)[0]


def copy_kernel(info, x, out):
    out[...] = x[...]


def copy_after(deps, info, x):
    return call(copy_kernel, [(x.shape, x.dtype)], [], (info, x), 4, deps)[0]


def qkv_kernel(info, a0, a1, a2, a3, b0, b1, b2, b3, near, far, cosine, sine, *refs):
    q, k, v, low_out, n1, w, a, b_q, b_k, b_v, a_o, b_o, rest = refs
    z_at, x_at, y_at, core = info[7], info[8], info[0], info[1]
    for dz in range(4):
        for dx in range(4):
            f = ((z_at + dz) % 4) * 4 + (x_at + dx) % 4
            rows = aligned(f * ROWS, ROWS)
            w[rows, :] = (a0, a1, a2, a3)[dz][dx, :, :768]
            piece = (b0, b1, b2, b3)[dx]
            a[rows, :] = piece[dz, :, :384]
            rest[rows, :] = piece[dz, :, 384:640]
            b_o[rows, :] = piece[dz, :, 640:]
    for head in range(4):
        first = (4 * y_at + head) * ROWS
        for half in range(2):
            to = slice(half * 128 + head * 32, half * 128 + head * 32 + 32)
            b_q[to, :] = rest[aligned(first + 32 * half, 32), :128]
            b_k[to, :] = rest[aligned(first + 64 + 32 * half, 32), :128]
        b_v[64 * head : 64 * head + 64, :] = rest[aligned(first, 64), 128:]
    for f in range(16):
        a_o[64 * f : 64 * f + 64, :] = rest[f * ROWS + 64 : f * ROWS + 128, 128:]
    for block in range(8):
        d, same = block // 2, core == block % 2
        n1[block * ROWS : block * ROWS + ROWS, :] = jnp.where(same, near[d], far[d])
    for chip in range(4):
        at = slice(256 * chip, 256 * chip + 256)
        rows = n1[at, :]
        mask = lane_mask(info, 256 * chip, 256)
        low = jnp.where(jnp.concatenate([mask] * 3, 1), mm(rows, a[...]), 0.0).astype(BF)
        low_out[at, :] = low
        cos, sin = cosine[at, :], sine[at, :]
        for j, (b, out) in enumerate(((b_q, q), (b_k, k))):
            base = mm(rows, w[:, 256 * j : 256 * j + 256])
            values = base + mm_nt(low[:, 128 * j : 128 * j + 128], b[...])
            first, second = turn(values[:, :128], values[:, 128:], cos, sin)
            out[at, :128] = first.astype(BF)
            out[at, 128:] = second.astype(BF)
        v[at, :] = (mm(rows, w[:, 512:]) + mm_nt(low[:, 256:], b_v[...])).astype(BF)


def project_qkv(deps, info, w_parts, ab_parts, near, far, cosine, sine):
    return call(
        qkv_kernel,
        [
            ((1024, 256), BF),
            ((1024, 256), BF),
            ((1024, 256), BF),
            ((1024, 384), BF),
            ((1024, WIDTH), BF),
            ((WIDTH, 768), BF),
            ((WIDTH, 384), BF),
            ((256, 128), BF),
            ((256, 128), BF),
            ((256, 128), BF),
            ((1024, 128), BF),
            ((WIDTH, 128), BF),
        ],
        [((WIDTH, 256), BF)],
        (info, *w_parts, *ab_parts, near, far, cosine, sine),
        16,
        deps,
    )


def head_lanes(head, rows, paired):
    lane = lax.broadcasted_iota(jnp.int32, (rows, 256), 1)
    return ((lane % 128) // 32 if paired else lane // 64) == head


def key_bias(info, block):
    n = 256 * (block + 1)
    j = lax.broadcasted_iota(jnp.int32, (n, 256), 0)
    i = 256 * block + lax.broadcasted_iota(jnp.int32, (n, 256), 1)
    allowed = (j <= i) & ((j < info[2]) | (j >= info[3]) | (i < info[3]))
    return jnp.where(allowed, 0.0, MASK_FILL)


def attend_kernel(info, q, k, v, mix, log_total, v_heads, probs):
    for head in range(4):
        v_heads[head] = jnp.where(head_lanes(head, 1024, False), v[...], 0)
    for block in range(4):
        n = 256 * (block + 1)
        rows = slice(256 * block, 256 * block + 256)
        bias = key_bias(info, block)
        out = jnp.zeros((256, 256), F32)
        for head in range(4):
            q_head = jnp.where(head_lanes(head, 256, True), q[rows, :], 0) * jnp.array(0.125, BF)
            scores = mm_nt(k[:n, :], q_head) + bias
            top = jnp.max(scores, 0, keepdims=True)
            weights = jnp.exp(scores - top)
            total = jnp.sum(weights, 0, keepdims=True)
            log_total[head : head + 1, rows] = top + jnp.log(total)
            probs[head, :n, :] = (weights * (1.0 / total)).astype(BF)
        for head in range(4):
            out = out + mm_tn(probs[head, :n, :], v_heads[head, :n, :])
        out = out.astype(BF)
        for part in range(2):
            row = own_first(info, 2 * block + part)
            mix[aligned(row, ROWS), :] = out[part * ROWS : part * ROWS + ROWS]


def attend(info, q, k, v):
    return call(
        attend_kernel,
        [((1024, 256), BF), ((8, 1024), F32)],
        [((4, 1024, 256), BF), ((4, 1024, 256), BF)],
        (info, q, k, v),
        16,
    )


def attend_back_kernel(
    info, q, k, v, g0, g1, g2, g3, log_total, cosine, sine, out, q_heads, g_heads, k_heads, probs, grads, dk, dv
):
    chip, core = info[0], info[1]
    for d, part in enumerate((g0, g1, g2, g3)):
        block = (chip - d + 4) % 4
        for other in range(2):
            rows = part[other * ROWS : other * ROWS + ROWS, :256]
            second = (core + other) % 2
            for head in range(4):
                g_heads[block, aligned(256 * head + ROWS * second, ROWS), :] = jnp.where(
                    head_lanes(head, ROWS, False), rows, 0
                )
    for head in range(4):
        k_heads[head] = jnp.where(head_lanes(head, 1024, True), k[...], 0) * jnp.array(0.125, BF)
    dk[...] = jnp.zeros_like(dk)
    dv[...] = jnp.zeros_like(dv)

    def unrotate(values, rows):
        a, b = values[:, :128].astype(F32), values[:, 128:].astype(F32)
        first, last = turn(a, b, cosine[rows, :], -sine[rows, :])
        return jnp.concatenate([first, last], 1).astype(BF)

    for block in range(4):
        n = 256 * (block + 1)
        rows = slice(256 * block, 256 * block + 256)
        bias = key_bias(info, block)
        for head in range(4):
            at = slice(256 * head, 256 * head + 256)
            q_head = jnp.where(head_lanes(head, 256, True), q[rows, :], 0) * jnp.array(0.125, BF)
            q_heads[at, :] = q_head
            scores = mm_nt(k[:n, :], q_head) + bias
            p = jnp.exp(scores - log_total[head : head + 1, rows])
            dp = mm_nt(v[:n, :], g_heads[block, at, :])
            inner = jnp.sum(p * dp, 0, keepdims=True)
            probs[:n, at] = p.astype(BF)
            grads[:n, at] = (p * (dp - inner)).astype(BF)
        dv[:n, :] += mm(probs[:n, :], g_heads[block])
        dk[:n, :] += mm(grads[:n, :], q_heads[...])
        dq = jnp.zeros((256, 256), F32)
        for head in range(4):
            dq = dq + mm_tn(grads[:n, 256 * head : 256 * head + 256], k_heads[head, :n, :])
        out[rows, 0:256] = unrotate(dq.astype(BF), rows)
    for block in range(4):
        rows = slice(256 * block, 256 * block + 256)
        out[rows, 256:512] = unrotate(dk[rows, :].astype(BF), rows)
        out[rows, 512:768] = dv[rows, :].astype(BF)


def attend_back(info, q, k, v, parts, log_total, cosine, sine):
    return call(
        attend_back_kernel,
        [((1024, 768), BF)],
        [
            ((1024, 256), BF),
            ((4, 1024, 256), BF),
            ((4, 1024, 256), BF),
            ((1024, 1024), BF),
            ((1024, 1024), BF),
            ((1024, 256), F32),
            ((1024, 256), F32),
        ],
        (info, q, k, v, *parts, log_total, cosine, sine),
        20,
    )[0]


def output_kernel(info, parts, w0, w1, w2, w3, a_o, keep, send, w, mix):
    z_at, x_at = info[7], info[8]
    for dy, piece in enumerate((w0, w1, w2, w3)):
        chip = (info[0] + dy) % 4
        mix[:, 256 * dy : 256 * dy + 256] = parts[dy]
        for dz in range(4):
            for dx in range(4):
                f = ((z_at + dz) % 4) * 4 + (x_at + dx) % 4
                rows = aligned(f * 64 + 16 * chip, 16)
                for part in range(8):
                    w[rows, 256 * part : 256 * part + 256] = piece[dz, dx, 16 * part : 16 * part + 16]
    keep[:, :WIDTH] = mm(mix[:ROWS, :], w[...])
    keep[:, WIDTH:] = mm(mix[:ROWS, :], a_o[...])
    send[:, :WIDTH] = mm(mix[ROWS:, :], w[...]).astype(BF)
    send[:, WIDTH:] = mm(mix[ROWS:, :], a_o[...]).astype(BF)


def project_output(info, mixes, pieces, a_o):
    return call(
        output_kernel,
        [((ROWS, 2176), F32), ((ROWS, 2176), BF), ((1024, WIDTH), BF)],
        [((256, 1024), BF)],
        (info, mixes, *pieces, a_o),
        8,
    )


def middle_kernel(info, keep, got, x, b_o, gain, resid, n2, low):
    summed = keep[...] + got[...].astype(F32)
    mask = lane_mask(info, (2 * info[0] + info[1]) * ROWS, ROWS)
    low_o = jnp.where(mask, summed[:, WIDTH:], 0.0).astype(BF)
    low[...] = low_o
    values = x[...].astype(F32) + summed[:, :WIDTH] + mm_nt(low_o, b_o[...])
    resid[...] = values
    inverse = lax.rsqrt(jnp.mean(values * values, -1, keepdims=True) + NORM_EPS)
    n2[...] = (values * inverse * gain[1:2, :]).astype(BF)


def middle(deps, info, keep, got, x, b_o, gain):
    return call(
        middle_kernel,
        [((ROWS, WIDTH), F32), ((ROWS, WIDTH), BF), ((ROWS, 128), BF)],
        [],
        (info, keep, got, x, b_o, gain),
        10,
        deps,
    )


def feed_kernel(
    step, info, n_near, n_far, g_near, g_far, w_g, w_u, w_d, a_gu, b_d, ff,
    keep_down, send_down, keep_back, send_back, hidden, grad_gate, grad_up, lows, n_rows, g_rows,
):
    chip = (info[0] + step) % 4
    n_rows[:ROWS] = n_near[chip]
    n_rows[ROWS:] = n_far[chip]
    g_rows[:ROWS] = g_near[chip]
    g_rows[ROWS:] = g_far[chip]
    mask = chip_mask(info, step)
    twice = jnp.concatenate([mask, mask], 1)
    low = jnp.where(twice, mm(n_rows[...], a_gu[...]), 0.0).astype(BF)
    glow = jnp.where(mask, mm(g_rows[...], b_d[...]), 0.0).astype(BF)
    lows[:, :256] = low
    lows[:, 256:384] = glow
    for block in range(4):
        at = slice(256 * block, 256 * block + 256)
        gate = mm(n_rows[...], w_g[:, at]) + mm_nt(low[:, :128], ff[at, 128:256])
        up = mm(n_rows[...], w_u[:, at]) + mm_nt(low[:, 128:], ff[at, 256:])
        grad_hidden = mm_nt(g_rows[...], w_d[at, :]) + mm_nt(glow, ff[at, :128])
        sig = 1.0 / (1.0 + jnp.exp(-gate))
        act = gate * sig
        hidden[:, at] = (act * up).astype(BF)
        grad_gate[:, at] = (grad_hidden * up * sig * (1.0 + gate * (1.0 - sig))).astype(BF)
        grad_up[:, at] = (grad_hidden * act).astype(BF)

    def put(keep, send, at, values):
        keep[:, at] = values[:ROWS]
        send[:, at] = values[ROWS:].astype(BF)

    for block in range(8):
        at = slice(256 * block, 256 * block + 256)
        put(keep_back, send_back, at, mm_nt(grad_gate[...], w_g[at, :]) + mm_nt(grad_up[...], w_u[at, :]))
        put(keep_down, send_down, at, mm(hidden[...], w_d[:, at]))
    glow_g = mm(grad_gate[...], ff[:, 128:256])
    glow_u = mm(grad_up[...], ff[:, 256:])
    low_d = mm(hidden[...], ff[:, :128])
    put(keep_back, send_back, slice(WIDTH, WIDTH + 128), glow_g)
    put(keep_back, send_back, slice(WIDTH + 128, WIDTH + 256), glow_u)
    put(keep_down, send_down, slice(WIDTH, WIDTH + 128), low_d)
    lows[:, 384:512] = jnp.where(mask, glow_g, 0.0).astype(BF)
    lows[:, 512:640] = jnp.where(mask, glow_u, 0.0).astype(BF)
    lows[:, 640:] = jnp.where(mask, low_d, 0.0).astype(BF)


def feed(step, deps, info, n_near, n_far, g_near, g_far, *weights):
    return call(
        functools.partial(feed_kernel, step),
        [
            ((ROWS, 2176), F32),
            ((ROWS, 2176), BF),
            ((ROWS, 2304), F32),
            ((ROWS, 2304), BF),
            ((256, 1024), BF),
            ((256, 1024), BF),
            ((256, 1024), BF),
            ((256, 768), BF),
        ],
        [((256, WIDTH), BF), ((256, WIDTH), BF)],
        (info, n_near, n_far, g_near, g_far, *weights),
        14,
        deps,
    )


def early_kernel(info, n_near, n_far, g_near, g_far, *refs):
    chunks, by_token, by_hidden = [refs[4 * i : 4 * i + 4] for i in range(4)], refs[-2], refs[-1]
    flip = lambda values: values.astype(F32).T.astype(BF)
    thins = [flip(chunk[3][...]) for chunk in chunks]
    rows = lambda i, j: thins[i][128 * j : 128 * j + 128]
    for j, (row, name) in enumerate(((2, 0), (0, 1), (1, 2))):
        total = sum(mm(rows(i, row), chunks[i][name][...]) for i in range(4))
        by_hidden[:, 128 * j : 128 * j + 128] = total.T.astype(BF)
    for j, (row, near, far) in enumerate(((3, n_near, n_far), (4, n_near, n_far), (5, g_near, g_far))):
        total = 0.0
        for i, d in enumerate(ORDER):
            chip = (info[0] + d) % 4
            total = total + mm(rows(i, row)[:, :ROWS], near[chip]) + mm(rows(i, row)[:, ROWS:], far[chip])
        by_token[:, 128 * j : 128 * j + 128] = total.T.astype(BF)


def early_sums(tokens, chunks, deps):
    args = [(), *tokens] + [part for chunk in chunks for part in chunk]
    return call(
        early_kernel, [((WIDTH, 384), BF), ((1024, 384), BF)], [], args, 8, deps
    )


def between_kernel(info, own, r1, r2, r3, a_gu, resid, og, gain, grad_resid, grad_attn):
    total = own[...] + r1[...].astype(F32) + r2[...].astype(F32) + r3[...].astype(F32)
    mask = lane_mask(info, (2 * info[0] + info[1]) * ROWS, ROWS)
    glow = jnp.where(jnp.concatenate([mask, mask], 1), total[:, WIDTH:], 0.0).astype(BF)
    grad = total[:, :WIDTH] + mm_nt(glow, a_gu[...])
    values = resid[...]
    inverse = lax.rsqrt(jnp.mean(values * values, -1, keepdims=True) + NORM_EPS)
    result = og[...].astype(F32) + norm_back(grad, values, inverse, gain[1:2, :])
    grad_resid[...] = result
    grad_attn[...] = result.astype(BF)


def between(deps, info, own, r1, r2, r3, a_gu, resid, og, gain):
    return call(
        between_kernel,
        [((ROWS, WIDTH), F32), ((ROWS, WIDTH), BF)],
        [],
        (info, own, r1, r2, r3, a_gu, resid, og, gain),
        10,
        deps,
    )


def combine_kernel(info, by_token, by_hidden, out):
    for f in range(16):
        out[f, :ROWS, :] = by_token[f * ROWS : f * ROWS + ROWS, :]
        out[f, ROWS:, :] = by_hidden[64 * f : 64 * f + 64, :]


def combine(by_token, by_hidden):
    return call(combine_kernel, [((16, 192, 384), BF)], [], ((), by_token, by_hidden), 8)[0]


def down_kernel(info, k0, k1, k2, k3, got, own, *outs):
    for i, (d, keep) in enumerate(zip(ORDER, (k0, k1, k2, k3))):
        total = keep[...] + got[i].astype(F32)
        if d:
            outs[d - 1][...] = total.astype(BF)
        else:
            own[...] = total


def down_pair(deps, kept, got):
    return call(
        down_kernel,
        [((ROWS, 2176), F32)] + [((ROWS, 2176), BF)] * 3,
        [],
        ((), *kept, got),
        8,
        deps,
    )


def result_kernel(info, own, r1, r2, r3, resid, b_d, out):
    total = own[...] + r1[...].astype(F32) + r2[...].astype(F32) + r3[...].astype(F32)
    mask = lane_mask(info, (2 * info[0] + info[1]) * ROWS, ROWS)
    low = jnp.where(mask, total[:, WIDTH:], 0.0).astype(BF)
    out[...] = (resid[...] + total[:, :WIDTH] + mm_nt(low, b_d[...])).astype(BF)


def result(info, own, r1, r2, r3, resid, b_d):
    return call(
        result_kernel, [((ROWS, WIDTH), BF)], [], (info, own, r1, r2, r3, resid, b_d), 10
    )[0]


def output_back_kernel(info, own, other, low_own, low_other, b_o, w_o, a_o, p0, p1, p2, p3, half, grad, mix):
    grad[:ROWS] = own[...]
    grad[ROWS:] = other[...]
    glow = jnp.where(chip_mask(info, 0), mm(grad[...], b_o[...]), 0.0).astype(BF)
    for chip in range(4):
        at = slice(256 * chip, 256 * chip + 256)
        mix[:, at] = (mm_nt(grad[...], w_o[at, :]) + mm_nt(glow, a_o[at, :])).astype(BF)
    for d, part in enumerate((p0, p1, p2, p3)):
        part[:, :256] = mix[:, aligned(256 * ((info[0] + d) % 4), 256)]
        part[:, 256:] = glow
    flip = lambda values: values.astype(F32).T.astype(BF)
    total = (mm(flip(low_own[...]), grad[:ROWS]) + mm(flip(low_other[...]), grad[ROWS:])).T.astype(BF)
    for f in range(16):
        rows = total[f * ROWS : f * ROWS + ROWS]
        half[64 * f : 64 * f + 64, :] = jnp.where(info[1] == 0, rows[:64], rows[64:])


def output_back(info, own, other, low_own, low_other, b_o, w_o, a_o):
    return call(
        output_back_kernel,
        [((256, 384), BF)] * 4 + [((1024, 128), BF)],
        [((256, WIDTH), BF), ((256, 1024), BF)],
        (info, own, other, low_own, low_other, b_o, w_o, a_o),
        8,
    )


def pick_rows(info, g, core, out):
    for d in range(4):
        chip = (info[0] + d) % 4
        out[d * ROWS : d * ROWS + ROWS, :] = g[aligned(256 * chip + ROWS * core, ROWS), :]


def input_send_kernel(info, g, w, send, rows):
    pick_rows(info, g, 1 - info[1], rows)
    for block in range(8):
        at = slice(256 * block, 256 * block + 256)
        send[:, at] = mm_nt(rows[...], w[at, :]).astype(BF)


def input_send(info, g, w):
    return call(input_send_kernel, [((512, WIDTH), BF)], [((512, 768), BF)], (info, g, w), 8)[0]


def input_pair_kernel(info, g, w, got, own, p1, p2, p3, rows):
    pick_rows(info, g, info[1], rows)
    for block in range(8):
        at = slice(256 * block, 256 * block + 256)
        total = mm_nt(rows[...], w[at, :]) + got[:, at].astype(F32)
        own[:, at] = total[:ROWS]
        for d, out in enumerate((p1, p2, p3)):
            out[:, at] = total[ROWS * (d + 1) : ROWS * (d + 2)].astype(BF)


def input_pair(deps, info, g, w, got):
    return call(
        input_pair_kernel,
        [((ROWS, WIDTH), F32)] + [((ROWS, WIDTH), BF)] * 3,
        [((512, 768), BF)],
        (info, g, w, got),
        8,
        deps,
    )


def squeeze(rows):
    i = lax.broadcasted_iota(jnp.int32, rows, 0) % ADAPTER_RANK
    j = lax.broadcasted_iota(jnp.int32, rows, 1) % ADAPTER_RANK
    return (i == j).astype(BF)


def narrow_kernel(info, g, b_q, b_k, b_v, low, mix, o0, o1, o2, o3, narrow, own):
    mask = lane_mask(info, 0, 1024)
    fold = squeeze((16, 128))
    flip = lambda values: values.astype(F32).T.astype(BF)
    for j, b in enumerate((b_q, b_k, b_v)):
        term = jnp.where(mask, mm(g[:, 256 * j : 256 * j + 256], b[...]), 0.0).astype(BF)
        narrow[16 * j : 16 * j + 16, :] = mm_nt(fold, term).astype(BF)
    low_t = flip(low[...])
    for j in range(3):
        total = mm(low_t[128 * j : 128 * j + 128], g[:, 256 * j : 256 * j + 256]).T.astype(BF)
        lanes = slice(128 * (j + 1), 128 * (j + 2))
        for head in range(4):
            if j == 2:
                own[head, :, lanes] = total[64 * head : 64 * head + 64]
            else:
                own[head, :32, lanes] = total[32 * head : 32 * head + 32]
                own[head, 32:, lanes] = total[128 + 32 * head : 160 + 32 * head]
    total = sum(
        mm(flip(part[:, 256:]), mix[aligned(256 * ((info[0] - d + 4) % 4), 256), :])
        for d, part in enumerate((o0, o1, o2, o3))
    ).T.astype(BF)
    for head in range(4):
        own[head, :, :128] = total[64 * head : 64 * head + 64]


def narrow_sums(deps, info, g, b_q, b_k, b_v, low, mix, parts):
    return call(
        narrow_kernel,
        [((48, 1024), BF), ((4, 64, 512), BF)],
        [],
        (info, g, b_q, b_k, b_v, low, mix, *parts),
        10,
        deps,
    )


def late_kernel(info, n0, n1, n2, n3, rows, out, glow_own):
    total = n0[...].astype(F32) + n1[...].astype(F32) + n2[...].astype(F32) + n3[...].astype(F32)
    total = total.astype(BF)
    s_at = 2 * info[0] + info[1]
    mask = lane_mask(info, 0, 1024)
    spread = squeeze((16, 128))
    wide = []
    for j in range(3):
        term = jnp.where(mask, mm_tn(total[16 * j : 16 * j + 16], spread), 0.0)
        wide.append(term)
    mask_own = lane_mask(info, s_at * ROWS, ROWS)
    for j in range(3):
        piece = jnp.zeros((ROWS, 128), F32)
        for block in range(8):
            piece = jnp.where(s_at == block, wide[j][block * ROWS : block * ROWS + ROWS], piece)
        glow_own[:, 128 * j : 128 * j + 128] = jnp.where(mask_own, piece, 0.0).astype(BF)
    thin = jnp.concatenate([term.T.astype(BF) for term in wide], 0)
    for f in range(8):
        at = slice(256 * f, 256 * f + 256)
        total = mm(thin, rows[:, at]).T
        for second in range(2):
            piece = jnp.zeros((16, 384), F32)
            for s in range(8):
                first = second * ROWS + 16 * s
                piece = jnp.where(s_at == s, total[first : first + 16], piece)
            out[2 * f + second] = piece.astype(BF)


def late_sums(deps, info, parts, rows):
    return call(
        late_kernel,
        [((16, 16, 384), BF), ((ROWS, 384), BF)],
        [],
        (info, *parts, rows),
        10,
        deps,
    )


def groups_kernel(info, values, out):
    total = values[0].astype(F32)
    for f in range(1, 16):
        total = total + values[f].astype(F32)
    out[...] = total.astype(BF)


def sum_groups(deps, values):
    return call(groups_kernel, [(values.shape[1:], BF)], [], ((), values), 8, deps)[0]


def last_kernel(info, own, r1, r2, r3, glow, a, resid_grad, x, gain, out):
    grad = own[...] + r1[...].astype(F32) + r2[...].astype(F32) + r3[...].astype(F32) + mm_nt(glow[...], a[...])
    values = x[...].astype(F32)
    inverse = lax.rsqrt(jnp.mean(values * values, -1, keepdims=True) + NORM_EPS)
    out[...] = resid_grad[...] + norm_back(grad, values, inverse, gain[0:1, :])


def last(info, own, r1, r2, r3, glow, a, resid_grad, x, gain):
    return call(
        last_kernel,
        [((ROWS, WIDTH), F32)],
        [],
        (info, own, r1, r2, r3, glow, a, resid_grad, x, gain),
        10,
    )[0]


def rms_inverse(values):
    return lax.rsqrt(jnp.mean(values * values, -1, keepdims=True) + NORM_EPS)


def norm_back(grad_norm, values, inverse, gain):
    normed = values * inverse
    scaled = grad_norm * gain
    return inverse * (scaled - normed * jnp.mean(scaled * normed, -1, keepdims=True))


def body(
    layer_input,
    output_gradient,
    norm_gain_pair,
    query_key_value_weight,
    output_weight,
    gate_up_weight,
    down_weight,
    adapter_input_model,
    adapter_output_model,
    adapter_input_hidden,
    adapter_output_hidden,
    spans,
    adapter_choice_rows,
):
    f_at, s_at = lax.axis_index("fs"), lax.axis_index("sp")
    y_at, c_at = s_at >> 1, s_at & 1
    z_at = f_at >> 2
    x_l = layer_input[0]
    og_l = output_gradient[0]
    rows = x_l.shape[0]
    tokens = 8 * rows
    gains = norm_gain_pair
    info = (spans, adapter_choice_rows)

    w_pack, ab_pack = pack(
        query_key_value_weight.transpose(1, 0, 2), adapter_input_model, adapter_output_model, output_weight
    )
    w_line, ab_line = line(w_pack, shift_x), line(ab_pack, shift_z)
    w_line, ab_line = stack_rows((), w_line, ab_line)
    w_parts, ab_parts = line(w_line, shift_z), line(ab_line, shift_x)
    n1_l = norm_first((w_pack,), info, x_l, gains)
    near = gather_y(n1_l)
    far = swap(near)
    g_near = gather_y(og_l)
    g_far = swap(g_near)
    feed_pack = pack_feed(
        (*w_parts[1:], *ab_parts[1:]),
        gate_up_weight,
        down_weight,
        adapter_input_model,
        adapter_output_model,
        adapter_input_hidden,
        adapter_output_hidden,
    )
    feed_all = lax.all_gather(feed_pack, "fs", axis=0, tiled=False)
    w_g = feed_all[:, :ROWS, :1024].reshape(WIDTH, 1024)
    w_u = feed_all[:, :ROWS, 1024:2048].reshape(WIDTH, 1024)
    a_gu = feed_all[:, :ROWS, 2048:2304].reshape(WIDTH, 256)
    b_d = feed_all[:, :ROWS, 2304:].reshape(WIDTH, 128)
    w_d = feed_all[:, ROWS:, :2048].reshape(1024, WIDTH)
    ff = feed_all[:, ROWS:, 2048:].reshape(1024, 384)

    at = jnp.arange(tokens, dtype=jnp.int32)
    position = at - jnp.where(at >= spans[0, 0] + spans[0, 1], spans[0, 1], 0)
    freq = ROPE_BASE ** (-(jnp.arange(32, dtype=F32) * 2.0 / HEAD_SIZE))
    phase = position.astype(F32)[:, None] * jnp.tile(freq, 4)[None, :]
    cosine, sine = jnp.cos(phase), jnp.sin(phase)

    o_parts = line(stack_output(tuple(ab_parts[1:]), w_parts), shift)
    q, k, v, low_qkv, n1, w_qkv, a_qkv, b_q, b_k, b_v, a_o, b_o = project_qkv(
        (), info, w_parts, ab_parts, near, far, cosine, sine
    )
    mix, log_total = attend(info, q, k, v)
    mixes = exchange_y(mix.reshape(4, 256, 256))
    keep, send, w_o = project_output(info, mixes, o_parts, a_o)
    resid, n2_l, low_o = middle((), info, keep, swap(send), x_l, b_o, gains)

    n_near = order_chips(line(n2_l, shift))
    token_rows = (n_near, swap(n_near), g_near, g_far)
    chunks, kept, sent, back, got = [], [], [], {}, []
    for d in ORDER:
        deps = [chunks[-1][-1]] if chunks else []
        deps += got[-2:-1]
        keep_down, send_down, keep_back, send_back, *chunk = feed(
            d, deps, info, *token_rows, w_g, w_u, w_d, a_gu, b_d, ff
        )
        chunks.append(chunk)
        kept.append(keep_down)
        sent.append(send_down)
        got.append(swap(send_back))
        pair = keep_back + got[-1].astype(F32)
        back[d] = shift(pair.astype(BF), d if d < 3 else -1) if d else pair
    by_token, by_hidden = early_sums(token_rows, chunks, [got[-1]])
    early = combine(by_token, by_hidden)
    low_other = swap(low_o)
    early = lax.all_to_all(early, "fs", split_axis=0, concat_axis=0, tiled=False)
    grad_resid, grad_attn = between((by_token,), info, back[0], back[1], back[2], back[3], a_gu, resid, og_l, gains)

    *parts, half_o = output_back(info, grad_attn, swap(grad_attn), low_o, low_other, b_o, w_o, a_o)
    parts = [parts[0]] + [shift(parts[d], d) for d in (1, 2, 3)]
    g_all = attend_back(info, q, k, v, parts, log_total, cosine, sine)
    send = input_send(info, g_all, w_qkv)
    narrow, own = narrow_sums((send,), info, g_all, b_q, b_k, b_v, low_qkv, mix, parts)
    pair, *total = input_pair((narrow,), info, g_all, w_qkv, swap(send))
    total = [shift(total[d - 1], d if d < 3 else -1) for d in (1, 2, 3)]
    narrow = (narrow.astype(F32) + swap(narrow).astype(F32)).astype(BF)
    late, glow_own = late_sums((pair, early), info, line(narrow, shift), n1)
    grad_in = last(info, pair, *total, glow_own, a_qkv, grad_resid, x_l, gains)
    down = down_pair(tuple(total), kept, swap(stack_rows((g_all,), sent)[0]))
    layer_output = result(
        info, down[0], *[shift(down[d], d if d < 3 else -1) for d in (1, 2, 3)], resid, b_d
    )

    def to_all(values):
        mine = jnp.stack(line(values, shift))
        other = swap(mine)
        both = jnp.stack([jnp.where(c_at == 0, mine, other), jnp.where(c_at == 0, other, mine)], 1)
        both = lax.dynamic_slice_in_dim(jnp.concatenate([both, both], 0), (4 - y_at) & 3, 4, 0)
        return both.astype(F32)

    early = to_all(sum_groups((late,), early))
    spread = jnp.sum(early[:, :, :128], (0, 1)).reshape(128, 3, 128).transpose(1, 0, 2)
    fed = early[:, :, 128:].reshape(512, 3, 128).transpose(1, 0, 2)
    own = lax.dynamic_update_slice(jnp.zeros((16, 16, 2048), BF), own.reshape(4, 16, 2048), (4 * y_at, 0, 0))
    final = jnp.concatenate([late, own, half_o.reshape(16, 16, 512)], 2)
    final = lax.all_to_all(final, "fs", split_axis=0, concat_axis=0, tiled=False)
    final = to_all(sum_groups(total, final))
    first = final[..., :384].reshape(128, 3, 128).transpose(1, 0, 2)
    own = lax.dynamic_index_in_dim(final[..., 384:2432], z_at, 0, False).reshape(128, 4, 128).transpose(1, 0, 2)
    b_o_grad = jnp.sum(final[..., 2432:], 0).reshape(1, 128, 128)
    grad_in_d = jnp.concatenate([first, own[:1], spread[:2]], 0)
    grad_out_d = jnp.concatenate([own[1:], b_o_grad, spread[2:]], 0)
    return (layer_output[None], grad_in[None], grad_in_d, grad_out_d, fed[:1], fed[1:])


def solution(mesh):
    in_specs = (
        P("fs", "sp", None),
        P("fs", "sp", None),
        P(),
        P("fs", None, None),
        P("fs", None),
        P("fs", None, None),
        P("fs", None),
        P(None, "fs", None),
        P(None, "fs", None),
        P(None, "fs", None),
        P(None, "fs", None),
        P("fs", None),
        P("fs", None),
    )
    out_specs = (
        P("fs", "sp", None),
        P("fs", "sp", None),
        P(None, "fs", None),
        P(None, "fs", None),
        P(None, "fs", None),
        P(None, "fs", None),
    )
    return jax.shard_map(body, mesh=mesh, in_specs=in_specs, out_specs=out_specs, check_vma=False)
```

```python
import functools

import jax
import jax.numpy as jnp
from jax import lax
from jax.experimental import pallas as pl
from jax.experimental.pallas import tpu as pltpu
from jax.sharding import PartitionSpec as P

HEAD_SIZE = 64
ADAPTER_RANK = 16
NORM_EPS = 1e-05
ROPE_BASE = 130000.0
MASK_FILL = -1e30
BF = jnp.bfloat16
F32 = jnp.float32
WIDTH = 2048
ROWS = 128
ORDER = (2, 1, 3, 0)
SPEED = 1e3


def mm(left, right):
    return jnp.dot(left, right, preferred_element_type=F32)


def mm_nt(left, right):
    return lax.dot_general(left, right, (((1,), (1,)), ((), ())), preferred_element_type=F32)


def mm_tn(left, right):
    return lax.dot_general(left, right, (((0,), (0,)), ((), ())), preferred_element_type=F32)


def shift(x, chips):
    return lax.ppermute(x, "sp", [(i, ((i // 2 + chips) % 4) * 2 + i % 2) for i in range(8)])


def swap(x):
    return lax.ppermute(x, "sp", [(i, i ^ 1) for i in range(8)])


def shift_z(x, chips):
    return lax.ppermute(x, "fs", [(i, (i + 4 * chips) % 16) for i in range(16)])


def shift_x(x, chips):
    return lax.ppermute(x, "fs", [(i, i - i % 4 + (i + chips) % 4) for i in range(16)])


Y_LINES = [[0, 2, 4, 6], [1, 3, 5, 7]]


def gather_y(x):
    return lax.all_gather(x, "sp", axis=0, tiled=False, axis_index_groups=Y_LINES)


def exchange_y(x):
    return lax.all_to_all(x, "sp", split_axis=0, concat_axis=0, axis_index_groups=Y_LINES)


def line(x, move):
    return [x, move(x, -1), move(x, 2), move(x, 1)]


VMEM = pl.BlockSpec(memory_space=pltpu.VMEM)
SMEM = pl.BlockSpec(memory_space=pltpu.SMEM)


def after(x, *deps):
    anywhere = pl.BlockSpec(memory_space=pl.ANY)
    return pl.pallas_call(
        lambda *refs: None,
        out_shape=jax.ShapeDtypeStruct(x.shape, x.dtype),
        in_specs=[anywhere] * (1 + len(deps)),
        out_specs=anywhere,
        input_output_aliases={0: 0},
        cost_estimate=pl.CostEstimate(flops=0, bytes_accessed=0, transcendentals=0),
    )(x, *deps)


class Info:
    def __init__(self, spans, choice):
        s_at, f_at = lax.axis_index("sp"), lax.axis_index("fs")
        self.values = [s_at >> 1, s_at & 1]
        if spans is None:
            self.values += [None] * 5
        else:
            self.values += [spans[0, 0], spans[0, 0] + spans[0, 1]] + [choice[0, i] for i in range(3)]
        self.values += [f_at >> 2, f_at & 3]

    def __getitem__(self, index):
        return self.values[index]


def call(kernel, outs, scratch, args, limit, deps=(), anywhere=(), to=pltpu.VMEM, us=2.0, token=False):
    outs = [jax.ShapeDtypeStruct(shape, dtype) for shape, dtype in outs]
    rows, args = args[0], args[1:]
    first = len(rows)
    count = first + len(args) + len(anywhere)
    skip = count + len(deps)
    spread = [pl.BlockSpec(memory_space=pl.ANY)] * len(anywhere)
    mark = count + len(deps) + len(outs)
    spread += [pl.BlockSpec(memory_space=pl.ANY)] * len(deps)

    def run(*refs):
        info = Info(*refs[:2]) if rows else Info(None, None)
        if token:
            refs[mark][...] = jnp.zeros((8, 128), F32)
            refs = refs[:mark] + refs[mark + 1 :]
        kernel(info, *refs[first:count], *refs[skip:])

    return pl.pallas_call(
        run,
        out_shape=outs + [jax.ShapeDtypeStruct((8, 128), F32)] * token,
        in_specs=[SMEM] * first + [VMEM] * len(args) + spread,
        out_specs=[pl.BlockSpec(memory_space=to)] * len(outs) + [VMEM] * token,
        scratch_shapes=[pltpu.VMEM(*item) if isinstance(item, tuple) else item for item in scratch],
        compiler_params=pltpu.CompilerParams(vmem_limit_bytes=limit << 20),
        cost_estimate=pl.CostEstimate(flops=int(us * SPEED), bytes_accessed=1 << 10, transcendentals=0),
    )(*rows, *args, *anywhere, *deps)


def lane_mask(info, first, rows):
    token = first + lax.broadcasted_iota(jnp.int32, (rows, 128), 0)
    lane = lax.broadcasted_iota(jnp.int32, (rows, 128), 1) // ADAPTER_RANK
    chosen = jnp.where(token < info[2], info[4], jnp.where(token < info[3], info[5], info[6]))
    return lane == chosen


def chip_mask(info, step):
    chip, core = (info[0] + step) % 4, info[1]
    return jnp.concatenate(
        [
            lane_mask(info, (2 * chip + core) * ROWS, ROWS),
            lane_mask(info, (2 * chip + 1 - core) * ROWS, ROWS),
        ],
        0,
    )


def turn(a, b, cosine, sine):
    return a * cosine - b * sine, b * cosine + a * sine


def aligned(index, unit):
    return pl.ds(pl.multiple_of(index, unit), unit)


def own_first(info, block):
    return (block // 2) * 256 + ((info[1] + block) % 2) * ROWS


def pack_kernel(info, w_hbm, a_in_hbm, a_out_hbm, w_o_hbm, w_pack, ab_pack, w, a_in, a_out, w_o, sems):
    y_at, core = info[0], info[1]
    half = aligned(64 * core, 64)
    copies = [
        pltpu.make_async_copy(w_hbm.at[:, :, aligned(512 * y_at, 512)], w, sems.at[0]),
        pltpu.make_async_copy(a_in_hbm.at[0:4], a_in, sems.at[1]),
        pltpu.make_async_copy(a_out_hbm.at[0:4], a_out, sems.at[2]),
        pltpu.make_async_copy(w_o_hbm.at[aligned(64 * core + 16 * y_at, 16)], w_o, sems.at[3]),
    ]
    for copy in copies:
        copy.start()
    i = lax.broadcasted_iota(jnp.int32, (512, 256), 0)
    j = lax.broadcasted_iota(jnp.int32, (512, 256), 1)
    pick_qk = i == ((j % 128) // 32) * 128 + core * 64 + (j // 128) * 32 + j % 32
    pick_v = i == (j // 64) * 128 + core * 64 + j % 64
    for copy in copies:
        copy.wait()
    for part, pick in enumerate((pick_qk, pick_qk, pick_v)):
        w_pack[:, 256 * part : 256 * part + 256] = mm(w[part], pick.astype(BF)).astype(BF)
    for part in range(3):
        ab_pack[:, 128 * part : 128 * part + 128] = a_in[part]
    ab_pack[:64, 384:512] = a_out[0, half, :]
    ab_pack[64:, 384:512] = a_out[1, half, :]
    ab_pack[:64, 512:640] = a_out[2, half, :]
    ab_pack[64:, 512:640] = a_in[3, half, :]
    ab_pack[:, 640:] = a_out[3]
    for part in range(8):
        lanes = slice(256 * part, 256 * part + 256)
        w_pack[16 * part : 16 * part + 16, 768:] = w_o[:, lanes]


def pack(w, a_in, a_out, w_o):
    scratch = [
        ((3, ROWS, 512), BF),
        ((4, ROWS, 128), BF),
        ((4, ROWS, 128), BF),
        ((16, WIDTH), BF),
        pltpu.SemaphoreType.DMA((4,)),
    ]
    outs = [((ROWS, 1024), BF), ((ROWS, 768), BF)]
    return call(pack_kernel, outs, scratch, ((),), 60, (), (w, a_in, a_out, w_o), us=1.5)


def pack_feed_kernel(info, w_gu, w_d, a_in, a_out, in_ff, out_ff, out):
    y_at, core = info[0], info[1]
    i = lax.broadcasted_iota(jnp.int32, (128, 128), 0)
    j = lax.broadcasted_iota(jnp.int32, (128, 128), 1)
    first = ((j < 64) & (i == j + 64 * core)).astype(BF)
    second = ((j >= 64) & (i == j - 64 + 64 * core)).astype(BF)
    for part in range(2):
        for block in range(8):
            left = w_gu[:, part, aligned(1024 * block + 128 * y_at, 128)]
            right = w_gu[:, part, aligned(1024 * block + 512 + 128 * y_at, 128)]
            lanes = slice(1024 * part + 128 * block, 1024 * part + 128 * block + 128)
            out[:ROWS, lanes] = (mm(left, first) + mm(right, second)).astype(BF)
    out[:ROWS, 2048:2176] = a_in[4]
    out[:ROWS, 2176:2304] = a_in[5]
    out[:ROWS, 2304:] = a_out[4]
    eighth = aligned(64 * (2 * y_at + core), 64)
    out[ROWS:, :WIDTH] = w_d[eighth, :]
    out[ROWS:, 2048:2176] = in_ff[0, eighth, :]
    out[ROWS:, 2176:2304] = out_ff[0, eighth, :]
    out[ROWS:, 2304:] = out_ff[1, eighth, :]


def pack_feed(deps, *args):
    return call(pack_feed_kernel, [((192, 2432), BF)], [], ((), *args), 12, deps, us=3)[0]


def stack_rows(deps, *lists):
    counts = [len(parts) for parts in lists]

    def kernel(info, *refs):
        sems, outs, refs = refs[-1], refs[sum(counts) : -1], refs[: sum(counts)]
        copies = []
        for count, out in zip(counts, outs):
            for i in range(count):
                copies.append(pltpu.make_async_copy(refs[len(copies)], out.at[i], sems.at[len(copies)]))
        for copy in copies:
            copy.start()
        for copy in copies:
            copy.wait()

    outs = [((len(parts),) + parts[0].shape, parts[0].dtype) for parts in lists]
    sems = pltpu.SemaphoreType.DMA((sum(counts),))
    return call(kernel, outs, [sems], ((),), 4, deps, sum(lists, []), pl.ANY, us=1)


def stack_output(others, parts):
    def kernel(info, *refs):
        for i, part in enumerate(refs[:4]):
            refs[-1][i] = part[:, :, 768:]

    shape = ((4, 4, ROWS, 256), BF)
    return call(kernel, [shape], [], ((), *parts), 8, (), others, us=1, token=True)


def arrived(*parts):
    return [part[:8, :128] for part in parts]


def norm_kernel(info, x, gain, out):
    values = x[...].astype(F32)
    inverse = lax.rsqrt(jnp.mean(values * values, -1, keepdims=True) + NORM_EPS)
    out[...] = (values * inverse * gain[0:1, :]).astype(BF)


def norm_first(deps, info, x, gain):
    return call(norm_kernel, [((ROWS, WIDTH), BF)], [], (info, x, gain), 4, deps, us=0.6)[0]


def copy_kernel(info, x, out):
    out[...] = x[...]


def copy_after(deps, info, x):
    return call(copy_kernel, [(x.shape, x.dtype)], [], (info, x), 4, deps)[0]


def qkv_kernel(info, cosine, sine, a0, a1, a2, a3, b0, b1, b2, b3, near, far, *refs):
    q, k, v, low_out, n1, w, a, b_q, b_k, b_v, a_o, b_o, rest, sems = refs
    z_at, x_at, y_at, core = info[7], info[8], info[0], info[1]
    copies, weights = [], []
    for dz in range(4):
        for dx in range(4):
            f = ((z_at + dz) % 4) * 4 + (x_at + dx) % 4
            rows = aligned(f * ROWS, ROWS)
            one, two = (a0, a1, a2, a3)[dz].at[dx], (b0, b1, b2, b3)[dx].at[dz]
            weights.append(pltpu.make_async_copy(two.at[:, :384], a.at[rows], sems.at[1]))
            weights.append(pltpu.make_async_copy(two.at[:, 384:640], rest.at[rows], sems.at[2]))
            weights.append(pltpu.make_async_copy(one.at[:, :768], w.at[rows], sems.at[3]))
            copies.append(pltpu.make_async_copy(two.at[:, 640:], b_o.at[rows], sems.at[4]))
    tokens = []
    for chip in range(4):
        own, other = chip * 256 + ROWS * core, chip * 256 + ROWS * (1 - core)
        tokens.append(pltpu.make_async_copy(near.at[chip], n1.at[aligned(own, ROWS)], sems.at[0]))
        tokens.append(pltpu.make_async_copy(far.at[chip], n1.at[aligned(other, ROWS)], sems.at[0]))
    for copy in tokens + weights + copies:
        copy.start()
    for copy in tokens + weights:
        copy.wait()
    for head in range(4):
        first = (4 * y_at + head) * ROWS
        for half in range(2):
            to = slice(half * 128 + head * 32, half * 128 + head * 32 + 32)
            b_q[to, :] = rest[aligned(first + 32 * half, 32), :128]
            b_k[to, :] = rest[aligned(first + 64 + 32 * half, 32), :128]
        b_v[64 * head : 64 * head + 64, :] = rest[aligned(first, 64), 128:]
    for f in range(16):
        a_o[64 * f : 64 * f + 64, :] = rest[f * ROWS + 64 : f * ROWS + 128, 128:]
    for chip in range(4):
        at = slice(256 * chip, 256 * chip + 256)
        rows = n1[at, :]
        mask = lane_mask(info, 256 * chip, 256)
        low = jnp.where(jnp.concatenate([mask] * 3, 1), mm(rows, a[...]), 0.0).astype(BF)
        low_out[at, :] = low
        cos, sin = cosine[at, :], sine[at, :]
        for j, (b, out) in enumerate(((b_q, q), (b_k, k))):
            base = mm(rows, w[:, 256 * j : 256 * j + 256])
            values = base + mm_nt(low[:, 128 * j : 128 * j + 128], b[...])
            first, second = turn(values[:, :128], values[:, 128:], cos, sin)
            out[at, :128] = first.astype(BF)
            out[at, 128:] = second.astype(BF)
        v[at, :] = (mm(rows, w[:, 512:]) + mm_nt(low[:, 256:], b_v[...])).astype(BF)
    for copy in copies:
        copy.wait()


def project_qkv(deps, info, w_parts, ab_parts, near, far, cosine, sine):
    return call(
        qkv_kernel,
        [
            ((1024, 256), BF),
            ((1024, 256), BF),
            ((1024, 256), BF),
            ((1024, 384), BF),
            ((1024, WIDTH), BF),
            ((WIDTH, 768), BF),
            ((WIDTH, 384), BF),
            ((256, 128), BF),
            ((256, 128), BF),
            ((256, 128), BF),
            ((1024, 128), BF),
            ((WIDTH, 128), BF),
        ],
        [((WIDTH, 256), BF), pltpu.SemaphoreType.DMA((5,))],
        (info, cosine, sine),
        48,
        deps,
        (*w_parts, *ab_parts, near, far), us=9)


def head_lanes(head, rows, paired):
    lane = lax.broadcasted_iota(jnp.int32, (rows, 256), 1)
    return ((lane % 128) // 32 if paired else lane // 64) == head


def key_bias(info, block):
    n = 256 * (block + 1)
    j = lax.broadcasted_iota(jnp.int32, (n, 256), 0)
    i = 256 * block + lax.broadcasted_iota(jnp.int32, (n, 256), 1)
    allowed = (j <= i) & ((j < info[2]) | (j >= info[3]) | (i < info[3]))
    return jnp.where(allowed, 0.0, MASK_FILL)


def attend_kernel(info, q, k, v, mix, log_total, v_heads, probs):
    for head in range(4):
        v_heads[head] = jnp.where(head_lanes(head, 1024, False), v[...], 0)
    for block in range(4):
        n = 256 * (block + 1)
        rows = slice(256 * block, 256 * block + 256)
        bias = key_bias(info, block)
        out = jnp.zeros((256, 256), F32)
        for head in range(4):
            q_head = jnp.where(head_lanes(head, 256, True), q[rows, :], 0) * jnp.array(0.125, BF)
            scores = mm_nt(k[:n, :], q_head) + bias
            top = jnp.max(scores, 0, keepdims=True)
            weights = jnp.exp(scores - top)
            total = jnp.sum(weights, 0, keepdims=True)
            log_total[head : head + 1, rows] = top + jnp.log(total)
            probs[head, :n, :] = (weights * (1.0 / total)).astype(BF)
        for head in range(4):
            out = out + mm_tn(probs[head, :n, :], v_heads[head, :n, :])
        out = out.astype(BF)
        for part in range(2):
            row = own_first(info, 2 * block + part)
            mix[aligned(row, ROWS), :] = out[part * ROWS : part * ROWS + ROWS]


def attend(info, q, k, v):
    return call(
        attend_kernel,
        [((1024, 256), BF), ((8, 1024), F32)],
        [((4, 1024, 256), BF), ((4, 1024, 256), BF)],
        (info, q, k, v),
        16, us=6)


def attend_back_kernel(
    info, q, k, v, g0, g1, g2, g3, log_total, cosine, sine, out, q_heads, g_heads, k_heads, probs, grads, dk, dv
):
    core = info[1]
    for d, part in enumerate((g0, g1, g2, g3)):
        block = (info[0] - d + 4) % 4
        for other in range(2):
            rows = part[other * ROWS : other * ROWS + ROWS, :256]
            second = (core + other) % 2
            for head in range(4):
                g_heads[block, aligned(256 * head + ROWS * second, ROWS), :] = jnp.where(
                    head_lanes(head, ROWS, False), rows, 0
                )
    for head in range(4):
        k_heads[head] = jnp.where(head_lanes(head, 1024, True), k[...], 0) * jnp.array(0.125, BF)
    dk[...] = jnp.zeros_like(dk)
    dv[...] = jnp.zeros_like(dv)

    def unrotate(values, rows):
        a, b = values[:, :128].astype(F32), values[:, 128:].astype(F32)
        first, last = turn(a, b, cosine[rows, :], -sine[rows, :])
        return jnp.concatenate([first, last], 1).astype(BF)

    for block in range(4):
        n = 256 * (block + 1)
        rows = slice(256 * block, 256 * block + 256)
        bias = key_bias(info, block)
        for head in range(4):
            at = slice(256 * head, 256 * head + 256)
            q_head = jnp.where(head_lanes(head, 256, True), q[rows, :], 0) * jnp.array(0.125, BF)
            q_heads[at, :] = q_head
            scores = mm_nt(k[:n, :], q_head) + bias
            p = jnp.exp(scores - log_total[head : head + 1, rows])
            dp = mm_nt(v[:n, :], g_heads[block, at, :])
            inner = jnp.sum(p * dp, 0, keepdims=True)
            probs[:n, at] = p.astype(BF)
            grads[:n, at] = (p * (dp - inner)).astype(BF)
        dv[:n, :] += mm(probs[:n, :], g_heads[block])
        dk[:n, :] += mm(grads[:n, :], q_heads[...])
        dq = jnp.zeros((256, 256), F32)
        for head in range(4):
            dq = dq + mm_tn(grads[:n, 256 * head : 256 * head + 256], k_heads[head, :n, :])
        out[rows, 0:256] = unrotate(dq.astype(BF), rows)
    for block in range(4):
        rows = slice(256 * block, 256 * block + 256)
        out[rows, 256:512] = unrotate(dk[rows, :].astype(BF), rows)
        out[rows, 512:768] = dv[rows, :].astype(BF)


def attend_back(deps, info, q, k, v, parts, log_total, cosine, sine):
    return call(
        attend_back_kernel,
        [((1024, 768), BF)],
        [
            ((1024, 256), BF),
            ((4, 1024, 256), BF),
            ((4, 1024, 256), BF),
            ((1024, 1024), BF),
            ((1024, 1024), BF),
            ((1024, 256), F32),
            ((1024, 256), F32),
        ],
        (info, q, k, v, *parts, log_total, cosine, sine),
        15,
        deps, us=9, token=True)


def output_kernel(info, parts, w0, w1, w2, w3, a_o, keep, send, w, mix):
    z_at, x_at = info[7], info[8]
    for dy, piece in enumerate((w0, w1, w2, w3)):
        chip = (info[0] + dy) % 4
        mix[:, 256 * dy : 256 * dy + 256] = parts[dy]
        for dz in range(4):
            for dx in range(4):
                f = ((z_at + dz) % 4) * 4 + (x_at + dx) % 4
                rows = aligned(f * 64 + 16 * chip, 16)
                for part in range(8):
                    w[rows, 256 * part : 256 * part + 256] = piece[dz, dx, 16 * part : 16 * part + 16]
    keep[:, :WIDTH] = mm(mix[:ROWS, :], w[...])
    keep[:, WIDTH:] = mm(mix[:ROWS, :], a_o[...])
    send[:, :WIDTH] = mm(mix[ROWS:, :], w[...]).astype(BF)
    send[:, WIDTH:] = mm(mix[ROWS:, :], a_o[...]).astype(BF)


def project_output(info, mixes, pieces, a_o):
    return call(
        output_kernel,
        [((ROWS, 2176), F32), ((ROWS, 2176), BF), ((1024, WIDTH), BF)],
        [((256, 1024), BF)],
        (info, mixes, *pieces, a_o),
        8, us=4)


def middle_kernel(info, keep, got, x, b_o, gain, resid, n2, low):
    summed = keep[...] + got[...].astype(F32)
    mask = lane_mask(info, (2 * info[0] + info[1]) * ROWS, ROWS)
    low_o = jnp.where(mask, summed[:, WIDTH:], 0.0).astype(BF)
    low[...] = low_o
    values = x[...].astype(F32) + summed[:, :WIDTH] + mm_nt(low_o, b_o[...])
    resid[...] = values
    inverse = lax.rsqrt(jnp.mean(values * values, -1, keepdims=True) + NORM_EPS)
    n2[...] = (values * inverse * gain[1:2, :]).astype(BF)


def middle(deps, info, keep, got, x, b_o, gain):
    return call(
        middle_kernel,
        [((ROWS, WIDTH), F32), ((ROWS, WIDTH), BF), ((ROWS, 128), BF)],
        [],
        (info, keep, got, x, b_o, gain),
        10,
        deps, us=1)


def load_weights(gathered, w_g, w_u, w_d, a_gu, b_d, ff, sems):
    small = [
        pltpu.make_async_copy(gathered.at[:, :ROWS, 2048:2304], a_gu, sems.at[0]),
        pltpu.make_async_copy(gathered.at[:, :ROWS, 2304:], b_d, sems.at[1]),
        pltpu.make_async_copy(gathered.at[:, ROWS:, 2048:], ff, sems.at[2]),
    ]
    blocks = []
    for i in range(4):
        at, up = pl.ds(256 * i, 256), pl.ds(1024 + 256 * i, 256)
        rows = pl.ds(4 * i, 4)
        blocks.append(
            [
                pltpu.make_async_copy(gathered.at[:, :ROWS, at], w_g.at[:, :, at], sems.at[3 + 3 * i]),
                pltpu.make_async_copy(gathered.at[:, :ROWS, up], w_u.at[:, :, at], sems.at[4 + 3 * i]),
                pltpu.make_async_copy(gathered.at[rows, ROWS:, :WIDTH], w_d.at[rows], sems.at[5 + 3 * i]),
            ]
        )
    for group in [small] + blocks:
        for copy in group:
            copy.start()
    return [small] + blocks


def feed_kernel(step, first, info, *refs):
    if first:
        n_near, n_far, g_near, g_far, gathered, *outs = refs[:13]
        w_g, w_u, w_d, a_gu, b_d, ff, n_rows, g_rows, row_sems, sems = refs[13:]
    else:
        w_g, w_u, w_d, a_gu, b_d, ff, n_near, n_far, g_near, g_far, *outs = refs[:18]
        n_rows, g_rows, row_sems = refs[18:]
    keep_down, send_down, keep_back, send_back, hidden, grad_gate, grad_up, lows = outs
    chip = (info[0] + step) % 4
    row_copies = [
        pltpu.make_async_copy(part, rows.at[at : at + ROWS], row_sems.at[i])
        for i, (part, rows, at) in enumerate(
            (
                (n_near, n_rows, 0),
                (n_far, n_rows, ROWS),
                (g_near.at[chip], g_rows, 0),
                (g_far.at[chip], g_rows, ROWS),
            )
        )
    ]
    for copy in row_copies:
        copy.start()
    groups = load_weights(gathered, w_g, w_u, w_d, a_gu, b_d, ff, sems) if first else [[]] * 5
    for copy in row_copies[:2]:
        copy.wait()
    mask = chip_mask(info, step)
    twice = jnp.concatenate([mask, mask], 1)
    for copy in groups[0]:
        copy.wait()
    low = jnp.where(twice, mm(n_rows[...], a_gu[...].reshape(WIDTH, 256)), 0.0).astype(BF)
    for copy in row_copies[2:]:
        copy.wait()
    glow = jnp.where(mask, mm(g_rows[...], b_d[...].reshape(WIDTH, 128)), 0.0).astype(BF)
    lows[:, :256] = low
    lows[:, 256:384] = glow
    for block in range(4):
        at = slice(256 * block, 256 * block + 256)
        rows = slice(4 * block, 4 * block + 4)
        for copy in groups[1 + block]:
            copy.wait()
        thin = ff[rows].reshape(256, 384)
        gate = mm(n_rows[...], w_g[:, :, at].reshape(WIDTH, 256)) + mm_nt(low[:, :128], thin[:, 128:256])
        up = mm(n_rows[...], w_u[:, :, at].reshape(WIDTH, 256)) + mm_nt(low[:, 128:], thin[:, 256:])
        grad_hidden = mm_nt(g_rows[...], w_d[rows].reshape(256, WIDTH)) + mm_nt(glow, thin[:, :128])
        sig = 1.0 / (1.0 + jnp.exp(-gate))
        act = gate * sig
        hidden[:, at] = (act * up).astype(BF)
        grad_gate[:, at] = (grad_hidden * up * sig * (1.0 + gate * (1.0 - sig))).astype(BF)
        grad_up[:, at] = (grad_hidden * act).astype(BF)

    def put(keep, send, at, values):
        keep[:, at] = values[:ROWS].astype(BF)
        send[:, at] = values[ROWS:].astype(BF)

    for block in range(8):
        at = slice(256 * block, 256 * block + 256)
        pair = slice(2 * block, 2 * block + 2)
        left = mm_nt(grad_gate[...], w_g[pair].reshape(256, 1024))
        right = mm_nt(grad_up[...], w_u[pair].reshape(256, 1024))
        put(keep_back, send_back, at, left + right)
        put(keep_down, send_down, at, mm(hidden[...], w_d[:, :, at].reshape(1024, 256)))
    thin = ff[...].reshape(1024, 384)
    glow_g = mm(grad_gate[...], thin[:, 128:256])
    glow_u = mm(grad_up[...], thin[:, 256:])
    low_d = mm(hidden[...], thin[:, :128])
    put(keep_back, send_back, slice(WIDTH, WIDTH + 128), glow_g)
    put(keep_back, send_back, slice(WIDTH + 128, WIDTH + 256), glow_u)
    put(keep_down, send_down, slice(WIDTH, WIDTH + 128), low_d)
    lows[:, 384:512] = jnp.where(mask, glow_g, 0.0).astype(BF)
    lows[:, 512:640] = jnp.where(mask, glow_u, 0.0).astype(BF)
    lows[:, 640:] = jnp.where(mask, low_d, 0.0).astype(BF)


def feed(step, deps, info, tokens, weights):
    first = len(weights) == 1
    shapes = [
        ((ROWS, 2176), BF),
        ((ROWS, 2176), BF),
        ((ROWS, 2304), BF),
        ((ROWS, 2304), BF),
        ((256, 1024), BF),
        ((256, 1024), BF),
        ((256, 1024), BF),
        ((256, 768), BF),
    ]
    scratch = [((256, WIDTH), BF), ((256, WIDTH), BF), pltpu.SemaphoreType.DMA((4,))]
    kernel = functools.partial(feed_kernel, step, first)
    if not first:
        return call(kernel, shapes, scratch, (info, *weights), 10, deps, tokens, us=9), weights
    held = [(16, ROWS, 1024), (16, ROWS, 1024), (16, 64, WIDTH), (16, ROWS, 256), (16, ROWS, 128), (16, 64, 384)]
    shapes += [(shape, BF) for shape in held]
    scratch.append(pltpu.SemaphoreType.DMA((15,)))
    outs = call(kernel, shapes, scratch, (info,), 26, deps, (*tokens, *weights), us=12)
    return outs[:8], outs[8:]


def early_kernel(info, *refs):
    chunks = [refs[4 * i : 4 * i + 4] for i in range(4)]
    parts = refs[16:24]
    g_near, g_far, by_token, by_hidden, n_rows, g_rows, sems = refs[24:]
    copies = []
    for i, d in enumerate(ORDER):
        chip = (info[0] + d) % 4
        for far in range(2):
            to = pl.ds((2 * i + far) * ROWS, ROWS)
            copies.append(pltpu.make_async_copy(parts[4 * far + d], n_rows.at[to], sems.at[2 * i + far]))
            source = (g_near, g_far)[far].at[chip]
            copies.append(pltpu.make_async_copy(source, g_rows.at[to], sems.at[8 + 2 * i + far]))
    for copy in copies:
        copy.start()
    flip = lambda values: values.astype(F32).T.astype(BF)
    thins = [flip(chunk[3][...]) for chunk in chunks]
    for j, (row, name) in enumerate(((2, 0), (0, 1), (1, 2))):
        rows = slice(128 * row, 128 * row + 128)
        total = sum(mm(thins[i][rows], chunks[i][name][...]) for i in range(4))
        by_hidden[:, 128 * j : 128 * j + 128] = total.T.astype(BF)
    for copy in copies:
        copy.wait()
    for j, (row, tokens) in enumerate(((3, n_rows), (4, n_rows), (5, g_rows))):
        rows = slice(128 * row, 128 * row + 128)
        total = sum(mm(thins[i][rows], tokens[256 * i : 256 * i + 256, :]) for i in range(4))
        by_token[:, 128 * j : 128 * j + 128] = total.T.astype(BF)


def early_sums(tokens, chunks, deps):
    args = [()] + [part for chunk in chunks for part in chunk]
    scratch = [((1024, WIDTH), BF), ((1024, WIDTH), BF), pltpu.SemaphoreType.DMA((16,))]
    outs = [((WIDTH, 384), BF), ((1024, 384), BF)]
    return call(early_kernel, outs, scratch, args, 16, deps, tokens, us=4.5)


def between_kernel(info, own, r1, r2, r3, a_gu, resid, og, low, gain, grad_resid, grad_attn):
    total = own[...] + r1[...].astype(F32) + r2[...].astype(F32) + r3[...].astype(F32)
    mask = lane_mask(info, (2 * info[0] + info[1]) * ROWS, ROWS)
    glow = jnp.where(jnp.concatenate([mask, mask], 1), total[:, WIDTH:], 0.0).astype(BF)
    grad = total[:, :WIDTH] + mm_nt(glow, a_gu[...].reshape(WIDTH, 256))
    values = resid[...]
    inverse = lax.rsqrt(jnp.mean(values * values, -1, keepdims=True) + NORM_EPS)
    result = og[...].astype(F32) + norm_back(grad, values, inverse, gain[1:2, :])
    grad_resid[...] = result
    grad_attn[:, :WIDTH] = result.astype(BF)
    grad_attn[:, WIDTH:] = low[...]


def between(deps, info, own, r1, r2, r3, a_gu, resid, og, low, gain):
    return call(
        between_kernel,
        [((ROWS, WIDTH), F32), ((ROWS, 2176), BF)],
        [],
        (info, own, r1, r2, r3, a_gu, resid, og, low, gain),
        10,
        deps, us=1.4)


def combine_kernel(info, by_token, by_hidden, out):
    for f in range(16):
        out[f, :ROWS, :] = by_token[f * ROWS : f * ROWS + ROWS, :]
        out[f, ROWS:, :] = by_hidden[64 * f : 64 * f + 64, :]


def combine(by_token, by_hidden):
    return call(
        combine_kernel, [((16, 192, 384), BF)], [], ((), by_token, by_hidden), 8, us=1.6, token=True
    )


def down_kernel(info, k0, k1, k2, k3, got, own, *outs):
    for i, (d, keep) in enumerate(zip(ORDER, (k0, k1, k2, k3))):
        total = keep[...].astype(F32) + got[i].astype(F32)
        if d:
            outs[d - 1][...] = total.astype(BF)
        else:
            own[...] = total


def down_pair(deps, kept, got):
    return call(
        down_kernel,
        [((ROWS, 2176), F32)] + [((ROWS, 2176), BF)] * 3,
        [],
        ((), *kept, got),
        8,
        deps, us=1.5, token=True)


def result_kernel(info, own, r1, r2, r3, resid, b_d, out):
    total = own[...] + r1[...].astype(F32) + r2[...].astype(F32) + r3[...].astype(F32)
    mask = lane_mask(info, (2 * info[0] + info[1]) * ROWS, ROWS)
    low = jnp.where(mask, total[:, WIDTH:], 0.0).astype(BF)
    out[...] = (resid[...] + total[:, :WIDTH] + mm_nt(low, b_d[...].reshape(WIDTH, 128))).astype(BF)


def result(info, own, r1, r2, r3, resid, b_d):
    return call(
        result_kernel, [((ROWS, WIDTH), BF)], [], (info, own, r1, r2, r3, resid, b_d), 10, us=1.8, token=True)


def output_back_kernel(info, own, other, b_o, w_o, a_o, p0, p1, p2, p3, half, grad, mix):
    grad[:ROWS] = own[:, :WIDTH]
    grad[ROWS:] = other[:, :WIDTH]
    glow = jnp.where(chip_mask(info, 0), mm(grad[...], b_o[...]), 0.0).astype(BF)
    for chip in range(4):
        at = slice(256 * chip, 256 * chip + 256)
        mix[:, at] = (mm_nt(grad[...], w_o[at, :]) + mm_nt(glow, a_o[at, :])).astype(BF)
    for d, part in enumerate((p0, p1, p2, p3)):
        part[:, :256] = mix[:, aligned(256 * ((info[0] + d) % 4), 256)]
        part[:, 256:] = glow
    flip = lambda values: values.astype(F32).T.astype(BF)
    total = (mm(flip(own[:, WIDTH:]), grad[:ROWS]) + mm(flip(other[:, WIDTH:]), grad[ROWS:])).T.astype(BF)
    for f in range(16):
        rows = total[f * ROWS : f * ROWS + ROWS]
        half[64 * f : 64 * f + 64, :] = jnp.where(info[1] == 0, rows[:64], rows[64:])


def output_back(info, own, other, b_o, w_o, a_o):
    return call(
        output_back_kernel,
        [((256, 384), BF)] * 4 + [((1024, 128), BF)],
        [((256, WIDTH), BF), ((256, 1024), BF)],
        (info, own, other, b_o, w_o, a_o),
        8, us=2.7)


def pick_rows(info, g, core, out):
    for d in range(4):
        chip = (info[0] + d) % 4
        out[d * ROWS : d * ROWS + ROWS, :] = g[aligned(256 * chip + ROWS * core, ROWS), :]


def input_send_kernel(info, g, w, send, rows):
    pick_rows(info, g, 1 - info[1], rows)
    for block in range(8):
        at = slice(256 * block, 256 * block + 256)
        send[:, at] = mm_nt(rows[...], w[at, :]).astype(BF)


def input_send(deps, info, g, w):
    return call(input_send_kernel, [((512, WIDTH), BF)], [((512, 768), BF)], (info, g, w), 8, deps=deps, us=3.7, token=True)


def input_pair_kernel(info, g, w, got, own, p1, p2, p3, rows):
    pick_rows(info, g, info[1], rows)
    for block in range(8):
        at = slice(256 * block, 256 * block + 256)
        total = mm_nt(rows[...], w[at, :]) + got[:, at].astype(F32)
        own[:, at] = total[:ROWS]
        for d, out in enumerate((p1, p2, p3)):
            out[:, at] = total[ROWS * (d + 1) : ROWS * (d + 2)].astype(BF)


def input_pair(deps, info, g, w, got):
    return call(
        input_pair_kernel,
        [((ROWS, WIDTH), F32)] + [((ROWS, WIDTH), BF)] * 3,
        [((512, 768), BF)],
        (info, g, w, got),
        8,
        deps, us=3.5, token=True)


def squeeze(rows):
    i = lax.broadcasted_iota(jnp.int32, rows, 0) % ADAPTER_RANK
    j = lax.broadcasted_iota(jnp.int32, rows, 1) % ADAPTER_RANK
    return (i == j).astype(BF)


def narrow_kernel(info, g, b_q, b_k, b_v, low, mix, o0, o1, o2, o3, narrow, own):
    mask = lane_mask(info, 0, 1024)
    fold = squeeze((16, 128))
    flip = lambda values: values.astype(F32).T.astype(BF)
    for j, b in enumerate((b_q, b_k, b_v)):
        term = jnp.where(mask, mm(g[:, 256 * j : 256 * j + 256], b[...]), 0.0).astype(BF)
        narrow[16 * j : 16 * j + 16, :] = mm_nt(fold, term).astype(BF)
    low_t = flip(low[...])
    for j in range(3):
        total = mm(low_t[128 * j : 128 * j + 128], g[:, 256 * j : 256 * j + 256]).T.astype(BF)
        lanes = slice(128 * (j + 1), 128 * (j + 2))
        for head in range(4):
            if j == 2:
                own[head, :, lanes] = total[64 * head : 64 * head + 64]
            else:
                own[head, :32, lanes] = total[32 * head : 32 * head + 32]
                own[head, 32:, lanes] = total[128 + 32 * head : 160 + 32 * head]
    total = sum(
        mm(flip(part[:, 256:]), mix[aligned(256 * ((info[0] - d + 4) % 4), 256), :])
        for d, part in enumerate((o0, o1, o2, o3))
    ).T.astype(BF)
    for head in range(4):
        own[head, :, :128] = total[64 * head : 64 * head + 64]


def narrow_sums(deps, info, g, b_q, b_k, b_v, low, mix, parts):
    return call(
        narrow_kernel,
        [((48, 1024), BF), ((4, 64, 512), BF)],
        [],
        (info, g, b_q, b_k, b_v, low, mix, *parts),
        10,
        deps, us=2.3)


def late_kernel(info, n0, n1, n2, n3, rows, out, glow_own):
    total = n0[...].astype(F32) + n1[...].astype(F32) + n2[...].astype(F32) + n3[...].astype(F32)
    total = total.astype(BF)
    s_at = 2 * info[0] + info[1]
    mask = lane_mask(info, 0, 1024)
    spread = squeeze((16, 128))
    wide = []
    for j in range(3):
        term = jnp.where(mask, mm_tn(total[16 * j : 16 * j + 16], spread), 0.0)
        wide.append(term)
    mask_own = lane_mask(info, s_at * ROWS, ROWS)
    for j in range(3):
        piece = jnp.zeros((ROWS, 128), F32)
        for block in range(8):
            piece = jnp.where(s_at == block, wide[j][block * ROWS : block * ROWS + ROWS], piece)
        glow_own[:, 128 * j : 128 * j + 128] = jnp.where(mask_own, piece, 0.0).astype(BF)
    thin = jnp.concatenate([term.T.astype(BF) for term in wide], 0)
    for f in range(8):
        at = slice(256 * f, 256 * f + 256)
        total = mm(thin, rows[:, at]).T
        for second in range(2):
            piece = jnp.zeros((16, 384), F32)
            for s in range(8):
                first = second * ROWS + 16 * s
                piece = jnp.where(s_at == s, total[first : first + 16], piece)
            out[2 * f + second] = piece.astype(BF)


def late_sums(deps, info, parts, rows):
    return call(
        late_kernel,
        [((16, 16, 384), BF), ((ROWS, 384), BF)],
        [],
        (info, *parts, rows),
        10,
        deps, us=2.9)


def groups_kernel(info, values, out):
    total = values[0].astype(F32)
    for f in range(1, 16):
        total = total + values[f].astype(F32)
    out[...] = total.astype(BF)


def sum_groups(deps, values):
    return call(groups_kernel, [(values.shape[1:], BF)], [], ((), values), 8, deps, us=1.6)[0]


def early_result_kernel(info, values, one, two, spread):
    for j in range(3):
        lanes = slice(128 * j, 128 * j + 128)
        spread[j] = sum(values[s, :ROWS, lanes].astype(F32) for s in range(8))
        out, at = (one, 0) if j == 0 else (two, j - 1)
        for s in range(8):
            out[at, 64 * s : 64 * s + 64, :] = values[s, ROWS:, lanes].astype(F32)


def early_result(values):
    outs = [((1, 512, 128), F32), ((2, 512, 128), F32), ((3, ROWS, 128), F32)]
    return call(early_result_kernel, outs, [], ((), values), 8, us=2, token=True)


def final_kernel(info, *refs):
    y_at, core, z_at = info[0], info[1], info[7]
    spread, grad_in, grad_out, own = refs[8:]
    last = [0.0, 0.0]
    for d in range(4):
        chip = (y_at + d) % 4
        for other in range(2):
            part, at = refs[4 * other + d], (core + other) % 2
            for j in range(3):
                grad_in[j, aligned((2 * chip + at) * 16, 16), :] = part[:, 128 * j : 128 * j + 128].astype(F32)
            rows = aligned(64 * at, 16)

            @pl.when(chip == z_at)
            def _():
                own[pl.ds(16 * at, 16), :] = part[:, 384:2432].astype(F32)

            last[other] = last[other] + part[:, 2432:].astype(F32)
    for r in range(4):
        for j in range(4):
            lanes = slice(512 * r + 128 * j, 512 * r + 128 * j + 128)
            values = own[:, lanes]
            for i in range(32):
                out, at = (grad_in, 3) if j == 0 else (grad_out, j - 1)
                out[at, 4 * i + r : 4 * i + r + 1, :] = values[i : i + 1]
        lanes = slice(128 * r, 128 * r + 128)
        first = jnp.where(core == 0, last[0][:, lanes], last[1][:, lanes])
        second = jnp.where(core == 0, last[1][:, lanes], last[0][:, lanes])
        for i in range(16):
            grad_out[3, 4 * i + r : 4 * i + r + 1, :] = first[i : i + 1]
            grad_out[3, 64 + 4 * i + r : 64 + 4 * i + r + 1, :] = second[i : i + 1]
    grad_in[4] = spread[0]
    grad_in[5] = spread[1]
    grad_out[4] = spread[2]


def final_result(deps, near, far, spread):
    outs = [((6, ROWS, 128), F32), ((5, ROWS, 128), F32)]
    return call(final_kernel, outs, [((32, 2048), F32)], ((), *near, *far, spread), 8, deps, us=2)


def last_kernel(info, own, r1, r2, r3, glow, a, resid_grad, x, gain, out):
    grad = own[...] + r1[...].astype(F32) + r2[...].astype(F32) + r3[...].astype(F32) + mm_nt(glow[...], a[...])
    values = x[...].astype(F32)
    inverse = lax.rsqrt(jnp.mean(values * values, -1, keepdims=True) + NORM_EPS)
    out[...] = resid_grad[...] + norm_back(grad, values, inverse, gain[0:1, :])


def last(deps, info, own, r1, r2, r3, glow, a, resid_grad, x, gain):
    return call(
        last_kernel,
        [((ROWS, WIDTH), F32)],
        [],
        (info, own, r1, r2, r3, glow, a, resid_grad, x, gain),
        10, deps=deps, us=2.5, token=True)


def rms_inverse(values):
    return lax.rsqrt(jnp.mean(values * values, -1, keepdims=True) + NORM_EPS)


def norm_back(grad_norm, values, inverse, gain):
    normed = values * inverse
    scaled = grad_norm * gain
    return inverse * (scaled - normed * jnp.mean(scaled * normed, -1, keepdims=True))


def body(
    layer_input,
    output_gradient,
    norm_gain_pair,
    query_key_value_weight,
    output_weight,
    gate_up_weight,
    down_weight,
    adapter_input_model,
    adapter_output_model,
    adapter_input_hidden,
    adapter_output_hidden,
    spans,
    adapter_choice_rows,
):
    f_at, s_at = lax.axis_index("fs"), lax.axis_index("sp")
    y_at, c_at = s_at >> 1, s_at & 1
    z_at = f_at >> 2
    x_l = layer_input[0]
    og_l = output_gradient[0]
    rows = x_l.shape[0]
    tokens = 8 * rows
    gains = norm_gain_pair
    info = (spans, adapter_choice_rows)

    w_pack, ab_pack = pack(
        query_key_value_weight.transpose(1, 0, 2), adapter_input_model, adapter_output_model, output_weight
    )
    w_line, ab_line = line(w_pack, shift_x), line(ab_pack, shift_z)
    w_line, ab_line = stack_rows((), w_line, ab_line)
    w_parts, ab_parts = line(w_line, shift_z), line(ab_line, shift_x)
    n1_l = norm_first((w_pack,), info, x_l, gains)
    near = gather_y(n1_l)
    far = swap(near)
    g_near = gather_y(og_l)
    g_far = swap(g_near)
    feed_pack = pack_feed(
        (w_pack,),
        gate_up_weight,
        down_weight,
        adapter_input_model,
        adapter_output_model,
        adapter_input_hidden,
        adapter_output_hidden,
    )
    o_stack, p1_done = stack_output(ab_parts, w_parts)
    feed_all = lax.all_gather(after(feed_pack, p1_done), "fs", axis=0, tiled=False)

    at = jnp.arange(tokens, dtype=jnp.int32)
    position = at - jnp.where(at >= spans[0, 0] + spans[0, 1], spans[0, 1], 0)
    freq = ROPE_BASE ** (-(jnp.arange(32, dtype=F32) * 2.0 / HEAD_SIZE))
    phase = position.astype(F32)[:, None] * jnp.tile(freq, 4)[None, :]
    cosine, sine = jnp.cos(phase), jnp.sin(phase)

    o_parts = line(o_stack, shift)
    q, k, v, low_qkv, n1, w_qkv, a_qkv, b_q, b_k, b_v, a_o, b_o = project_qkv(
        (), info, w_parts, ab_parts, near, far, cosine, sine
    )
    mix, log_total = attend(info, q, k, v)
    mixes = exchange_y(mix.reshape(4, 256, 256))
    keep, send, w_o = project_output(info, mixes, o_parts, a_o)
    resid, n2_l, low_o = middle((), info, keep, swap(send), x_l, b_o, gains)

    n_near = line(n2_l, shift)
    n_far = [swap(part) for part in n_near]
    chunks, kept, sent, back, got = [], [], [], {}, []
    rows_there = arrived(*n_near[1:], *n_far)
    pairs = []
    weights = (feed_all,)
    for d in ORDER:
        deps = [chunks[-1][-1]] if chunks else rows_there
        if len(chunks) == 2:
            deps += arrived(pairs[0])
        if len(chunks) == 3:
            deps += arrived(pairs[2], back[ORDER[0]])
        outs, weights = feed(d, deps, info, (n_near[d], n_far[d], g_near, g_far), weights)
        keep_down, send_down, keep_back, send_back, *chunk = outs
        chunks.append(chunk)
        kept.append(keep_down)
        sent.append(send_down)
        got.append(swap(send_back))
        pair = keep_back.astype(F32) + got[-1].astype(F32)
        if d:
            pair = pair.astype(BF)
        pairs.append(pair)
        back[d] = shift(pair, d if d < 3 else -1) if d else pair
    a_gu, b_d = weights[3], weights[4]
    by_token, by_hidden = early_sums((*n_near, *n_far, g_near, g_far), chunks, arrived(back[ORDER[1]], back[ORDER[2]]))
    early, early_done = combine(by_token, by_hidden)
    early = lax.psum_scatter(early.reshape(16 * 192, 384), "fs", scatter_dimension=0, tiled=True)
    grad_resid, grad_attn = between((early_done,), info, back[0], back[1], back[2], back[3], a_gu, resid, og_l, low_o, gains)

    *parts, half_o = output_back(info, grad_attn, swap(grad_attn), b_o, w_o, a_o)
    parts = [parts[0]] + [shift(parts[d], d) for d in (1, 2, 3)]
    *down, down_done = down_pair((half_o,), kept, swap(jnp.stack(sent)))
    g_all, attention_done = attend_back((down_done,), info, q, k, v, parts, log_total, cosine, sine)
    down = [down[0]] + [shift(after(down[d], attention_done), d if d < 3 else -1) for d in (1, 2, 3)]
    send, send_done = input_send((), info, g_all, w_qkv)
    layer_output, output_done = result(info, *down, resid, b_d)
    narrow, own = narrow_sums((send_done,), info, g_all, b_q, b_k, b_v, low_qkv, mix, parts)
    pair, *total, pair_done = input_pair((narrow,), info, g_all, w_qkv, swap(send))
    total = [shift(total[d - 1], d if d < 3 else -1) for d in (1, 2, 3)]
    narrow = (narrow.astype(F32) + swap(narrow).astype(F32)).astype(BF)
    late, glow_own = late_sums((pair_done, *arrived(down[1], down[3])), info, line(narrow, shift), n1)
    grad_in, input_done = last((), info, pair, *total, glow_own, a_qkv, grad_resid, x_l, gains)

    early = lax.all_gather(after(early, glow_own), "sp", axis=0, tiled=False)
    *fed, spread, spread_done = early_result(early)
    own = lax.dynamic_update_slice(jnp.zeros((16, 16, 2048), BF), own.reshape(4, 16, 2048), (4 * y_at, 0, 0))
    final = jnp.concatenate([late, own, half_o.reshape(16, 16, 512)], 2)
    final = lax.all_to_all(final, "fs", split_axis=0, concat_axis=0, tiled=False)
    final = sum_groups((input_done, output_done, spread_done), final)
    near = line(final, shift)
    grad_in_d, grad_out_d = final_result((), near, [swap(part) for part in near], spread)
    return (layer_output[None], grad_in[None], grad_in_d, grad_out_d, *fed)


def solution(mesh):
    in_specs = (
        P("fs", "sp", None),
        P("fs", "sp", None),
        P(),
        P("fs", None, None),
        P("fs", None),
        P("fs", None, None),
        P("fs", None),
        P(None, "fs", None),
        P(None, "fs", None),
        P(None, "fs", None),
        P(None, "fs", None),
        P("fs", None),
        P("fs", None),
    )
    out_specs = (
        P("fs", "sp", None),
        P("fs", "sp", None),
        P(None, "fs", None),
        P(None, "fs", None),
        P(None, "fs", None),
        P(None, "fs", None),
    )
    return jax.shard_map(body, mesh=mesh, in_specs=in_specs, out_specs=out_specs, check_vma=False)
```

```python
import functools

import jax
import jax.numpy as jnp
from jax import lax
from jax.experimental import pallas as pl
from jax.experimental.pallas import tpu as pltpu
from jax.sharding import PartitionSpec as P

HEAD_SIZE = 64
ADAPTER_RANK = 16
NORM_EPS = 1e-05
ROPE_BASE = 130000.0
MASK_FILL = -1e30
BF = jnp.bfloat16
F32 = jnp.float32
WIDTH = 2048
ROWS = 128
ORDER = (2, 1, 3, 0)
SPEED = 1e3


def mm(left, right):
    return jnp.dot(left, right, preferred_element_type=F32)


def mm_nt(left, right):
    return lax.dot_general(left, right, (((1,), (1,)), ((), ())), preferred_element_type=F32)


def mm_tn(left, right):
    return lax.dot_general(left, right, (((0,), (0,)), ((), ())), preferred_element_type=F32)


def shift(x, chips):
    return lax.ppermute(x, "sp", [(i, ((i // 2 + chips) % 4) * 2 + i % 2) for i in range(8)])


def swap(x):
    return lax.ppermute(x, "sp", [(i, i ^ 1) for i in range(8)])


def shift_z(x, chips):
    return lax.ppermute(x, "fs", [(i, (i + 4 * chips) % 16) for i in range(16)])


def shift_x(x, chips):
    return lax.ppermute(x, "fs", [(i, i - i % 4 + (i + chips) % 4) for i in range(16)])


Y_LINES = [[0, 2, 4, 6], [1, 3, 5, 7]]


def gather_y(x):
    return lax.all_gather(x, "sp", axis=0, tiled=False, axis_index_groups=Y_LINES)


def exchange_y(x):
    return lax.all_to_all(x, "sp", split_axis=0, concat_axis=0, axis_index_groups=Y_LINES)


def line(x, move):
    return [x, move(x, -1), move(x, 2), move(x, 1)]


VMEM = pl.BlockSpec(memory_space=pltpu.VMEM)
SMEM = pl.BlockSpec(memory_space=pltpu.SMEM)


def after(x, *deps):
    anywhere = pl.BlockSpec(memory_space=pl.ANY)
    return pl.pallas_call(
        lambda *refs: None,
        out_shape=jax.ShapeDtypeStruct(x.shape, x.dtype),
        in_specs=[anywhere] * (1 + len(deps)),
        out_specs=anywhere,
        input_output_aliases={0: 0},
        cost_estimate=pl.CostEstimate(flops=0, bytes_accessed=0, transcendentals=0),
    )(x, *deps)


class Info:
    def __init__(self, spans, choice):
        s_at, f_at = lax.axis_index("sp"), lax.axis_index("fs")
        self.values = [s_at >> 1, s_at & 1]
        if spans is None:
            self.values += [None] * 5
        else:
            self.values += [spans[0, 0], spans[0, 0] + spans[0, 1]] + [choice[0, i] for i in range(3)]
        self.values += [f_at >> 2, f_at & 3]

    def __getitem__(self, index):
        return self.values[index]


def call(kernel, outs, scratch, args, limit, deps=(), anywhere=(), to=pltpu.VMEM, us=2.0, token=False):
    outs = [jax.ShapeDtypeStruct(shape, dtype) for shape, dtype in outs]
    rows, args = args[0], args[1:]
    first = len(rows)
    count = first + len(args) + len(anywhere)
    skip = count + len(deps)
    spread = [pl.BlockSpec(memory_space=pl.ANY)] * len(anywhere)
    mark = count + len(deps) + len(outs)
    spread += [pl.BlockSpec(memory_space=pl.ANY)] * len(deps)

    def run(*refs):
        info = Info(*refs[:2]) if rows else Info(None, None)
        if token:
            refs[mark][...] = jnp.zeros((8, 128), F32)
            refs = refs[:mark] + refs[mark + 1 :]
        kernel(info, *refs[first:count], *refs[skip:])

    return pl.pallas_call(
        run,
        out_shape=outs + [jax.ShapeDtypeStruct((8, 128), F32)] * token,
        in_specs=[SMEM] * first + [VMEM] * len(args) + spread,
        out_specs=[pl.BlockSpec(memory_space=to)] * len(outs) + [VMEM] * token,
        scratch_shapes=[pltpu.VMEM(*item) if isinstance(item, tuple) else item for item in scratch],
        compiler_params=pltpu.CompilerParams(vmem_limit_bytes=limit << 20),
        cost_estimate=pl.CostEstimate(flops=int(us * SPEED), bytes_accessed=1 << 10, transcendentals=0),
    )(*rows, *args, *anywhere, *deps)


def lane_mask(info, first, rows):
    token = first + lax.broadcasted_iota(jnp.int32, (rows, 128), 0)
    lane = lax.broadcasted_iota(jnp.int32, (rows, 128), 1) // ADAPTER_RANK
    chosen = jnp.where(token < info[2], info[4], jnp.where(token < info[3], info[5], info[6]))
    return lane == chosen


def chip_mask(info, step):
    chip, core = (info[0] + step) % 4, info[1]
    return jnp.concatenate(
        [
            lane_mask(info, (2 * chip + core) * ROWS, ROWS),
            lane_mask(info, (2 * chip + 1 - core) * ROWS, ROWS),
        ],
        0,
    )


def turn(a, b, cosine, sine):
    return a * cosine - b * sine, b * cosine + a * sine


def aligned(index, unit):
    return pl.ds(pl.multiple_of(index, unit), unit)


def own_first(info, block):
    return (block // 2) * 256 + ((info[1] + block) % 2) * ROWS


def pack_kernel(info, w_hbm, a_in_hbm, a_out_hbm, w_o_hbm, w_pack, ab_pack, w, a_in, a_out, w_o, sems):
    y_at, core = info[0], info[1]
    half = aligned(64 * core, 64)
    copies = [
        pltpu.make_async_copy(w_hbm.at[:, :, aligned(512 * y_at, 512)], w, sems.at[0]),
        pltpu.make_async_copy(a_in_hbm.at[0:4], a_in, sems.at[1]),
        pltpu.make_async_copy(a_out_hbm.at[0:4], a_out, sems.at[2]),
        pltpu.make_async_copy(w_o_hbm.at[aligned(64 * core + 16 * y_at, 16)], w_o, sems.at[3]),
    ]
    for copy in copies:
        copy.start()
    i = lax.broadcasted_iota(jnp.int32, (512, 256), 0)
    j = lax.broadcasted_iota(jnp.int32, (512, 256), 1)
    pick_qk = i == ((j % 128) // 32) * 128 + core * 64 + (j // 128) * 32 + j % 32
    pick_v = i == (j // 64) * 128 + core * 64 + j % 64
    for copy in copies:
        copy.wait()
    for part, pick in enumerate((pick_qk, pick_qk, pick_v)):
        columns = mm(w[part], pick.astype(BF)).astype(BF)
        if part < 2:
            w_pack[:, 256 * part : 256 * part + 256] = columns
        else:
            w_pack[:, 512:640] = columns[:, :128]
            ab_pack[:, 768:] = columns[:, 128:]
    for part in range(3):
        ab_pack[:, 128 * part : 128 * part + 128] = a_in[part]
    ab_pack[:64, 384:512] = a_out[0, half, :]
    ab_pack[64:, 384:512] = a_out[1, half, :]
    ab_pack[:64, 512:640] = a_out[2, half, :]
    ab_pack[64:, 512:640] = a_in[3, half, :]
    ab_pack[:, 640:768] = a_out[3]
    for part in range(8):
        lanes = slice(256 * part, 256 * part + 256)
        w_pack[16 * part : 16 * part + 16, 640:] = w_o[:, lanes]


def pack(w, a_in, a_out, w_o):
    scratch = [
        ((3, ROWS, 512), BF),
        ((4, ROWS, 128), BF),
        ((4, ROWS, 128), BF),
        ((16, WIDTH), BF),
        pltpu.SemaphoreType.DMA((4,)),
    ]
    outs = [((ROWS, 896), BF), ((ROWS, 896), BF)]
    return call(pack_kernel, outs, scratch, ((),), 60, (), (w, a_in, a_out, w_o), us=1.5)


def pack_feed_kernel(info, w_gu, w_d, a_in, a_out, in_ff, out_ff, out):
    y_at, core = info[0], info[1]
    i = lax.broadcasted_iota(jnp.int32, (128, 128), 0)
    j = lax.broadcasted_iota(jnp.int32, (128, 128), 1)
    first = ((j < 64) & (i == j + 64 * core)).astype(BF)
    second = ((j >= 64) & (i == j - 64 + 64 * core)).astype(BF)
    for part in range(2):
        for block in range(8):
            left = w_gu[:, part, aligned(1024 * block + 128 * y_at, 128)]
            right = w_gu[:, part, aligned(1024 * block + 512 + 128 * y_at, 128)]
            lanes = slice(1024 * part + 128 * block, 1024 * part + 128 * block + 128)
            out[:ROWS, lanes] = (mm(left, first) + mm(right, second)).astype(BF)
    out[:ROWS, 2048:2176] = a_in[4]
    out[:ROWS, 2176:2304] = a_in[5]
    out[:ROWS, 2304:] = a_out[4]
    eighth = aligned(64 * (2 * y_at + core), 64)
    out[ROWS:, :WIDTH] = w_d[eighth, :]
    out[ROWS:, 2048:2176] = in_ff[0, eighth, :]
    out[ROWS:, 2176:2304] = out_ff[0, eighth, :]
    out[ROWS:, 2304:] = out_ff[1, eighth, :]


def pack_feed(deps, *args):
    return call(pack_feed_kernel, [((192, 2432), BF)], [], ((), *args), 12, deps, us=3)[0]


def stack_rows(deps, *lists):
    counts = [len(parts) for parts in lists]

    def kernel(info, *refs):
        sems, outs, refs = refs[-1], refs[sum(counts) : -1], refs[: sum(counts)]
        copies = []
        for count, out in zip(counts, outs):
            for i in range(count):
                copies.append(pltpu.make_async_copy(refs[len(copies)], out.at[i], sems.at[len(copies)]))
        for copy in copies:
            copy.start()
        for copy in copies:
            copy.wait()

    outs = [((len(parts),) + parts[0].shape, parts[0].dtype) for parts in lists]
    sems = pltpu.SemaphoreType.DMA((sum(counts),))
    return call(kernel, outs, [sems], ((),), 4, deps, sum(lists, []), pl.ANY, us=1)


def stack_output(others, parts):
    def kernel(info, *refs):
        for i, part in enumerate(refs[:4]):
            refs[-1][i] = part[:, :, 640:]

    shape = ((4, 4, ROWS, 256), BF)
    return call(kernel, [shape], [], ((), *parts), 8, (), others, us=1, token=True)


def arrived(*parts):
    return [part[:8, :128] for part in parts]


def norm_kernel(info, x, gain, out):
    values = x[...].astype(F32)
    inverse = lax.rsqrt(jnp.mean(values * values, -1, keepdims=True) + NORM_EPS)
    out[...] = (values * inverse * gain[0:1, :]).astype(BF)


def norm_first(deps, info, x, gain):
    return call(norm_kernel, [((ROWS, WIDTH), BF)], [], (info, x, gain), 4, deps, us=0.6)[0]


def copy_kernel(info, x, out):
    out[...] = x[...]


def copy_after(deps, info, x):
    return call(copy_kernel, [(x.shape, x.dtype)], [], (info, x), 4, deps)[0]


def qkv_kernel(info, cosine, sine, a0, a1, a2, a3, b0, b1, b2, b3, near, far, *refs):
    q, k, v, low_out, n1, w, a, b_q, b_k, b_v, a_o, b_o, rest, sems = refs
    z_at, x_at, y_at, core = info[7], info[8], info[0], info[1]
    copies, weights = [], []
    for dz in range(4):
        for dx in range(4):
            f = ((z_at + dz) % 4) * 4 + (x_at + dx) % 4
            rows = aligned(f * ROWS, ROWS)
            one, two = (a0, a1, a2, a3)[dz].at[dx], (b0, b1, b2, b3)[dx].at[dz]
            weights.append(pltpu.make_async_copy(two.at[:, :384], a.at[rows], sems.at[1]))
            weights.append(pltpu.make_async_copy(two.at[:, 384:640], rest.at[rows], sems.at[2]))
            weights.append(pltpu.make_async_copy(one.at[:, :640], w.at[rows, :640], sems.at[3]))
            weights.append(pltpu.make_async_copy(two.at[:, 768:], w.at[rows, 640:], sems.at[5]))
            copies.append(pltpu.make_async_copy(two.at[:, 640:768], b_o.at[rows], sems.at[4]))
    tokens = []
    for chip in range(4):
        own, other = chip * 256 + ROWS * core, chip * 256 + ROWS * (1 - core)
        tokens.append(pltpu.make_async_copy(near.at[chip], n1.at[aligned(own, ROWS)], sems.at[0]))
        tokens.append(pltpu.make_async_copy(far.at[chip], n1.at[aligned(other, ROWS)], sems.at[0]))
    for copy in tokens + weights + copies:
        copy.start()
    for copy in tokens + weights:
        copy.wait()
    for head in range(4):
        first = (4 * y_at + head) * ROWS
        for half in range(2):
            to = slice(half * 128 + head * 32, half * 128 + head * 32 + 32)
            b_q[to, :] = rest[aligned(first + 32 * half, 32), :128]
            b_k[to, :] = rest[aligned(first + 64 + 32 * half, 32), :128]
        b_v[64 * head : 64 * head + 64, :] = rest[aligned(first, 64), 128:]
    for f in range(16):
        a_o[64 * f : 64 * f + 64, :] = rest[f * ROWS + 64 : f * ROWS + 128, 128:]
    for chip in range(4):
        at = slice(256 * chip, 256 * chip + 256)
        rows = n1[at, :]
        mask = lane_mask(info, 256 * chip, 256)
        low = jnp.where(jnp.concatenate([mask] * 3, 1), mm(rows, a[...]), 0.0).astype(BF)
        low_out[at, :] = low
        cos, sin = cosine[at, :], sine[at, :]
        for j, (b, out) in enumerate(((b_q, q), (b_k, k))):
            base = mm(rows, w[:, 256 * j : 256 * j + 256])
            values = base + mm_nt(low[:, 128 * j : 128 * j + 128], b[...])
            first, second = turn(values[:, :128], values[:, 128:], cos, sin)
            out[at, :128] = first.astype(BF)
            out[at, 128:] = second.astype(BF)
        v[at, :] = (mm(rows, w[:, 512:]) + mm_nt(low[:, 256:], b_v[...])).astype(BF)
    for copy in copies:
        copy.wait()


def project_qkv(deps, info, w_parts, ab_parts, near, far, cosine, sine):
    return call(
        qkv_kernel,
        [
            ((1024, 256), BF),
            ((1024, 256), BF),
            ((1024, 256), BF),
            ((1024, 384), BF),
            ((1024, WIDTH), BF),
            ((WIDTH, 768), BF),
            ((WIDTH, 384), BF),
            ((256, 128), BF),
            ((256, 128), BF),
            ((256, 128), BF),
            ((1024, 128), BF),
            ((WIDTH, 128), BF),
        ],
        [((WIDTH, 256), BF), pltpu.SemaphoreType.DMA((6,))],
        (info, cosine, sine),
        48,
        deps,
        (*w_parts, *ab_parts, near, far), us=9)


def head_lanes(head, rows, paired):
    lane = lax.broadcasted_iota(jnp.int32, (rows, 256), 1)
    return ((lane % 128) // 32 if paired else lane // 64) == head


def key_bias(info, block):
    n = 256 * (block + 1)
    j = lax.broadcasted_iota(jnp.int32, (n, 256), 0)
    i = 256 * block + lax.broadcasted_iota(jnp.int32, (n, 256), 1)
    allowed = (j <= i) & ((j < info[2]) | (j >= info[3]) | (i < info[3]))
    return jnp.where(allowed, 0.0, MASK_FILL)


def attend_kernel(info, q, k, v, mix, log_total, v_heads, probs):
    for head in range(4):
        v_heads[head] = jnp.where(head_lanes(head, 1024, False), v[...], 0)
    for block in range(4):
        n = 256 * (block + 1)
        rows = slice(256 * block, 256 * block + 256)
        bias = key_bias(info, block)
        out = jnp.zeros((256, 256), F32)
        for head in range(4):
            q_head = jnp.where(head_lanes(head, 256, True), q[rows, :], 0) * jnp.array(0.125, BF)
            scores = mm_nt(k[:n, :], q_head) + bias
            top = jnp.max(scores, 0, keepdims=True)
            weights = jnp.exp(scores - top)
            total = jnp.sum(weights, 0, keepdims=True)
            log_total[head : head + 1, rows] = top + jnp.log(total)
            probs[head, :n, :] = (weights * (1.0 / total)).astype(BF)
        for head in range(4):
            out = out + mm_tn(probs[head, :n, :], v_heads[head, :n, :])
        out = out.astype(BF)
        for part in range(2):
            row = own_first(info, 2 * block + part)
            mix[aligned(row, ROWS), :] = out[part * ROWS : part * ROWS + ROWS]


def attend(info, q, k, v):
    return call(
        attend_kernel,
        [((1024, 256), BF), ((8, 1024), F32)],
        [((4, 1024, 256), BF), ((4, 1024, 256), BF)],
        (info, q, k, v),
        16, us=6)


def attend_back_kernel(
    info, q, k, v, g0, g1, g2, g3, log_total, cosine, sine, out, q_heads, g_heads, k_heads, probs, grads, dk, dv
):
    core = info[1]
    for d, part in enumerate((g0, g1, g2, g3)):
        block = (info[0] - d + 4) % 4
        for other in range(2):
            rows = part[other * ROWS : other * ROWS + ROWS, :256]
            second = (core + other) % 2
            for head in range(4):
                g_heads[block, aligned(256 * head + ROWS * second, ROWS), :] = jnp.where(
                    head_lanes(head, ROWS, False), rows, 0
                )
    for head in range(4):
        k_heads[head] = jnp.where(head_lanes(head, 1024, True), k[...], 0) * jnp.array(0.125, BF)
    dk[...] = jnp.zeros_like(dk)
    dv[...] = jnp.zeros_like(dv)

    def unrotate(values, rows):
        a, b = values[:, :128].astype(F32), values[:, 128:].astype(F32)
        first, last = turn(a, b, cosine[rows, :], -sine[rows, :])
        return jnp.concatenate([first, last], 1).astype(BF)

    for block in range(4):
        n = 256 * (block + 1)
        rows = slice(256 * block, 256 * block + 256)
        bias = key_bias(info, block)
        for head in range(4):
            at = slice(256 * head, 256 * head + 256)
            q_head = jnp.where(head_lanes(head, 256, True), q[rows, :], 0) * jnp.array(0.125, BF)
            q_heads[at, :] = q_head
            scores = mm_nt(k[:n, :], q_head) + bias
            p = jnp.exp(scores - log_total[head : head + 1, rows])
            dp = mm_nt(v[:n, :], g_heads[block, at, :])
            inner = jnp.sum(p * dp, 0, keepdims=True)
            probs[:n, at] = p.astype(BF)
            grads[:n, at] = (p * (dp - inner)).astype(BF)
        dv[:n, :] += mm(probs[:n, :], g_heads[block])
        dk[:n, :] += mm(grads[:n, :], q_heads[...])
        dq = jnp.zeros((256, 256), F32)
        for head in range(4):
            dq = dq + mm_tn(grads[:n, 256 * head : 256 * head + 256], k_heads[head, :n, :])
        out[rows, 0:256] = unrotate(dq.astype(BF), rows)
    for block in range(4):
        rows = slice(256 * block, 256 * block + 256)
        out[rows, 256:512] = unrotate(dk[rows, :].astype(BF), rows)
        out[rows, 512:768] = dv[rows, :].astype(BF)


def attend_back(deps, info, q, k, v, parts, log_total, cosine, sine):
    return call(
        attend_back_kernel,
        [((1024, 768), BF)],
        [
            ((1024, 256), BF),
            ((4, 1024, 256), BF),
            ((4, 1024, 256), BF),
            ((1024, 1024), BF),
            ((1024, 1024), BF),
            ((1024, 256), F32),
            ((1024, 256), F32),
        ],
        (info, q, k, v, *parts, log_total, cosine, sine),
        15,
        deps, us=9, token=True)


def output_kernel(info, parts, w0, w1, w2, w3, a_o, keep, send, w, mix):
    z_at, x_at = info[7], info[8]
    for dy, piece in enumerate((w0, w1, w2, w3)):
        chip = (info[0] + dy) % 4
        mix[:, 256 * dy : 256 * dy + 256] = parts[dy]
        for dz in range(4):
            for dx in range(4):
                f = ((z_at + dz) % 4) * 4 + (x_at + dx) % 4
                rows = aligned(f * 64 + 16 * chip, 16)
                for part in range(8):
                    w[rows, 256 * part : 256 * part + 256] = piece[dz, dx, 16 * part : 16 * part + 16]
    keep[:, :WIDTH] = mm(mix[:ROWS, :], w[...])
    keep[:, WIDTH:] = mm(mix[:ROWS, :], a_o[...])
    send[:, :WIDTH] = mm(mix[ROWS:, :], w[...]).astype(BF)
    send[:, WIDTH:] = mm(mix[ROWS:, :], a_o[...]).astype(BF)


def project_output(info, mixes, pieces, a_o):
    return call(
        output_kernel,
        [((ROWS, 2176), F32), ((ROWS, 2176), BF), ((1024, WIDTH), BF)],
        [((256, 1024), BF)],
        (info, mixes, *pieces, a_o),
        8, us=4)


def middle_kernel(info, keep, got, x, b_o, gain, resid, n2, low):
    summed = keep[...] + got[...].astype(F32)
    mask = lane_mask(info, (2 * info[0] + info[1]) * ROWS, ROWS)
    low_o = jnp.where(mask, summed[:, WIDTH:], 0.0).astype(BF)
    low[...] = low_o
    values = x[...].astype(F32) + summed[:, :WIDTH] + mm_nt(low_o, b_o[...])
    resid[...] = values
    inverse = lax.rsqrt(jnp.mean(values * values, -1, keepdims=True) + NORM_EPS)
    n2[...] = (values * inverse * gain[1:2, :]).astype(BF)


def middle(deps, info, keep, got, x, b_o, gain):
    return call(
        middle_kernel,
        [((ROWS, WIDTH), F32), ((ROWS, WIDTH), BF), ((ROWS, 128), BF)],
        [],
        (info, keep, got, x, b_o, gain),
        10,
        deps, us=1)


def load_weights(gathered, w_g, w_u, w_d, a_gu, b_d, ff, sems):
    small = [
        pltpu.make_async_copy(gathered.at[:, :ROWS, 2048:2304], a_gu, sems.at[0]),
        pltpu.make_async_copy(gathered.at[:, :ROWS, 2304:], b_d, sems.at[1]),
        pltpu.make_async_copy(gathered.at[:, ROWS:, 2048:], ff, sems.at[2]),
    ]
    blocks = []
    for i in range(4):
        at, up = pl.ds(256 * i, 256), pl.ds(1024 + 256 * i, 256)
        rows = pl.ds(4 * i, 4)
        blocks.append(
            [
                pltpu.make_async_copy(gathered.at[:, :ROWS, at], w_g.at[:, :, at], sems.at[3 + 3 * i]),
                pltpu.make_async_copy(gathered.at[:, :ROWS, up], w_u.at[:, :, at], sems.at[4 + 3 * i]),
                pltpu.make_async_copy(gathered.at[rows, ROWS:, :WIDTH], w_d.at[rows], sems.at[5 + 3 * i]),
            ]
        )
    for group in [small] + blocks:
        for copy in group:
            copy.start()
    return [small] + blocks


def feed_kernel(step, first, info, *refs):
    if first:
        n_near, n_far, g_near, g_far, gathered, *outs = refs[:13]
        w_g, w_u, w_d, a_gu, b_d, ff, n_rows, g_rows, row_sems, sems = refs[13:]
    else:
        w_g, w_u, w_d, a_gu, b_d, ff, n_near, n_far, g_near, g_far, *outs = refs[:18]
        n_rows, g_rows, row_sems = refs[18:]
    keep_down, send_down, keep_back, send_back, hidden, grad_gate, grad_up, lows = outs
    chip = (info[0] + step) % 4
    row_copies = [
        pltpu.make_async_copy(part, rows.at[at : at + ROWS], row_sems.at[i])
        for i, (part, rows, at) in enumerate(
            (
                (n_near, n_rows, 0),
                (n_far, n_rows, ROWS),
                (g_near.at[chip], g_rows, 0),
                (g_far.at[chip], g_rows, ROWS),
            )
        )
    ]
    for copy in row_copies:
        copy.start()
    groups = load_weights(gathered, w_g, w_u, w_d, a_gu, b_d, ff, sems) if first else [[]] * 5
    for copy in row_copies[:2]:
        copy.wait()
    mask = chip_mask(info, step)
    twice = jnp.concatenate([mask, mask], 1)
    for copy in groups[0]:
        copy.wait()
    low = jnp.where(twice, mm(n_rows[...], a_gu[...].reshape(WIDTH, 256)), 0.0).astype(BF)
    for copy in row_copies[2:]:
        copy.wait()
    glow = jnp.where(mask, mm(g_rows[...], b_d[...].reshape(WIDTH, 128)), 0.0).astype(BF)
    lows[:, :256] = low
    lows[:, 256:384] = glow
    for block in range(4):
        at = slice(256 * block, 256 * block + 256)
        rows = slice(4 * block, 4 * block + 4)
        for copy in groups[1 + block]:
            copy.wait()
        thin = ff[rows].reshape(256, 384)
        gate = mm(n_rows[...], w_g[:, :, at].reshape(WIDTH, 256)) + mm_nt(low[:, :128], thin[:, 128:256])
        up = mm(n_rows[...], w_u[:, :, at].reshape(WIDTH, 256)) + mm_nt(low[:, 128:], thin[:, 256:])
        grad_hidden = mm_nt(g_rows[...], w_d[rows].reshape(256, WIDTH)) + mm_nt(glow, thin[:, :128])
        sig = 1.0 / (1.0 + jnp.exp(-gate))
        act = gate * sig
        hidden[:, at] = (act * up).astype(BF)
        grad_gate[:, at] = (grad_hidden * up * sig * (1.0 + gate * (1.0 - sig))).astype(BF)
        grad_up[:, at] = (grad_hidden * act).astype(BF)

    def put(keep, send, at, values):
        keep[:, at] = values[:ROWS].astype(BF)
        send[:, at] = values[ROWS:].astype(BF)

    for block in range(8):
        at = slice(256 * block, 256 * block + 256)
        pair = slice(2 * block, 2 * block + 2)
        left = mm_nt(grad_gate[...], w_g[pair].reshape(256, 1024))
        right = mm_nt(grad_up[...], w_u[pair].reshape(256, 1024))
        put(keep_back, send_back, at, left + right)
        put(keep_down, send_down, at, mm(hidden[...], w_d[:, :, at].reshape(1024, 256)))
    thin = ff[...].reshape(1024, 384)
    glow_g = mm(grad_gate[...], thin[:, 128:256])
    glow_u = mm(grad_up[...], thin[:, 256:])
    low_d = mm(hidden[...], thin[:, :128])
    put(keep_back, send_back, slice(WIDTH, WIDTH + 128), glow_g)
    put(keep_back, send_back, slice(WIDTH + 128, WIDTH + 256), glow_u)
    put(keep_down, send_down, slice(WIDTH, WIDTH + 128), low_d)
    lows[:, 384:512] = jnp.where(mask, glow_g, 0.0).astype(BF)
    lows[:, 512:640] = jnp.where(mask, glow_u, 0.0).astype(BF)
    lows[:, 640:] = jnp.where(mask, low_d, 0.0).astype(BF)


def feed(step, deps, info, tokens, weights):
    first = len(weights) == 1
    shapes = [
        ((ROWS, 2176), BF),
        ((ROWS, 2176), BF),
        ((ROWS, 2304), BF),
        ((ROWS, 2304), BF),
        ((256, 1024), BF),
        ((256, 1024), BF),
        ((256, 1024), BF),
        ((256, 768), BF),
    ]
    scratch = [((256, WIDTH), BF), ((256, WIDTH), BF), pltpu.SemaphoreType.DMA((4,))]
    kernel = functools.partial(feed_kernel, step, first)
    if not first:
        return call(kernel, shapes, scratch, (info, *weights), 10, deps, tokens, us=9), weights
    held = [(16, ROWS, 1024), (16, ROWS, 1024), (16, 64, WIDTH), (16, ROWS, 256), (16, ROWS, 128), (16, 64, 384)]
    shapes += [(shape, BF) for shape in held]
    scratch.append(pltpu.SemaphoreType.DMA((15,)))
    outs = call(kernel, shapes, scratch, (info,), 26, deps, (*tokens, *weights), us=12)
    return outs[:8], outs[8:]


def early_kernel(info, *refs):
    chunks = [refs[4 * i : 4 * i + 4] for i in range(4)]
    parts = refs[16:24]
    g_near, g_far, by_token, by_hidden, n_rows, g_rows, sems = refs[24:]
    copies = []
    for i, d in enumerate(ORDER):
        chip = (info[0] + d) % 4
        for far in range(2):
            to = pl.ds((2 * i + far) * ROWS, ROWS)
            copies.append(pltpu.make_async_copy(parts[4 * far + d], n_rows.at[to], sems.at[2 * i + far]))
            source = (g_near, g_far)[far].at[chip]
            copies.append(pltpu.make_async_copy(source, g_rows.at[to], sems.at[8 + 2 * i + far]))
    for copy in copies:
        copy.start()
    flip = lambda values: values.astype(F32).T.astype(BF)
    thins = [flip(chunk[3][...]) for chunk in chunks]
    for j, (row, name) in enumerate(((2, 0), (0, 1), (1, 2))):
        rows = slice(128 * row, 128 * row + 128)
        total = sum(mm(thins[i][rows], chunks[i][name][...]) for i in range(4))
        by_hidden[:, 128 * j : 128 * j + 128] = total.T.astype(BF)
    for copy in copies:
        copy.wait()
    for j, (row, tokens) in enumerate(((3, n_rows), (4, n_rows), (5, g_rows))):
        rows = slice(128 * row, 128 * row + 128)
        total = sum(mm(thins[i][rows], tokens[256 * i : 256 * i + 256, :]) for i in range(4))
        by_token[:, 128 * j : 128 * j + 128] = total.T.astype(BF)


def early_sums(tokens, chunks, deps):
    args = [()] + [part for chunk in chunks for part in chunk]
    scratch = [((1024, WIDTH), BF), ((1024, WIDTH), BF), pltpu.SemaphoreType.DMA((16,))]
    outs = [((WIDTH, 384), BF), ((1024, 384), BF)]
    return call(early_kernel, outs, scratch, args, 16, deps, tokens, us=4.5)


def between_kernel(info, own, r1, r2, r3, a_gu, resid, og, low, gain, grad_resid, grad_attn):
    total = own[...] + r1[...].astype(F32) + r2[...].astype(F32) + r3[...].astype(F32)
    mask = lane_mask(info, (2 * info[0] + info[1]) * ROWS, ROWS)
    glow = jnp.where(jnp.concatenate([mask, mask], 1), total[:, WIDTH:], 0.0).astype(BF)
    grad = total[:, :WIDTH] + mm_nt(glow, a_gu[...].reshape(WIDTH, 256))
    values = resid[...]
    inverse = lax.rsqrt(jnp.mean(values * values, -1, keepdims=True) + NORM_EPS)
    result = og[...].astype(F32) + norm_back(grad, values, inverse, gain[1:2, :])
    grad_resid[...] = result
    grad_attn[:, :WIDTH] = result.astype(BF)
    grad_attn[:, WIDTH:] = low[...]


def between(deps, info, own, r1, r2, r3, a_gu, resid, og, low, gain):
    return call(
        between_kernel,
        [((ROWS, WIDTH), F32), ((ROWS, 2176), BF)],
        [],
        (info, own, r1, r2, r3, a_gu, resid, og, low, gain),
        10,
        deps, us=1.4)


def combine_kernel(info, by_token, by_hidden, out):
    for f in range(16):
        out[f, :ROWS, :] = by_token[f * ROWS : f * ROWS + ROWS, :]
        out[f, ROWS:, :] = by_hidden[64 * f : 64 * f + 64, :]


def combine(by_token, by_hidden):
    return call(
        combine_kernel, [((16, 192, 384), BF)], [], ((), by_token, by_hidden), 8, us=1.6, token=True
    )


def down_kernel(info, k0, k1, k2, k3, got, own, *outs):
    for i, (d, keep) in enumerate(zip(ORDER, (k0, k1, k2, k3))):
        total = keep[...].astype(F32) + got[i].astype(F32)
        if d:
            outs[d - 1][...] = total.astype(BF)
        else:
            own[...] = total


def down_pair(deps, kept, got):
    return call(
        down_kernel,
        [((ROWS, 2176), F32)] + [((ROWS, 2176), BF)] * 3,
        [],
        ((), *kept, got),
        8,
        deps, us=1.5, token=True)


def result_kernel(info, own, r1, r2, r3, resid, b_d, out):
    total = own[...] + r1[...].astype(F32) + r2[...].astype(F32) + r3[...].astype(F32)
    mask = lane_mask(info, (2 * info[0] + info[1]) * ROWS, ROWS)
    low = jnp.where(mask, total[:, WIDTH:], 0.0).astype(BF)
    out[...] = (resid[...] + total[:, :WIDTH] + mm_nt(low, b_d[...].reshape(WIDTH, 128))).astype(BF)


def result(info, own, r1, r2, r3, resid, b_d):
    return call(
        result_kernel, [((ROWS, WIDTH), BF)], [], (info, own, r1, r2, r3, resid, b_d), 10, us=1.8, token=True)


def output_back_kernel(info, own, other, b_o, w_o, a_o, p0, p1, p2, p3, half, grad, mix):
    grad[:ROWS] = own[:, :WIDTH]
    grad[ROWS:] = other[:, :WIDTH]
    glow = jnp.where(chip_mask(info, 0), mm(grad[...], b_o[...]), 0.0).astype(BF)
    for chip in range(4):
        at = slice(256 * chip, 256 * chip + 256)
        mix[:, at] = (mm_nt(grad[...], w_o[at, :]) + mm_nt(glow, a_o[at, :])).astype(BF)
    for d, part in enumerate((p0, p1, p2, p3)):
        part[:, :256] = mix[:, aligned(256 * ((info[0] + d) % 4), 256)]
        part[:, 256:] = glow
    flip = lambda values: values.astype(F32).T.astype(BF)
    total = (mm(flip(own[:, WIDTH:]), grad[:ROWS]) + mm(flip(other[:, WIDTH:]), grad[ROWS:])).T.astype(BF)
    for f in range(16):
        rows = total[f * ROWS : f * ROWS + ROWS]
        half[64 * f : 64 * f + 64, :] = jnp.where(info[1] == 0, rows[:64], rows[64:])


def output_back(info, own, other, b_o, w_o, a_o):
    return call(
        output_back_kernel,
        [((256, 384), BF)] * 4 + [((1024, 128), BF)],
        [((256, WIDTH), BF), ((256, 1024), BF)],
        (info, own, other, b_o, w_o, a_o),
        8, us=2.7)


def pick_rows(info, g, core, out):
    for d in range(4):
        chip = (info[0] + d) % 4
        out[d * ROWS : d * ROWS + ROWS, :] = g[aligned(256 * chip + ROWS * core, ROWS), :]


def input_send_kernel(info, g, w, send, rows):
    pick_rows(info, g, 1 - info[1], rows)
    for block in range(8):
        at = slice(256 * block, 256 * block + 256)
        send[:, at] = mm_nt(rows[...], w[at, :]).astype(BF)


def input_send(deps, info, g, w):
    return call(input_send_kernel, [((512, WIDTH), BF)], [((512, 768), BF)], (info, g, w), 8, deps=deps, us=3.7, token=True)


def input_pair_kernel(info, g, w, got, own, p1, p2, p3, rows):
    pick_rows(info, g, info[1], rows)
    for block in range(8):
        at = slice(256 * block, 256 * block + 256)
        total = mm_nt(rows[...], w[at, :]) + got[:, at].astype(F32)
        own[:, at] = total[:ROWS]
        for d, out in enumerate((p1, p2, p3)):
            out[:, at] = total[ROWS * (d + 1) : ROWS * (d + 2)].astype(BF)


def input_pair(deps, info, g, w, got):
    return call(
        input_pair_kernel,
        [((ROWS, WIDTH), F32)] + [((ROWS, WIDTH), BF)] * 3,
        [((512, 768), BF)],
        (info, g, w, got),
        8,
        deps, us=3.5, token=True)


def squeeze(rows):
    i = lax.broadcasted_iota(jnp.int32, rows, 0) % ADAPTER_RANK
    j = lax.broadcasted_iota(jnp.int32, rows, 1) % ADAPTER_RANK
    return (i == j).astype(BF)


def narrow_kernel(info, g, b_q, b_k, b_v, low, mix, o0, o1, o2, o3, narrow, own):
    mask = lane_mask(info, 0, 1024)
    fold = squeeze((16, 128))
    flip = lambda values: values.astype(F32).T.astype(BF)
    for j, b in enumerate((b_q, b_k, b_v)):
        term = jnp.where(mask, mm(g[:, 256 * j : 256 * j + 256], b[...]), 0.0).astype(BF)
        narrow[16 * j : 16 * j + 16, :] = mm_nt(fold, term).astype(BF)
    low_t = flip(low[...])
    for j in range(3):
        total = mm(low_t[128 * j : 128 * j + 128], g[:, 256 * j : 256 * j + 256]).T.astype(BF)
        lanes = slice(128 * (j + 1), 128 * (j + 2))
        for head in range(4):
            if j == 2:
                own[head, :, lanes] = total[64 * head : 64 * head + 64]
            else:
                own[head, :32, lanes] = total[32 * head : 32 * head + 32]
                own[head, 32:, lanes] = total[128 + 32 * head : 160 + 32 * head]
    total = sum(
        mm(flip(part[:, 256:]), mix[aligned(256 * ((info[0] - d + 4) % 4), 256), :])
        for d, part in enumerate((o0, o1, o2, o3))
    ).T.astype(BF)
    for head in range(4):
        own[head, :, :128] = total[64 * head : 64 * head + 64]


def narrow_sums(deps, info, g, b_q, b_k, b_v, low, mix, parts):
    return call(
        narrow_kernel,
        [((48, 1024), BF), ((4, 64, 512), BF)],
        [],
        (info, g, b_q, b_k, b_v, low, mix, *parts),
        10,
        deps, us=2.3)


def late_kernel(info, parts, rows, out, glow_own):
    total = sum(parts[chip].astype(F32) for chip in range(4))
    total = total.astype(BF)
    s_at = 2 * info[0] + info[1]
    mask = lane_mask(info, 0, 1024)
    spread = squeeze((16, 128))
    wide = []
    for j in range(3):
        term = jnp.where(mask, mm_tn(total[16 * j : 16 * j + 16], spread), 0.0)
        wide.append(term)
    mask_own = lane_mask(info, s_at * ROWS, ROWS)
    for j in range(3):
        piece = jnp.zeros((ROWS, 128), F32)
        for block in range(8):
            piece = jnp.where(s_at == block, wide[j][block * ROWS : block * ROWS + ROWS], piece)
        glow_own[:, 128 * j : 128 * j + 128] = jnp.where(mask_own, piece, 0.0).astype(BF)
    thin = jnp.concatenate([term.T.astype(BF) for term in wide], 0)
    for f in range(8):
        at = slice(256 * f, 256 * f + 256)
        total = mm(thin, rows[:, at]).T
        for second in range(2):
            piece = jnp.zeros((16, 384), F32)
            for s in range(8):
                first = second * ROWS + 16 * s
                piece = jnp.where(s_at == s, total[first : first + 16], piece)
            out[2 * f + second] = piece.astype(BF)


def late_sums(deps, info, parts, rows):
    return call(
        late_kernel,
        [((16, 16, 384), BF), ((ROWS, 384), BF)],
        [],
        (info, parts, rows),
        10,
        deps, us=2.9)


def groups_kernel(info, values, out):
    total = values[0].astype(F32)
    for f in range(1, 16):
        total = total + values[f].astype(F32)
    out[...] = total.astype(BF)


def sum_groups(deps, values):
    return call(groups_kernel, [(values.shape[1:], BF)], [], ((), values), 8, deps, us=1.6)[0]


def early_result_kernel(info, values, one, two, spread):
    for j in range(3):
        lanes = slice(128 * j, 128 * j + 128)
        spread[j] = sum(values[s, :ROWS, lanes].astype(F32) for s in range(8))
        out, at = (one, 0) if j == 0 else (two, j - 1)
        for s in range(8):
            out[at, 64 * s : 64 * s + 64, :] = values[s, ROWS:, lanes].astype(F32)


def early_result(values):
    outs = [((1, 512, 128), F32), ((2, 512, 128), F32), ((3, ROWS, 128), F32)]
    return call(early_result_kernel, outs, [], ((), values), 8, us=2, token=True)


def final_kernel(info, *refs):
    y_at, core, z_at = info[0], info[1], info[7]
    spread, grad_in, grad_out, own = refs[8:]
    last = [0.0, 0.0]
    for d in range(4):
        chip = (y_at + d) % 4
        for other in range(2):
            part, at = refs[4 * other + d], (core + other) % 2
            for j in range(3):
                grad_in[j, aligned((2 * chip + at) * 16, 16), :] = part[:, 128 * j : 128 * j + 128].astype(F32)
            rows = aligned(64 * at, 16)

            @pl.when(chip == z_at)
            def _():
                own[pl.ds(16 * at, 16), :] = part[:, 384:2432].astype(F32)

            last[other] = last[other] + part[:, 2432:].astype(F32)
    for r in range(4):
        for j in range(4):
            lanes = slice(512 * r + 128 * j, 512 * r + 128 * j + 128)
            values = own[:, lanes]
            for i in range(32):
                out, at = (grad_in, 3) if j == 0 else (grad_out, j - 1)
                out[at, 4 * i + r : 4 * i + r + 1, :] = values[i : i + 1]
        lanes = slice(128 * r, 128 * r + 128)
        first = jnp.where(core == 0, last[0][:, lanes], last[1][:, lanes])
        second = jnp.where(core == 0, last[1][:, lanes], last[0][:, lanes])
        for i in range(16):
            grad_out[3, 4 * i + r : 4 * i + r + 1, :] = first[i : i + 1]
            grad_out[3, 64 + 4 * i + r : 64 + 4 * i + r + 1, :] = second[i : i + 1]
    grad_in[4] = spread[0]
    grad_in[5] = spread[1]
    grad_out[4] = spread[2]


def final_result(deps, near, far, spread):
    outs = [((6, ROWS, 128), F32), ((5, ROWS, 128), F32)]
    return call(final_kernel, outs, [((32, 2048), F32)], ((), *near, *far, spread), 8, deps, us=2)


def last_kernel(info, own, r1, r2, r3, glow, a, resid_grad, x, gain, out):
    grad = own[...] + r1[...].astype(F32) + r2[...].astype(F32) + r3[...].astype(F32) + mm_nt(glow[...], a[...])
    values = x[...].astype(F32)
    inverse = lax.rsqrt(jnp.mean(values * values, -1, keepdims=True) + NORM_EPS)
    out[...] = resid_grad[...] + norm_back(grad, values, inverse, gain[0:1, :])


def last(deps, info, own, r1, r2, r3, glow, a, resid_grad, x, gain):
    return call(
        last_kernel,
        [((ROWS, WIDTH), F32)],
        [],
        (info, own, r1, r2, r3, glow, a, resid_grad, x, gain),
        10, deps=deps, us=2.5, token=True)


def rms_inverse(values):
    return lax.rsqrt(jnp.mean(values * values, -1, keepdims=True) + NORM_EPS)


def norm_back(grad_norm, values, inverse, gain):
    normed = values * inverse
    scaled = grad_norm * gain
    return inverse * (scaled - normed * jnp.mean(scaled * normed, -1, keepdims=True))


def body(
    layer_input,
    output_gradient,
    norm_gain_pair,
    query_key_value_weight,
    output_weight,
    gate_up_weight,
    down_weight,
    adapter_input_model,
    adapter_output_model,
    adapter_input_hidden,
    adapter_output_hidden,
    spans,
    adapter_choice_rows,
):
    f_at, s_at = lax.axis_index("fs"), lax.axis_index("sp")
    y_at, c_at = s_at >> 1, s_at & 1
    z_at = f_at >> 2
    x_l = layer_input[0]
    og_l = output_gradient[0]
    rows = x_l.shape[0]
    tokens = 8 * rows
    gains = norm_gain_pair
    info = (spans, adapter_choice_rows)

    w_pack, ab_pack = pack(
        query_key_value_weight.transpose(1, 0, 2), adapter_input_model, adapter_output_model, output_weight
    )
    w_line, ab_line = line(w_pack, shift_x), line(ab_pack, shift_z)
    w_line, ab_line = stack_rows((), w_line, ab_line)
    w_parts, ab_parts = line(w_line, shift_z), line(ab_line, shift_x)
    n1_l = norm_first((w_pack,), info, x_l, gains)
    near = gather_y(n1_l)
    far = swap(near)
    g_near = gather_y(og_l)
    g_far = swap(g_near)
    feed_pack = pack_feed(
        (w_pack,),
        gate_up_weight,
        down_weight,
        adapter_input_model,
        adapter_output_model,
        adapter_input_hidden,
        adapter_output_hidden,
    )
    o_stack, p1_done = stack_output(ab_parts, w_parts)
    feed_all = lax.all_gather(after(feed_pack, p1_done), "fs", axis=0, tiled=False)

    at = jnp.arange(tokens, dtype=jnp.int32)
    position = at - jnp.where(at >= spans[0, 0] + spans[0, 1], spans[0, 1], 0)
    freq = ROPE_BASE ** (-(jnp.arange(32, dtype=F32) * 2.0 / HEAD_SIZE))
    phase = position.astype(F32)[:, None] * jnp.tile(freq, 4)[None, :]
    cosine, sine = jnp.cos(phase), jnp.sin(phase)

    o_parts = line(o_stack, shift)
    q, k, v, low_qkv, n1, w_qkv, a_qkv, b_q, b_k, b_v, a_o, b_o = project_qkv(
        (), info, w_parts, ab_parts, near, far, cosine, sine
    )
    mix, log_total = attend(info, q, k, v)
    mixes = exchange_y(mix.reshape(4, 256, 256))
    keep, send, w_o = project_output(info, mixes, o_parts, a_o)
    resid, n2_l, low_o = middle((), info, keep, swap(send), x_l, b_o, gains)

    n_near = line(n2_l, shift)
    n_far = [swap(part) for part in n_near]
    chunks, kept, sent, back, got = [], [], [], {}, []
    rows_there = arrived(*n_near[1:], *n_far)
    pairs = []
    weights = (feed_all,)
    for d in ORDER:
        deps = [chunks[-1][-1]] if chunks else rows_there
        if len(chunks) == 2:
            deps += arrived(pairs[0])
        if len(chunks) == 3:
            deps += arrived(pairs[2], back[ORDER[0]])
        outs, weights = feed(d, deps, info, (n_near[d], n_far[d], g_near, g_far), weights)
        keep_down, send_down, keep_back, send_back, *chunk = outs
        chunks.append(chunk)
        kept.append(keep_down)
        sent.append(send_down)
        got.append(swap(send_back))
        pair = keep_back.astype(F32) + got[-1].astype(F32)
        if d:
            pair = pair.astype(BF)
        pairs.append(pair)
        back[d] = shift(pair, d if d < 3 else -1) if d else pair
    a_gu, b_d = weights[3], weights[4]
    by_token, by_hidden = early_sums((*n_near, *n_far, g_near, g_far), chunks, arrived(back[ORDER[1]], back[ORDER[2]]))
    early, early_done = combine(by_token, by_hidden)
    early = lax.psum_scatter(early.reshape(16 * 192, 384), "fs", scatter_dimension=0, tiled=True)
    grad_resid, grad_attn = between((early_done,), info, back[0], back[1], back[2], back[3], a_gu, resid, og_l, low_o, gains)

    *parts, half_o = output_back(info, grad_attn, swap(grad_attn), b_o, w_o, a_o)
    parts = [parts[0]] + [shift(parts[d], d) for d in (1, 2, 3)]
    *down, down_done = down_pair((half_o,), kept, swap(jnp.stack(sent)))
    g_all, attention_done = attend_back((down_done,), info, q, k, v, parts, log_total, cosine, sine)
    down = [down[0]] + [shift(after(down[d], attention_done), d if d < 3 else -1) for d in (1, 2, 3)]
    send, send_done = input_send((), info, g_all, w_qkv)
    narrow, own = narrow_sums((send_done,), info, g_all, b_q, b_k, b_v, low_qkv, mix, parts)
    pair, *total, pair_done = input_pair((narrow,), info, g_all, w_qkv, swap(send))
    total = [shift(total[d - 1], d if d < 3 else -1) for d in (1, 2, 3)]
    narrow = (narrow.astype(F32) + swap(narrow).astype(F32)).astype(BF)
    narrow = exchange_y(jnp.broadcast_to(narrow[None], (4,) + narrow.shape))
    down = [down[0]] + [after(part, pair_done) for part in down[1:]]
    layer_output, output_done = result(info, *down, resid, b_d)
    late, glow_own = late_sums((pair_done, *arrived(*down[1:])), info, narrow, n1)
    grad_in, input_done = last((), info, pair, *total, glow_own, a_qkv, grad_resid, x_l, gains)

    early = lax.all_gather(after(early, glow_own), "sp", axis=0, tiled=False)
    *fed, spread, spread_done = early_result(early)
    own = lax.dynamic_update_slice(jnp.zeros((16, 16, 2048), BF), own.reshape(4, 16, 2048), (4 * y_at, 0, 0))
    final = jnp.concatenate([late, own, half_o.reshape(16, 16, 512)], 2)
    final = lax.all_to_all(final, "fs", split_axis=0, concat_axis=0, tiled=False)
    final = sum_groups((input_done, output_done, spread_done), final)
    near = line(final, shift)
    grad_in_d, grad_out_d = final_result((), near, [swap(part) for part in near], spread)
    return (layer_output[None], grad_in[None], grad_in_d, grad_out_d, *fed)


def solution(mesh):
    in_specs = (
        P("fs", "sp", None),
        P("fs", "sp", None),
        P(),
        P("fs", None, None),
        P("fs", None),
        P("fs", None, None),
        P("fs", None),
        P(None, "fs", None),
        P(None, "fs", None),
        P(None, "fs", None),
        P(None, "fs", None),
        P("fs", None),
        P("fs", None),
    )
    out_specs = (
        P("fs", "sp", None),
        P("fs", "sp", None),
        P(None, "fs", None),
        P(None, "fs", None),
        P(None, "fs", None),
        P(None, "fs", None),
    )
    return jax.shard_map(body, mesh=mesh, in_specs=in_specs, out_specs=out_specs, check_vma=False)
```

```python
import functools

import jax
import jax.numpy as jnp
from jax import lax
from jax.experimental import pallas as pl
from jax.experimental.pallas import tpu as pltpu
from jax.sharding import PartitionSpec as P

HEAD_SIZE = 64
ADAPTER_RANK = 16
NORM_EPS = 1e-05
ROPE_BASE = 130000.0
MASK_FILL = -1e30
BF = jnp.bfloat16
F32 = jnp.float32
WIDTH = 2048
ROWS = 128
ORDER = (2, 1, 3, 0)
SPEED = 1e3


def mm(left, right):
    return jnp.dot(left, right, preferred_element_type=F32)


def mm_nt(left, right):
    return lax.dot_general(left, right, (((1,), (1,)), ((), ())), preferred_element_type=F32)


def mm_tn(left, right):
    return lax.dot_general(left, right, (((0,), (0,)), ((), ())), preferred_element_type=F32)


def shift(x, chips):
    return lax.ppermute(x, "sp", [(i, ((i // 2 + chips) % 4) * 2 + i % 2) for i in range(8)])


def swap(x):
    return lax.ppermute(x, "sp", [(i, i ^ 1) for i in range(8)])


def shift_z(x, chips):
    return lax.ppermute(x, "fs", [(i, (i + 4 * chips) % 16) for i in range(16)])


def shift_x(x, chips):
    return lax.ppermute(x, "fs", [(i, i - i % 4 + (i + chips) % 4) for i in range(16)])


Y_LINES = [[0, 2, 4, 6], [1, 3, 5, 7]]


def gather_y(x):
    return lax.all_gather(x, "sp", axis=0, tiled=False, axis_index_groups=Y_LINES)


def exchange_y(x):
    return lax.all_to_all(x, "sp", split_axis=0, concat_axis=0, axis_index_groups=Y_LINES)


def line(x, move):
    return [x, move(x, -1), move(x, 2), move(x, 1)]


VMEM = pl.BlockSpec(memory_space=pltpu.VMEM)
SMEM = pl.BlockSpec(memory_space=pltpu.SMEM)


def after(x, *deps):
    anywhere = pl.BlockSpec(memory_space=pl.ANY)
    return pl.pallas_call(
        lambda *refs: None,
        out_shape=jax.ShapeDtypeStruct(x.shape, x.dtype),
        in_specs=[anywhere] * (1 + len(deps)),
        out_specs=anywhere,
        input_output_aliases={0: 0},
        cost_estimate=pl.CostEstimate(flops=0, bytes_accessed=0, transcendentals=0),
    )(x, *deps)


class Info:
    def __init__(self, spans, choice):
        s_at, f_at = lax.axis_index("sp"), lax.axis_index("fs")
        self.values = [s_at >> 1, s_at & 1]
        if spans is None:
            self.values += [None] * 5
        else:
            self.values += [spans[0, 0], spans[0, 0] + spans[0, 1]] + [choice[0, i] for i in range(3)]
        self.values += [f_at >> 2, f_at & 3]

    def __getitem__(self, index):
        return self.values[index]


def call(kernel, outs, scratch, args, limit, deps=(), anywhere=(), to=pltpu.VMEM, us=2.0, token=False):
    outs = [jax.ShapeDtypeStruct(shape, dtype) for shape, dtype in outs]
    rows, args = args[0], args[1:]
    first = len(rows)
    count = first + len(args) + len(anywhere)
    skip = count + len(deps)
    spread = [pl.BlockSpec(memory_space=pl.ANY)] * len(anywhere)
    mark = count + len(deps) + len(outs)
    spread += [pl.BlockSpec(memory_space=pl.ANY)] * len(deps)

    def run(*refs):
        info = Info(*refs[:2]) if rows else Info(None, None)
        if token:
            refs[mark][...] = jnp.zeros((8, 128), F32)
            refs = refs[:mark] + refs[mark + 1 :]
        kernel(info, *refs[first:count], *refs[skip:])

    return pl.pallas_call(
        run,
        out_shape=outs + [jax.ShapeDtypeStruct((8, 128), F32)] * token,
        in_specs=[SMEM] * first + [VMEM] * len(args) + spread,
        out_specs=[pl.BlockSpec(memory_space=to)] * len(outs) + [VMEM] * token,
        scratch_shapes=[pltpu.VMEM(*item) if isinstance(item, tuple) else item for item in scratch],
        compiler_params=pltpu.CompilerParams(vmem_limit_bytes=limit << 20),
        cost_estimate=pl.CostEstimate(flops=int(us * SPEED), bytes_accessed=1 << 10, transcendentals=0),
    )(*rows, *args, *anywhere, *deps)


def lane_mask(info, first, rows):
    token = first + lax.broadcasted_iota(jnp.int32, (rows, 128), 0)
    lane = lax.broadcasted_iota(jnp.int32, (rows, 128), 1) // ADAPTER_RANK
    chosen = jnp.where(token < info[2], info[4], jnp.where(token < info[3], info[5], info[6]))
    return lane == chosen


def chip_mask(info, step):
    chip, core = (info[0] + step) % 4, info[1]
    return jnp.concatenate(
        [
            lane_mask(info, (2 * chip + core) * ROWS, ROWS),
            lane_mask(info, (2 * chip + 1 - core) * ROWS, ROWS),
        ],
        0,
    )


def turn(a, b, cosine, sine):
    return a * cosine - b * sine, b * cosine + a * sine


def aligned(index, unit):
    return pl.ds(pl.multiple_of(index, unit), unit)


def own_first(info, block):
    return (block // 2) * 256 + ((info[1] + block) % 2) * ROWS


def pack_kernel(info, w_hbm, a_in_hbm, a_out_hbm, w_o_hbm, w_pack, ab_pack, w, a_in, a_out, w_o, sems):
    y_at, core = info[0], info[1]
    half = aligned(64 * core, 64)
    copies = [
        pltpu.make_async_copy(w_hbm.at[:, :, aligned(512 * y_at, 512)], w, sems.at[0]),
        pltpu.make_async_copy(a_in_hbm.at[0:4], a_in, sems.at[1]),
        pltpu.make_async_copy(a_out_hbm.at[0:4], a_out, sems.at[2]),
        pltpu.make_async_copy(w_o_hbm.at[aligned(64 * core + 16 * y_at, 16)], w_o, sems.at[3]),
    ]
    for copy in copies:
        copy.start()
    i = lax.broadcasted_iota(jnp.int32, (512, 256), 0)
    j = lax.broadcasted_iota(jnp.int32, (512, 256), 1)
    pick_qk = i == ((j % 128) // 32) * 128 + core * 64 + (j // 128) * 32 + j % 32
    pick_v = i == (j // 64) * 128 + core * 64 + j % 64
    for copy in copies:
        copy.wait()
    for part, pick in enumerate((pick_qk, pick_qk, pick_v)):
        columns = mm(w[part], pick.astype(BF)).astype(BF)
        if part < 2:
            w_pack[:, 256 * part : 256 * part + 256] = columns
        else:
            w_pack[:, 512:640] = columns[:, :128]
            ab_pack[:, 768:] = columns[:, 128:]
    for part in range(3):
        ab_pack[:, 128 * part : 128 * part + 128] = a_in[part]
    ab_pack[:64, 384:512] = a_out[0, half, :]
    ab_pack[64:, 384:512] = a_out[1, half, :]
    ab_pack[:64, 512:640] = a_out[2, half, :]
    ab_pack[64:, 512:640] = a_in[3, half, :]
    ab_pack[:, 640:768] = a_out[3]
    for part in range(8):
        lanes = slice(256 * part, 256 * part + 256)
        w_pack[16 * part : 16 * part + 16, 640:] = w_o[:, lanes]


def pack(w, a_in, a_out, w_o):
    scratch = [
        ((3, ROWS, 512), BF),
        ((4, ROWS, 128), BF),
        ((4, ROWS, 128), BF),
        ((16, WIDTH), BF),
        pltpu.SemaphoreType.DMA((4,)),
    ]
    outs = [((ROWS, 896), BF), ((ROWS, 896), BF)]
    return call(pack_kernel, outs, scratch, ((),), 60, (), (w, a_in, a_out, w_o), us=1.5)


def pack_feed_kernel(info, w_gu, w_d, a_in, a_out, in_ff, out_ff, out):
    y_at, core = info[0], info[1]
    i = lax.broadcasted_iota(jnp.int32, (128, 128), 0)
    j = lax.broadcasted_iota(jnp.int32, (128, 128), 1)
    first = ((j < 64) & (i == j + 64 * core)).astype(BF)
    second = ((j >= 64) & (i == j - 64 + 64 * core)).astype(BF)
    for part in range(2):
        for block in range(8):
            left = w_gu[:, part, aligned(1024 * block + 128 * y_at, 128)]
            right = w_gu[:, part, aligned(1024 * block + 512 + 128 * y_at, 128)]
            lanes = slice(1024 * part + 128 * block, 1024 * part + 128 * block + 128)
            out[:ROWS, lanes] = (mm(left, first) + mm(right, second)).astype(BF)
    out[:ROWS, 2048:2176] = a_in[4]
    out[:ROWS, 2176:2304] = a_in[5]
    out[:ROWS, 2304:] = a_out[4]
    eighth = aligned(64 * (2 * y_at + core), 64)
    out[ROWS:, :WIDTH] = w_d[eighth, :]
    out[ROWS:, 2048:2176] = in_ff[0, eighth, :]
    out[ROWS:, 2176:2304] = out_ff[0, eighth, :]
    out[ROWS:, 2304:] = out_ff[1, eighth, :]


def pack_feed(deps, *args):
    return call(pack_feed_kernel, [((192, 2432), BF)], [], ((), *args), 12, deps, us=3)[0]


def stack_rows(deps, *lists):
    counts = [len(parts) for parts in lists]

    def kernel(info, *refs):
        sems, outs, refs = refs[-1], refs[sum(counts) : -1], refs[: sum(counts)]
        copies = []
        for count, out in zip(counts, outs):
            for i in range(count):
                copies.append(pltpu.make_async_copy(refs[len(copies)], out.at[i], sems.at[len(copies)]))
        for copy in copies:
            copy.start()
        for copy in copies:
            copy.wait()

    outs = [((len(parts),) + parts[0].shape, parts[0].dtype) for parts in lists]
    sems = pltpu.SemaphoreType.DMA((sum(counts),))
    return call(kernel, outs, [sems], ((),), 4, deps, sum(lists, []), pl.ANY, us=1)


def stack_output(others, parts):
    def kernel(info, *refs):
        for i, part in enumerate(refs[:4]):
            refs[-1][i] = part[:, :, 640:]

    shape = ((4, 4, ROWS, 256), BF)
    return call(kernel, [shape], [], ((), *parts), 8, (), others, us=1, token=True)


def arrived(*parts):
    return [part[:8, :128] for part in parts]


def norm_kernel(info, x, gain, out):
    values = x[...].astype(F32)
    inverse = lax.rsqrt(jnp.mean(values * values, -1, keepdims=True) + NORM_EPS)
    out[...] = (values * inverse * gain[0:1, :]).astype(BF)


def norm_first(deps, info, x, gain):
    return call(norm_kernel, [((ROWS, WIDTH), BF)], [], (info, x, gain), 4, deps, us=0.6)[0]


def copy_kernel(info, x, out):
    out[...] = x[...]


def copy_after(deps, info, x):
    return call(copy_kernel, [(x.shape, x.dtype)], [], (info, x), 4, deps)[0]


def qkv_kernel(info, cosine, sine, a0, a1, a2, a3, b0, b1, b2, b3, near, far, *refs):
    q, k, v, low_out, n1, w, a, b_q, b_k, b_v, a_o, b_o, rest, sems = refs
    z_at, x_at, y_at, core = info[7], info[8], info[0], info[1]
    copies, weights = [], []
    for dz in range(4):
        for dx in range(4):
            f = ((z_at + dz) % 4) * 4 + (x_at + dx) % 4
            rows = aligned(f * ROWS, ROWS)
            one, two = (a0, a1, a2, a3)[dz].at[dx], (b0, b1, b2, b3)[dx].at[dz]
            weights.append(pltpu.make_async_copy(two.at[:, :384], a.at[rows], sems.at[1]))
            weights.append(pltpu.make_async_copy(two.at[:, 384:640], rest.at[rows], sems.at[2]))
            weights.append(pltpu.make_async_copy(one.at[:, :640], w.at[rows, :640], sems.at[3]))
            weights.append(pltpu.make_async_copy(two.at[:, 768:], w.at[rows, 640:], sems.at[5]))
            copies.append(pltpu.make_async_copy(two.at[:, 640:768], b_o.at[rows], sems.at[4]))
    tokens = []
    for chip in range(4):
        own, other = chip * 256 + ROWS * core, chip * 256 + ROWS * (1 - core)
        tokens.append(pltpu.make_async_copy(near.at[chip], n1.at[aligned(own, ROWS)], sems.at[0]))
        tokens.append(pltpu.make_async_copy(far.at[chip], n1.at[aligned(other, ROWS)], sems.at[0]))
    for copy in tokens + weights + copies:
        copy.start()
    for copy in tokens + weights:
        copy.wait()
    for head in range(4):
        first = (4 * y_at + head) * ROWS
        for half in range(2):
            to = slice(half * 128 + head * 32, half * 128 + head * 32 + 32)
            b_q[to, :] = rest[aligned(first + 32 * half, 32), :128]
            b_k[to, :] = rest[aligned(first + 64 + 32 * half, 32), :128]
        b_v[64 * head : 64 * head + 64, :] = rest[aligned(first, 64), 128:]
    for f in range(16):
        a_o[64 * f : 64 * f + 64, :] = rest[f * ROWS + 64 : f * ROWS + 128, 128:]
    for chip in range(4):
        at = slice(256 * chip, 256 * chip + 256)
        rows = n1[at, :]
        mask = lane_mask(info, 256 * chip, 256)
        low = jnp.where(jnp.concatenate([mask] * 3, 1), mm(rows, a[...]), 0.0).astype(BF)
        low_out[at, :] = low
        cos, sin = cosine[at, :], sine[at, :]
        for j, (b, out) in enumerate(((b_q, q), (b_k, k))):
            base = mm(rows, w[:, 256 * j : 256 * j + 256])
            values = base + mm_nt(low[:, 128 * j : 128 * j + 128], b[...])
            first, second = turn(values[:, :128], values[:, 128:], cos, sin)
            out[at, :128] = first.astype(BF)
            out[at, 128:] = second.astype(BF)
        v[at, :] = (mm(rows, w[:, 512:]) + mm_nt(low[:, 256:], b_v[...])).astype(BF)
    for copy in copies:
        copy.wait()


def project_qkv(deps, info, w_parts, ab_parts, near, far, cosine, sine):
    return call(
        qkv_kernel,
        [
            ((1024, 256), BF),
            ((1024, 256), BF),
            ((1024, 256), BF),
            ((1024, 384), BF),
            ((1024, WIDTH), BF),
            ((WIDTH, 768), BF),
            ((WIDTH, 384), BF),
            ((256, 128), BF),
            ((256, 128), BF),
            ((256, 128), BF),
            ((1024, 128), BF),
            ((WIDTH, 128), BF),
        ],
        [((WIDTH, 256), BF), pltpu.SemaphoreType.DMA((6,))],
        (info, cosine, sine),
        48,
        deps,
        (*w_parts, *ab_parts, near, far), us=9)


def head_lanes(head, rows, paired):
    lane = lax.broadcasted_iota(jnp.int32, (rows, 256), 1)
    return ((lane % 128) // 32 if paired else lane // 64) == head


def key_bias(info, block):
    n = 256 * (block + 1)
    j = lax.broadcasted_iota(jnp.int32, (n, 256), 0)
    i = 256 * block + lax.broadcasted_iota(jnp.int32, (n, 256), 1)
    allowed = (j <= i) & ((j < info[2]) | (j >= info[3]) | (i < info[3]))
    return jnp.where(allowed, 0.0, MASK_FILL)


def attend_kernel(info, q, k, v, mix, log_total, v_heads, probs):
    for head in range(4):
        v_heads[head] = jnp.where(head_lanes(head, 1024, False), v[...], 0)
    for block in range(4):
        n = 256 * (block + 1)
        rows = slice(256 * block, 256 * block + 256)
        bias = key_bias(info, block)
        out = jnp.zeros((256, 256), F32)
        for head in range(4):
            q_head = jnp.where(head_lanes(head, 256, True), q[rows, :], 0) * jnp.array(0.125, BF)
            scores = mm_nt(k[:n, :], q_head) + bias
            top = jnp.max(scores, 0, keepdims=True)
            weights = jnp.exp(scores - top)
            total = jnp.sum(weights, 0, keepdims=True)
            log_total[head : head + 1, rows] = top + jnp.log(total)
            probs[head, :n, :] = (weights * (1.0 / total)).astype(BF)
        for head in range(4):
            out = out + mm_tn(probs[head, :n, :], v_heads[head, :n, :])
        out = out.astype(BF)
        for part in range(2):
            row = own_first(info, 2 * block + part)
            mix[aligned(row, ROWS), :] = out[part * ROWS : part * ROWS + ROWS]


def attend(info, q, k, v):
    return call(
        attend_kernel,
        [((1024, 256), BF), ((8, 1024), F32)],
        [((4, 1024, 256), BF), ((4, 1024, 256), BF)],
        (info, q, k, v),
        16, us=6)


def attend_back_kernel(
    info, q, k, v, g0, g1, g2, g3, log_total, cosine, sine, out, q_heads, g_heads, k_heads, probs, grads, dk, dv
):
    core = info[1]
    for d, part in enumerate((g0, g1, g2, g3)):
        block = (info[0] - d + 4) % 4
        for other in range(2):
            rows = part[other * ROWS : other * ROWS + ROWS, :256]
            second = (core + other) % 2
            for head in range(4):
                g_heads[block, aligned(256 * head + ROWS * second, ROWS), :] = jnp.where(
                    head_lanes(head, ROWS, False), rows, 0
                )
    for head in range(4):
        k_heads[head] = jnp.where(head_lanes(head, 1024, True), k[...], 0) * jnp.array(0.125, BF)
    dk[...] = jnp.zeros_like(dk)
    dv[...] = jnp.zeros_like(dv)

    def unrotate(values, rows):
        a, b = values[:, :128].astype(F32), values[:, 128:].astype(F32)
        first, last = turn(a, b, cosine[rows, :], -sine[rows, :])
        return jnp.concatenate([first, last], 1).astype(BF)

    for block in range(4):
        n = 256 * (block + 1)
        rows = slice(256 * block, 256 * block + 256)
        bias = key_bias(info, block)
        for head in range(4):
            at = slice(256 * head, 256 * head + 256)
            q_head = jnp.where(head_lanes(head, 256, True), q[rows, :], 0) * jnp.array(0.125, BF)
            q_heads[at, :] = q_head
            scores = mm_nt(k[:n, :], q_head) + bias
            p = jnp.exp(scores - log_total[head : head + 1, rows])
            dp = mm_nt(v[:n, :], g_heads[block, at, :])
            inner = jnp.sum(p * dp, 0, keepdims=True)
            probs[:n, at] = p.astype(BF)
            grads[:n, at] = (p * (dp - inner)).astype(BF)
        dv[:n, :] += mm(probs[:n, :], g_heads[block])
        dk[:n, :] += mm(grads[:n, :], q_heads[...])
        dq = jnp.zeros((256, 256), F32)
        for head in range(4):
            dq = dq + mm_tn(grads[:n, 256 * head : 256 * head + 256], k_heads[head, :n, :])
        out[rows, 0:256] = unrotate(dq.astype(BF), rows)
    for block in range(4):
        rows = slice(256 * block, 256 * block + 256)
        out[rows, 256:512] = unrotate(dk[rows, :].astype(BF), rows)
        out[rows, 512:768] = dv[rows, :].astype(BF)


def attend_back(deps, info, q, k, v, parts, log_total, cosine, sine):
    return call(
        attend_back_kernel,
        [((1024, 768), BF)],
        [
            ((1024, 256), BF),
            ((4, 1024, 256), BF),
            ((4, 1024, 256), BF),
            ((1024, 1024), BF),
            ((1024, 1024), BF),
            ((1024, 256), F32),
            ((1024, 256), F32),
        ],
        (info, q, k, v, *parts, log_total, cosine, sine),
        15,
        deps, us=9, token=True)


def output_kernel(info, parts, w0, w1, w2, w3, a_o, keep, send, w, mix):
    z_at, x_at = info[7], info[8]
    for dy, piece in enumerate((w0, w1, w2, w3)):
        chip = (info[0] + dy) % 4
        mix[:, 256 * dy : 256 * dy + 256] = parts[dy]
        for dz in range(4):
            for dx in range(4):
                f = ((z_at + dz) % 4) * 4 + (x_at + dx) % 4
                rows = aligned(f * 64 + 16 * chip, 16)
                for part in range(8):
                    w[rows, 256 * part : 256 * part + 256] = piece[dz, dx, 16 * part : 16 * part + 16]
    keep[:, :WIDTH] = mm(mix[:ROWS, :], w[...])
    keep[:, WIDTH:] = mm(mix[:ROWS, :], a_o[...])
    send[:, :WIDTH] = mm(mix[ROWS:, :], w[...]).astype(BF)
    send[:, WIDTH:] = mm(mix[ROWS:, :], a_o[...]).astype(BF)


def project_output(info, mixes, pieces, a_o):
    return call(
        output_kernel,
        [((ROWS, 2176), F32), ((ROWS, 2176), BF), ((1024, WIDTH), BF)],
        [((256, 1024), BF)],
        (info, mixes, *pieces, a_o),
        8, us=4)


def middle_kernel(info, keep, got, x, b_o, gain, resid, n2, low):
    summed = keep[...] + got[...].astype(F32)
    mask = lane_mask(info, (2 * info[0] + info[1]) * ROWS, ROWS)
    low_o = jnp.where(mask, summed[:, WIDTH:], 0.0).astype(BF)
    low[...] = low_o
    values = x[...].astype(F32) + summed[:, :WIDTH] + mm_nt(low_o, b_o[...])
    resid[...] = values
    inverse = lax.rsqrt(jnp.mean(values * values, -1, keepdims=True) + NORM_EPS)
    n2[...] = (values * inverse * gain[1:2, :]).astype(BF)


def middle(deps, info, keep, got, x, b_o, gain):
    return call(
        middle_kernel,
        [((ROWS, WIDTH), F32), ((ROWS, WIDTH), BF), ((ROWS, 128), BF)],
        [],
        (info, keep, got, x, b_o, gain),
        10,
        deps, us=1)


def load_weights(gathered, w_g, w_u, w_d, a_gu, b_d, ff, sems):
    small = [
        pltpu.make_async_copy(gathered.at[:, :ROWS, 2048:2304], a_gu, sems.at[0]),
        pltpu.make_async_copy(gathered.at[:, :ROWS, 2304:], b_d, sems.at[1]),
        pltpu.make_async_copy(gathered.at[:, ROWS:, 2048:], ff, sems.at[2]),
    ]
    blocks = []
    for i in range(4):
        at, up = pl.ds(256 * i, 256), pl.ds(1024 + 256 * i, 256)
        rows = pl.ds(4 * i, 4)
        blocks.append(
            [
                pltpu.make_async_copy(gathered.at[:, :ROWS, at], w_g.at[:, :, at], sems.at[3 + 3 * i]),
                pltpu.make_async_copy(gathered.at[:, :ROWS, up], w_u.at[:, :, at], sems.at[4 + 3 * i]),
                pltpu.make_async_copy(gathered.at[rows, ROWS:, :WIDTH], w_d.at[rows], sems.at[5 + 3 * i]),
            ]
        )
    for group in [small] + blocks:
        for copy in group:
            copy.start()
    return [small] + blocks


def feed_kernel(step, first, info, *refs):
    if first:
        n_near, n_far, g_near, g_far, gathered, *outs = refs[:13]
        w_g, w_u, w_d, a_gu, b_d, ff, n_rows, g_rows, row_sems, sems = refs[13:]
    else:
        w_g, w_u, w_d, a_gu, b_d, ff, n_near, n_far, g_near, g_far, *outs = refs[:18]
        n_rows, g_rows, row_sems = refs[18:]
    keep_down, send_down, keep_back, send_back, hidden, grad_gate, grad_up, lows = outs
    chip = (info[0] + step) % 4
    row_copies = [
        pltpu.make_async_copy(part, rows.at[at : at + ROWS], row_sems.at[i])
        for i, (part, rows, at) in enumerate(
            (
                (n_near, n_rows, 0),
                (n_far, n_rows, ROWS),
                (g_near.at[chip], g_rows, 0),
                (g_far.at[chip], g_rows, ROWS),
            )
        )
    ]
    for copy in row_copies:
        copy.start()
    groups = load_weights(gathered, w_g, w_u, w_d, a_gu, b_d, ff, sems) if first else [[]] * 5
    for copy in row_copies[:2]:
        copy.wait()
    mask = chip_mask(info, step)
    twice = jnp.concatenate([mask, mask], 1)
    for copy in groups[0]:
        copy.wait()
    low = jnp.where(twice, mm(n_rows[...], a_gu[...].reshape(WIDTH, 256)), 0.0).astype(BF)
    for copy in row_copies[2:]:
        copy.wait()
    glow = jnp.where(mask, mm(g_rows[...], b_d[...].reshape(WIDTH, 128)), 0.0).astype(BF)
    lows[:, :256] = low
    lows[:, 256:384] = glow
    for block in range(4):
        at = slice(256 * block, 256 * block + 256)
        rows = slice(4 * block, 4 * block + 4)
        for copy in groups[1 + block]:
            copy.wait()
        thin = ff[rows].reshape(256, 384)
        gate = mm(n_rows[...], w_g[:, :, at].reshape(WIDTH, 256)) + mm_nt(low[:, :128], thin[:, 128:256])
        up = mm(n_rows[...], w_u[:, :, at].reshape(WIDTH, 256)) + mm_nt(low[:, 128:], thin[:, 256:])
        grad_hidden = mm_nt(g_rows[...], w_d[rows].reshape(256, WIDTH)) + mm_nt(glow, thin[:, :128])
        sig = 1.0 / (1.0 + jnp.exp(-gate))
        act = gate * sig
        hidden[:, at] = (act * up).astype(BF)
        grad_gate[:, at] = (grad_hidden * up * sig * (1.0 + gate * (1.0 - sig))).astype(BF)
        grad_up[:, at] = (grad_hidden * act).astype(BF)

    def put(keep, send, at, values):
        keep[:, at] = values[:ROWS].astype(BF)
        send[:, at] = values[ROWS:].astype(BF)

    for block in range(8):
        at = slice(256 * block, 256 * block + 256)
        pair = slice(2 * block, 2 * block + 2)
        left = mm_nt(grad_gate[...], w_g[pair].reshape(256, 1024))
        right = mm_nt(grad_up[...], w_u[pair].reshape(256, 1024))
        put(keep_back, send_back, at, left + right)
        put(keep_down, send_down, at, mm(hidden[...], w_d[:, :, at].reshape(1024, 256)))
    thin = ff[...].reshape(1024, 384)
    glow_g = mm(grad_gate[...], thin[:, 128:256])
    glow_u = mm(grad_up[...], thin[:, 256:])
    low_d = mm(hidden[...], thin[:, :128])
    put(keep_back, send_back, slice(WIDTH, WIDTH + 128), glow_g)
    put(keep_back, send_back, slice(WIDTH + 128, WIDTH + 256), glow_u)
    put(keep_down, send_down, slice(WIDTH, WIDTH + 128), low_d)
    lows[:, 384:512] = jnp.where(mask, glow_g, 0.0).astype(BF)
    lows[:, 512:640] = jnp.where(mask, glow_u, 0.0).astype(BF)
    lows[:, 640:] = jnp.where(mask, low_d, 0.0).astype(BF)


def feed(step, deps, info, tokens, weights):
    first = len(weights) == 1
    shapes = [
        ((ROWS, 2176), BF),
        ((ROWS, 2176), BF),
        ((ROWS, 2304), BF),
        ((ROWS, 2304), BF),
        ((256, 1024), BF),
        ((256, 1024), BF),
        ((256, 1024), BF),
        ((256, 768), BF),
    ]
    scratch = [((256, WIDTH), BF), ((256, WIDTH), BF), pltpu.SemaphoreType.DMA((4,))]
    kernel = functools.partial(feed_kernel, step, first)
    if not first:
        return call(kernel, shapes, scratch, (info, *weights), 10, deps, tokens, us=9), weights
    held = [(16, ROWS, 1024), (16, ROWS, 1024), (16, 64, WIDTH), (16, ROWS, 256), (16, ROWS, 128), (16, 64, 384)]
    shapes += [(shape, BF) for shape in held]
    scratch.append(pltpu.SemaphoreType.DMA((15,)))
    outs = call(kernel, shapes, scratch, (info,), 26, deps, (*tokens, *weights), us=12)
    return outs[:8], outs[8:]


def early_kernel(info, *refs):
    chunks = [refs[4 * i : 4 * i + 4] for i in range(4)]
    parts = refs[16:24]
    g_near, g_far, by_token, by_hidden, n_rows, g_rows, sems = refs[24:]
    copies = []
    for i, d in enumerate(ORDER):
        chip = (info[0] + d) % 4
        for far in range(2):
            to = pl.ds((2 * i + far) * ROWS, ROWS)
            copies.append(pltpu.make_async_copy(parts[4 * far + d], n_rows.at[to], sems.at[2 * i + far]))
            source = (g_near, g_far)[far].at[chip]
            copies.append(pltpu.make_async_copy(source, g_rows.at[to], sems.at[8 + 2 * i + far]))
    for copy in copies:
        copy.start()
    flip = lambda values: values.astype(F32).T.astype(BF)
    thins = [flip(chunk[3][...]) for chunk in chunks]
    for j, (row, name) in enumerate(((2, 0), (0, 1), (1, 2))):
        rows = slice(128 * row, 128 * row + 128)
        total = sum(mm(thins[i][rows], chunks[i][name][...]) for i in range(4))
        by_hidden[:, 128 * j : 128 * j + 128] = total.T.astype(BF)
    for copy in copies:
        copy.wait()
    for j, (row, tokens) in enumerate(((3, n_rows), (4, n_rows), (5, g_rows))):
        rows = slice(128 * row, 128 * row + 128)
        total = sum(mm(thins[i][rows], tokens[256 * i : 256 * i + 256, :]) for i in range(4))
        by_token[:, 128 * j : 128 * j + 128] = total.T.astype(BF)


def early_sums(tokens, chunks, deps):
    args = [()] + [part for chunk in chunks for part in chunk]
    scratch = [((1024, WIDTH), BF), ((1024, WIDTH), BF), pltpu.SemaphoreType.DMA((16,))]
    outs = [((WIDTH, 384), BF), ((1024, 384), BF)]
    return call(early_kernel, outs, scratch, args, 16, deps, tokens, us=4.5)


def between_kernel(info, own, r1, r2, r3, a_gu, resid, og, low, gain, grad_resid, grad_attn):
    total = own[...] + r1[...].astype(F32) + r2[...].astype(F32) + r3[...].astype(F32)
    mask = lane_mask(info, (2 * info[0] + info[1]) * ROWS, ROWS)
    glow = jnp.where(jnp.concatenate([mask, mask], 1), total[:, WIDTH:], 0.0).astype(BF)
    grad = total[:, :WIDTH] + mm_nt(glow, a_gu[...].reshape(WIDTH, 256))
    values = resid[...]
    inverse = lax.rsqrt(jnp.mean(values * values, -1, keepdims=True) + NORM_EPS)
    result = og[...].astype(F32) + norm_back(grad, values, inverse, gain[1:2, :])
    grad_resid[...] = result
    grad_attn[:, :WIDTH] = result.astype(BF)
    grad_attn[:, WIDTH:] = low[...]


def between(deps, info, own, r1, r2, r3, a_gu, resid, og, low, gain):
    return call(
        between_kernel,
        [((ROWS, WIDTH), F32), ((ROWS, 2176), BF)],
        [],
        (info, own, r1, r2, r3, a_gu, resid, og, low, gain),
        10,
        deps, us=1.4)


def combine_kernel(info, by_token, by_hidden, out):
    for f in range(16):
        out[f, :ROWS, :] = by_token[f * ROWS : f * ROWS + ROWS, :]
        out[f, ROWS:, :] = by_hidden[64 * f : 64 * f + 64, :]


def combine(by_token, by_hidden):
    return call(
        combine_kernel, [((16, 192, 384), BF)], [], ((), by_token, by_hidden), 8, us=1.6, token=True
    )


def down_kernel(info, k0, k1, k2, k3, got, own, *outs):
    for i, (d, keep) in enumerate(zip(ORDER, (k0, k1, k2, k3))):
        total = keep[...].astype(F32) + got[i].astype(F32)
        if d:
            outs[d - 1][...] = total.astype(BF)
        else:
            own[...] = total


def down_pair(deps, kept, got):
    return call(
        down_kernel,
        [((ROWS, 2176), F32)] + [((ROWS, 2176), BF)] * 3,
        [],
        ((), *kept, got),
        8,
        deps, us=1.5, token=True)


def result_kernel(info, own, r1, r2, r3, resid, b_d, out):
    total = own[...] + r1[...].astype(F32) + r2[...].astype(F32) + r3[...].astype(F32)
    mask = lane_mask(info, (2 * info[0] + info[1]) * ROWS, ROWS)
    low = jnp.where(mask, total[:, WIDTH:], 0.0).astype(BF)
    out[...] = (resid[...] + total[:, :WIDTH] + mm_nt(low, b_d[...].reshape(WIDTH, 128))).astype(BF)


def result(info, own, r1, r2, r3, resid, b_d):
    return call(
        result_kernel, [((ROWS, WIDTH), BF)], [], (info, own, r1, r2, r3, resid, b_d), 10, us=1.8, token=True)


def output_back_kernel(info, own, other, b_o, w_o, a_o, p0, p1, p2, p3, half, grad, mix):
    grad[:ROWS] = own[:, :WIDTH]
    grad[ROWS:] = other[:, :WIDTH]
    glow = jnp.where(chip_mask(info, 0), mm(grad[...], b_o[...]), 0.0).astype(BF)
    for chip in range(4):
        at = slice(256 * chip, 256 * chip + 256)
        mix[:, at] = (mm_nt(grad[...], w_o[at, :]) + mm_nt(glow, a_o[at, :])).astype(BF)
    for d, part in enumerate((p0, p1, p2, p3)):
        part[:, :256] = mix[:, aligned(256 * ((info[0] + d) % 4), 256)]
        part[:, 256:] = glow
    flip = lambda values: values.astype(F32).T.astype(BF)
    total = (mm(flip(own[:, WIDTH:]), grad[:ROWS]) + mm(flip(other[:, WIDTH:]), grad[ROWS:])).T.astype(BF)
    for f in range(16):
        rows = total[f * ROWS : f * ROWS + ROWS]
        half[64 * f : 64 * f + 64, :] = jnp.where(info[1] == 0, rows[:64], rows[64:])


def output_back(info, own, other, b_o, w_o, a_o):
    return call(
        output_back_kernel,
        [((256, 384), BF)] * 4 + [((1024, 128), BF)],
        [((256, WIDTH), BF), ((256, 1024), BF)],
        (info, own, other, b_o, w_o, a_o),
        8, us=2.7)


def pick_rows(info, g, core, out):
    for d in range(4):
        chip = (info[0] + d) % 4
        out[d * ROWS : d * ROWS + ROWS, :] = g[aligned(256 * chip + ROWS * core, ROWS), :]


def input_send_kernel(info, g, w, send, rows):
    pick_rows(info, g, 1 - info[1], rows)
    for block in range(8):
        at = slice(256 * block, 256 * block + 256)
        send[:, at] = mm_nt(rows[...], w[at, :]).astype(BF)


def input_send(deps, info, g, w):
    return call(input_send_kernel, [((512, WIDTH), BF)], [((512, 768), BF)], (info, g, w), 8, deps=deps, us=3.7, token=True)


def input_pair_kernel(info, g, w, got, own, p1, p2, p3, rows):
    pick_rows(info, g, info[1], rows)
    for block in range(8):
        at = slice(256 * block, 256 * block + 256)
        total = mm_nt(rows[...], w[at, :]) + got[:, at].astype(F32)
        own[:, at] = total[:ROWS]
        for d, out in enumerate((p1, p2, p3)):
            out[:, at] = total[ROWS * (d + 1) : ROWS * (d + 2)].astype(BF)


def input_pair(deps, info, g, w, got):
    return call(
        input_pair_kernel,
        [((ROWS, WIDTH), F32)] + [((ROWS, WIDTH), BF)] * 3,
        [((512, 768), BF)],
        (info, g, w, got),
        8,
        deps, us=3.5, token=True)


def squeeze(rows):
    i = lax.broadcasted_iota(jnp.int32, rows, 0) % ADAPTER_RANK
    j = lax.broadcasted_iota(jnp.int32, rows, 1) % ADAPTER_RANK
    return (i == j).astype(BF)


def narrow_kernel(info, g, b_q, b_k, b_v, low, mix, o0, o1, o2, o3, narrow, own):
    mask = lane_mask(info, 0, 1024)
    fold = squeeze((16, 128))
    flip = lambda values: values.astype(F32).T.astype(BF)
    for j, b in enumerate((b_q, b_k, b_v)):
        term = jnp.where(mask, mm(g[:, 256 * j : 256 * j + 256], b[...]), 0.0).astype(BF)
        narrow[16 * j : 16 * j + 16, :] = mm_nt(fold, term).astype(BF)
    low_t = flip(low[...])
    for j in range(3):
        total = mm(low_t[128 * j : 128 * j + 128], g[:, 256 * j : 256 * j + 256]).T.astype(BF)
        lanes = slice(128 * (j + 1), 128 * (j + 2))
        for head in range(4):
            if j == 2:
                own[head, :, lanes] = total[64 * head : 64 * head + 64]
            else:
                own[head, :32, lanes] = total[32 * head : 32 * head + 32]
                own[head, 32:, lanes] = total[128 + 32 * head : 160 + 32 * head]
    total = sum(
        mm(flip(part[:, 256:]), mix[aligned(256 * ((info[0] - d + 4) % 4), 256), :])
        for d, part in enumerate((o0, o1, o2, o3))
    ).T.astype(BF)
    for head in range(4):
        own[head, :, :128] = total[64 * head : 64 * head + 64]


def narrow_sums(deps, info, g, b_q, b_k, b_v, low, mix, parts):
    return call(
        narrow_kernel,
        [((48, 1024), BF), ((4, 64, 512), BF)],
        [],
        (info, g, b_q, b_k, b_v, low, mix, *parts),
        10,
        deps, us=2.3)


def late_kernel(info, parts, rows, out, glow_own):
    total = sum(parts[chip].astype(F32) for chip in range(4))
    total = total.astype(BF)
    s_at = 2 * info[0] + info[1]
    mask = lane_mask(info, 0, 1024)
    spread = squeeze((16, 128))
    wide = []
    for j in range(3):
        term = jnp.where(mask, mm_tn(total[16 * j : 16 * j + 16], spread), 0.0)
        wide.append(term)
    mask_own = lane_mask(info, s_at * ROWS, ROWS)
    for j in range(3):
        piece = jnp.zeros((ROWS, 128), F32)
        for block in range(8):
            piece = jnp.where(s_at == block, wide[j][block * ROWS : block * ROWS + ROWS], piece)
        glow_own[:, 128 * j : 128 * j + 128] = jnp.where(mask_own, piece, 0.0).astype(BF)
    thin = jnp.concatenate([term.T.astype(BF) for term in wide], 0)
    for f in range(8):
        at = slice(256 * f, 256 * f + 256)
        total = mm(thin, rows[:, at]).T
        for second in range(2):
            piece = jnp.zeros((16, 384), F32)
            for s in range(8):
                first = second * ROWS + 16 * s
                piece = jnp.where(s_at == s, total[first : first + 16], piece)
            out[2 * f + second] = piece.astype(BF)


def late_sums(deps, info, parts, rows):
    return call(
        late_kernel,
        [((16, 16, 384), BF), ((ROWS, 384), BF)],
        [],
        (info, parts, rows),
        10,
        deps, us=2.9)


def groups_kernel(info, values, out):
    total = values[0].astype(F32)
    for f in range(1, 16):
        total = total + values[f].astype(F32)
    out[...] = total.astype(BF)


def sum_groups(deps, values):
    return call(groups_kernel, [(values.shape[1:], BF)], [], ((), values), 8, deps, us=1.6)[0]


def early_result_kernel(info, values, one, two, spread):
    for j in range(3):
        lanes = slice(128 * j, 128 * j + 128)
        spread[j] = sum(values[s, :ROWS, lanes].astype(F32) for s in range(8))
        out, at = (one, 0) if j == 0 else (two, j - 1)
        for s in range(8):
            out[at, 64 * s : 64 * s + 64, :] = values[s, ROWS:, lanes].astype(F32)


def early_result(values):
    outs = [((1, 512, 128), F32), ((2, 512, 128), F32), ((3, ROWS, 128), F32)]
    return call(early_result_kernel, outs, [], ((), values), 8, us=2, token=True)


def final_kernel(info, *refs):
    y_at, core, z_at = info[0], info[1], info[7]
    spread, grad_in, grad_out, own = refs[8:]
    last = [0.0, 0.0]
    for d in range(4):
        chip = (y_at + d) % 4
        for other in range(2):
            part, at = refs[4 * other + d], (core + other) % 2
            for j in range(3):
                grad_in[j, aligned((2 * chip + at) * 16, 16), :] = part[:, 128 * j : 128 * j + 128].astype(F32)
            rows = aligned(64 * at, 16)

            @pl.when(chip == z_at)
            def _():
                own[pl.ds(16 * at, 16), :] = part[:, 384:2432].astype(F32)

            last[other] = last[other] + part[:, 2432:].astype(F32)
    for r in range(4):
        for j in range(4):
            lanes = slice(512 * r + 128 * j, 512 * r + 128 * j + 128)
            values = own[:, lanes]
            for i in range(32):
                out, at = (grad_in, 3) if j == 0 else (grad_out, j - 1)
                out[at, 4 * i + r : 4 * i + r + 1, :] = values[i : i + 1]
        lanes = slice(128 * r, 128 * r + 128)
        first = jnp.where(core == 0, last[0][:, lanes], last[1][:, lanes])
        second = jnp.where(core == 0, last[1][:, lanes], last[0][:, lanes])
        for i in range(16):
            grad_out[3, 4 * i + r : 4 * i + r + 1, :] = first[i : i + 1]
            grad_out[3, 64 + 4 * i + r : 64 + 4 * i + r + 1, :] = second[i : i + 1]
    grad_in[4] = spread[0]
    grad_in[5] = spread[1]
    grad_out[4] = spread[2]


def final_result(deps, near, far, spread):
    outs = [((6, ROWS, 128), F32), ((5, ROWS, 128), F32)]
    return call(final_kernel, outs, [((32, 2048), F32)], ((), *near, *far, spread), 8, deps, us=2)


def last_kernel(info, own, r1, r2, r3, glow, a, resid_grad, x, gain, out):
    grad = own[...] + r1[...].astype(F32) + r2[...].astype(F32) + r3[...].astype(F32) + mm_nt(glow[...], a[...])
    values = x[...].astype(F32)
    inverse = lax.rsqrt(jnp.mean(values * values, -1, keepdims=True) + NORM_EPS)
    out[...] = resid_grad[...] + norm_back(grad, values, inverse, gain[0:1, :])


def last(deps, info, own, r1, r2, r3, glow, a, resid_grad, x, gain):
    return call(
        last_kernel,
        [((ROWS, WIDTH), F32)],
        [],
        (info, own, r1, r2, r3, glow, a, resid_grad, x, gain),
        10, deps=deps, us=2.5, token=True)


def rms_inverse(values):
    return lax.rsqrt(jnp.mean(values * values, -1, keepdims=True) + NORM_EPS)


def norm_back(grad_norm, values, inverse, gain):
    normed = values * inverse
    scaled = grad_norm * gain
    return inverse * (scaled - normed * jnp.mean(scaled * normed, -1, keepdims=True))


def body(
    layer_input,
    output_gradient,
    norm_gain_pair,
    query_key_value_weight,
    output_weight,
    gate_up_weight,
    down_weight,
    adapter_input_model,
    adapter_output_model,
    adapter_input_hidden,
    adapter_output_hidden,
    spans,
    adapter_choice_rows,
):
    f_at, s_at = lax.axis_index("fs"), lax.axis_index("sp")
    y_at, c_at = s_at >> 1, s_at & 1
    z_at = f_at >> 2
    x_l = layer_input[0]
    og_l = output_gradient[0]
    rows = x_l.shape[0]
    tokens = 8 * rows
    gains = norm_gain_pair
    info = (spans, adapter_choice_rows)

    w_pack, ab_pack = pack(
        query_key_value_weight.transpose(1, 0, 2), adapter_input_model, adapter_output_model, output_weight
    )
    w_line, ab_line = line(w_pack, shift_x), line(ab_pack, shift_z)
    w_line, ab_line = stack_rows((), w_line, ab_line)
    w_parts, ab_parts = line(w_line, shift_z), line(ab_line, shift_x)
    n1_l = norm_first((w_pack,), info, x_l, gains)
    near = gather_y(n1_l)
    far = swap(near)
    g_near = gather_y(og_l)
    g_far = swap(g_near)
    feed_pack = pack_feed(
        (w_pack,),
        gate_up_weight,
        down_weight,
        adapter_input_model,
        adapter_output_model,
        adapter_input_hidden,
        adapter_output_hidden,
    )
    o_stack, p1_done = stack_output(ab_parts, w_parts)
    feed_all = lax.all_gather(after(feed_pack, p1_done), "fs", axis=0, tiled=False)

    at = jnp.arange(tokens, dtype=jnp.int32)
    position = at - jnp.where(at >= spans[0, 0] + spans[0, 1], spans[0, 1], 0)
    freq = ROPE_BASE ** (-(jnp.arange(32, dtype=F32) * 2.0 / HEAD_SIZE))
    phase = position.astype(F32)[:, None] * jnp.tile(freq, 4)[None, :]
    cosine, sine = jnp.cos(phase), jnp.sin(phase)

    o_parts = line(o_stack, shift)
    q, k, v, low_qkv, n1, w_qkv, a_qkv, b_q, b_k, b_v, a_o, b_o = project_qkv(
        (), info, w_parts, ab_parts, near, far, cosine, sine
    )
    mix, log_total = attend(info, q, k, v)
    mixes = exchange_y(mix.reshape(4, 256, 256))
    keep, send, w_o = project_output(info, mixes, o_parts, a_o)
    resid, n2_l, low_o = middle((), info, keep, swap(send), x_l, b_o, gains)

    n_near = line(n2_l, shift)
    n_far = [swap(part) for part in n_near]
    chunks, kept, sent, back, got = [], [], [], {}, []
    rows_there = arrived(*n_near[1:], *n_far)
    pairs = []
    weights = (feed_all,)
    for d in ORDER:
        deps = [chunks[-1][-1]] if chunks else rows_there
        if len(chunks) == 2:
            deps += arrived(pairs[0])
        if len(chunks) == 3:
            deps += arrived(pairs[2], back[ORDER[0]])
        outs, weights = feed(d, deps, info, (n_near[d], n_far[d], g_near, g_far), weights)
        keep_down, send_down, keep_back, send_back, *chunk = outs
        chunks.append(chunk)
        kept.append(keep_down)
        sent.append(send_down)
        got.append(swap(send_back))
        pair = keep_back.astype(F32) + got[-1].astype(F32)
        if d:
            pair = pair.astype(BF)
        pairs.append(pair)
        back[d] = shift(pair, d if d < 3 else -1) if d else pair
    a_gu, b_d = weights[3], weights[4]
    by_token, by_hidden = early_sums((*n_near, *n_far, g_near, g_far), chunks, arrived(back[ORDER[1]], back[ORDER[2]]))
    early, early_done = combine(by_token, by_hidden)
    early = lax.psum_scatter(early.reshape(16 * 192, 384), "fs", scatter_dimension=0, tiled=True)
    grad_resid, grad_attn = between((early_done,), info, back[0], back[1], back[2], back[3], a_gu, resid, og_l, low_o, gains)

    *parts, half_o = output_back(info, grad_attn, swap(grad_attn), b_o, w_o, a_o)
    parts = [parts[0]] + [shift(parts[d], d) for d in (1, 2, 3)]
    *down, down_done = down_pair((half_o,), kept, swap(jnp.stack(sent)))
    g_all, _ = attend_back((down_done,), info, q, k, v, parts, log_total, cosine, sine)
    send, send_done = input_send((), info, g_all, w_qkv)
    narrow, own = narrow_sums((send_done,), info, g_all, b_q, b_k, b_v, low_qkv, mix, parts)
    pair, *total, pair_done = input_pair((narrow,), info, g_all, w_qkv, swap(send))
    total = [shift(total[d - 1], d if d < 3 else -1) for d in (1, 2, 3)]
    narrow = (narrow.astype(F32) + swap(narrow).astype(F32)).astype(BF)
    narrow = exchange_y(jnp.broadcast_to(narrow[None], (4,) + narrow.shape))
    late, glow_own = late_sums((pair_done,), info, narrow, n1)
    down = [down[0]] + [shift(after(down[d], narrow), d if d < 3 else -1) for d in (1, 2, 3)]
    layer_output, output_done = result(info, *down, resid, b_d)
    grad_in, input_done = last((), info, pair, *total, glow_own, a_qkv, grad_resid, x_l, gains)

    early = lax.all_gather(after(early, glow_own), "sp", axis=0, tiled=False)
    *fed, spread, spread_done = early_result(early)
    own = lax.dynamic_update_slice(jnp.zeros((16, 16, 2048), BF), own.reshape(4, 16, 2048), (4 * y_at, 0, 0))
    final = jnp.concatenate([late, own, half_o.reshape(16, 16, 512)], 2)
    final = lax.all_to_all(final, "fs", split_axis=0, concat_axis=0, tiled=False)
    final = sum_groups((input_done, spread_done), final)
    near = line(final, shift)
    grad_in_d, grad_out_d = final_result((output_done,), near, [swap(part) for part in near], spread)
    return (layer_output[None], grad_in[None], grad_in_d, grad_out_d, *fed)


def solution(mesh):
    in_specs = (
        P("fs", "sp", None),
        P("fs", "sp", None),
        P(),
        P("fs", None, None),
        P("fs", None),
        P("fs", None, None),
        P("fs", None),
        P(None, "fs", None),
        P(None, "fs", None),
        P(None, "fs", None),
        P(None, "fs", None),
        P("fs", None),
        P("fs", None),
    )
    out_specs = (
        P("fs", "sp", None),
        P("fs", "sp", None),
        P(None, "fs", None),
        P(None, "fs", None),
        P(None, "fs", None),
        P(None, "fs", None),
    )
    return jax.shard_map(body, mesh=mesh, in_specs=in_specs, out_specs=out_specs, check_vma=False)
```
